32 devices in a mesh: blk: 4 (over y, core), bal: 8 (over z, x).
Axes of the slice: x: 2, y: 2, z: 4, core: 2. Of those that a mesh axis runs over, the one named last changes fastest.
Arguments:
- features: bfloat16 [32768, 512], P('blk', 'bal'), may hold values from -6 to 6
- tile_values: bfloat16 [4, 4, 32, 128, 128], P('blk'), may hold values from 0.049804688 to 1
- tile_rows: int32 [4, 4, 32], P('blk'), may hold values from 0 to 63
- tile_cols: int32 [4, 4, 32], P('blk'), may hold values from 0 to 63
- tile_counts: int32 [4, 4], P('blk'), may hold values from 8 to 32, as said below
- w_self: bfloat16 [512, 512], replicated, may hold values from -0.25 to 0.25
- w_neigh: bfloat16 [512, 512], replicated, may hold values from -5 to 5
- bias: float32 [512], replicated, may hold values from -3 to 3
- part_map: int32 [4, 64], P('blk'), may hold values from 0 to 7, as said below
Outputs:
- next_rows: bfloat16 [4, 8, 2048, 512], P('blk', 'bal')
The draws below stay inside these ranges and needn't reach their ends.
Inputs may be any that keep to these rules, and one draw needn't show every extreme that they name: `tile_counts`: live slots of one pair of vertex blocks; the most, 32, is reached by some pair in every draw. `part_map`: within one block of vertex rows at most 16 tiles go to any one value, and exactly 16 to some value.
All inputs are finite; a program needn't handle non-finite values.
Results may differ from the reference program's by a relative error of at most 0.0036.
Values may be sent and summed in bfloat16 or wider, within the bound.
A program may use at most 128 MiB of HBM per device.

```python
import math
import jax
import jax.numpy as jnp
from jax import lax

F = 512
TILE = 128
S = 32
TR = 64
CAP = 16
R = 8192
N = 32768
N_BLK = 4
N_BAL = 8


def draw_tile_counts(key, part):
    counts = jax.random.randint(key, (N_BLK * N_BLK,), S // 4, S + 1)
    where_full = jax.random.randint(jax.random.fold_in(key, 1), (), 0, N_BLK * N_BLK)
    counts = counts.at[where_full].set(S)
    return counts.reshape(N_BLK, N_BLK).astype(jnp.int32)


def draw_part_map(key, part):

    def one_block(index):
        block_key = jax.random.fold_in(key, index)
        chosen = jax.random.randint(jax.random.fold_in(block_key, 1), (), 0, 2 * TR // CAP)
        perm = jax.random.permutation(jax.random.fold_in(block_key, 2), 2 * TR)
        seats = jnp.arange(2 * TR)
        scores = jnp.where(seats // CAP == chosen, perm - 2 * TR, perm)
        order = jnp.argsort(scores, stable=True)[:TR]
        return (order // CAP).astype(jnp.int32)
    return jax.vmap(one_block)(jnp.arange(N_BLK))


def touch_ends(result, own_key, least, largest):
    dims = result.shape
    index_at = [jax.random.randint(jax.random.fold_in(own_key, axis), (), 0, dims[axis]) for axis in range(len(dims))]
    result = result.at[tuple(index_at)].set(least)
    longest = dims.index(max(dims))
    index_at[longest] = (index_at[longest] + 1) % dims[longest]
    return result.at[tuple(index_at)].set(largest)


def block_scale(rng, extent, split, least, largest):
    level, own = 1.0, jax.random.fold_in(rng, 6)
    for dim, parts in split:
        heights = jnp.exp(jax.random.uniform(jax.random.fold_in(own, dim), (parts,), jnp.float32, least / len(split), largest / len(split)))
        level = level * jnp.repeat(heights, extent[dim] // parts).reshape([-1 if axis == dim else 1 for axis in range(len(extent))])
    return level


def gaussian(own_key, dims, scale, limit, split=(), kind=jnp.bfloat16):
    result = scale * jax.random.normal(own_key, dims, jnp.float32)
    if split:
        result = result * block_scale(own_key, dims, split, -0.22, 0.18)
    return jnp.clip(result, -limit, limit).astype(kind)


def setup_inputs(seed: int = 0) -> dict:
    keys = jax.random.split(jax.random.key(seed), 10)
    return {
        "features": gaussian(keys[0], (N, F), 1.0, 6.0, ((0, 4), (1, 8))),
        "tile_values": jnp.clip(jnp.exp(math.log(1.0) - 2.9996462 * jax.random.uniform(keys[1], (N_BLK, N_BLK, S, TILE, TILE), jnp.float32) ** block_scale(keys[1], (N_BLK, N_BLK, S, TILE, TILE), ((0, 4),), -0.2, 0.2)), 0.049804688, 1.0).astype(jnp.bfloat16),
        "tile_rows": touch_ends(jax.random.randint(keys[2], (N_BLK, N_BLK, S), 0, TR), jax.random.fold_in(keys[2], 1), 0, TR - 1).astype(jnp.int32),
        "tile_cols": touch_ends(jax.random.randint(keys[3], (N_BLK, N_BLK, S), 0, TR), jax.random.fold_in(keys[3], 1), 0, TR - 1).astype(jnp.int32),
        "tile_counts": draw_tile_counts(jax.random.fold_in(keys[9], 71), 0),
        "w_self": gaussian(keys[5], (F, F), F ** -0.5, 0.25),
        "w_neigh": gaussian(keys[6], (F, F), (0.5 * (N_BLK * S * TILE // TR) ** 0.5 / F ** 0.5), 5.0),
        "bias": gaussian(keys[7], (F,), 0.5, 3.0, (), jnp.float32),
        "part_map": draw_part_map(jax.random.fold_in(keys[9], 71), 0),
    }


def arrange_rows(hidden_block, pm):
    dest_hot = (pm[:, None] == jnp.arange(N_BAL)[None, :]).astype(jnp.int32)
    ranks = jnp.cumsum(dest_hot, axis=0) - dest_hot
    place = pm * CAP + jnp.sum(ranks * dest_hot, axis=1)
    select = (jnp.arange(N_BAL * CAP)[:, None] == place[None, :]).astype(jnp.float32)
    tiles = hidden_block.reshape(TR, TILE, F).astype(jnp.float32)
    placed = jnp.einsum('kt,tif->kif', select, tiles, precision=lax.Precision.HIGHEST)
    return placed.astype(jnp.bfloat16).reshape(N_BAL, CAP * TILE, F)


def reference(features, tile_values, tile_rows, tile_cols, tile_counts, w_self, w_neigh, bias, part_map):
    feats = features.reshape(N_BLK, TR, TILE, F)

    def one_block(inputs):
        values, rows_idx, cols_idx, counts = inputs
        live = jnp.arange(S)[None, :] < counts[:, None]
        row_hot = ((rows_idx[:, :, None] == jnp.arange(TR)[None, None, :]) & live[:, :, None]).astype(jnp.float32)

        def per_source(total, piece):
            vals, picks, hot, source = piece
            gathered = jnp.take(feats[source], picks, axis=0)
            prod = jnp.einsum('sij,sjf->sif', vals.astype(jnp.float32), gathered.astype(jnp.float32), precision=lax.Precision.HIGHEST)
            return total + jnp.einsum('st,sif->tif', hot, prod, precision=lax.Precision.HIGHEST), None

        start = jnp.zeros((TR, TILE, F), jnp.float32)
        total, unused = lax.scan(per_source, start, (values, cols_idx, row_hot, jnp.arange(N_BLK)))
        mass = jnp.sum(values.astype(jnp.float32), axis=-1)
        degree = 1.0 + jnp.einsum('cst,csi->ti', row_hot, mass, precision=lax.Precision.HIGHEST)
        return (total / degree[:, :, None]).astype(jnp.bfloat16).reshape(TR * TILE, F)

    mean_agg = lax.map(one_block, (tile_values, tile_rows, tile_cols, tile_counts)).reshape(N, F)
    pre = jnp.dot(features, w_self, preferred_element_type=jnp.float32)
    pre = pre + jnp.dot(mean_agg, w_neigh, preferred_element_type=jnp.float32) + bias
    hidden = jnp.maximum(pre, 0.0).astype(jnp.bfloat16).reshape(N_BLK, R, F)
    return jax.vmap(arrange_rows)(hidden, part_map)
```

```python
import functools
import jax
import jax.numpy as jnp
from jax import lax
from jax.experimental import pallas as pl
from jax.experimental.pallas import tpu as pltpu
from jax.sharding import PartitionSpec as P

TILE = 128
HALF = 64
MESH = pl.DeviceIdType.MESH


def from_behind(block, axis, distance):
    devices = range(lax.axis_size(axis))
    route = [((i - distance) % len(devices), i) for i in devices]
    return lax.ppermute(block, axis, route)


def advance(block, steps_by):
    return from_behind(block, "blk", steps_by)


def on_device(
    features, tile_values, tile_rows, tile_cols, tile_counts, w_self, w_neigh, bias, part_map
):
    n_blk = lax.axis_size("blk")
    n_bal = lax.axis_size("bal")
    here = lax.axis_index("blk")
    column = lax.axis_index("bal")
    width = features.shape[1]
    tiles_per = part_map.shape[1]
    values = tile_values[0]
    rows_idx = tile_rows[0]
    cols_idx = tile_cols[0]
    counts = tile_counts[0]
    slots = values.shape[1]
    live = jnp.arange(slots)[None, :] < counts[:, None]
    row_hot = (
        (rows_idx[:, :, None] == jnp.arange(tiles_per)[None, None, :]) & live[:, :, None]
    ).astype(jnp.float32)
    row_mass = jnp.einsum(
        "csij,j->csi", values, jnp.ones((TILE,), jnp.bfloat16), preferred_element_type=jnp.float32
    )
    degree = 1.0 + jnp.einsum("cst,csi->ti", row_hot, row_mass, precision=lax.Precision.HIGHEST)

    def absorb(total, block, source):
        tiles = block.reshape(tiles_per, TILE, width)
        vals = lax.dynamic_index_in_dim(values, source, 0, keepdims=False)
        picks = lax.dynamic_index_in_dim(cols_idx, source, 0, keepdims=False)
        targets = lax.dynamic_index_in_dim(rows_idx, source, 0, keepdims=False)
        alive = lax.dynamic_index_in_dim(live, source, 0, keepdims=False)
        gathered = jnp.take(tiles, picks, axis=0)
        prod = jnp.einsum("sij,sjf->sif", vals, gathered, preferred_element_type=jnp.float32)
        masked = jnp.where(alive[:, None, None], prod, 0.0)
        return total.at[targets].add(masked)

    empty = jnp.zeros((tiles_per, TILE, width), jnp.float32)

    def step_one(index, carry):
        total, block = carry
        total = absorb(total, block, (here - index) % n_blk)
        block = advance(block, 1)
        return (total, block)

    total, block = lax.fori_loop(0, n_blk - 1, step_one, (empty, features))
    total = absorb(total, block, (here - (n_blk - 1)) % n_blk)
    mean_agg = (total / degree[:, :, None]).astype(jnp.bfloat16).reshape(tiles_per * TILE, width)
    capacity = 2 * tiles_per // n_bal
    mapping = part_map[0]
    dest_hot = (mapping[:, None] == jnp.arange(n_bal)[None, :]).astype(jnp.int32)
    ranks = jnp.cumsum(dest_hot, axis=0) - dest_hot
    place = mapping * capacity + jnp.sum(ranks * dest_hot, axis=1)
    select = (jnp.arange(n_bal * capacity)[:, None] == place[None, :]).astype(jnp.bfloat16)
    col_start = column * width
    zeros_out = jnp.zeros((tiles_per * TILE, width), jnp.float32)
    carry = zeros_out
    mean_piece = lax.all_gather(mean_agg, "bal", axis=1, tiled=True)
    feat_piece = lax.all_gather(features, "bal", axis=1, tiled=True)
    count = mean_piece.shape[1]
    neigh_part = lax.dynamic_slice(w_neigh, (0, col_start), (count, width))
    self_part = lax.dynamic_slice(w_self, (0, col_start), (count, width))
    carry = jnp.dot(mean_piece, neigh_part, preferred_element_type=jnp.float32)
    pre = carry + jnp.dot(feat_piece, self_part, preferred_element_type=jnp.float32)
    pre = pre + lax.dynamic_slice_in_dim(bias, col_start, width)
    hidden = jnp.maximum(pre, 0.0).astype(jnp.bfloat16)
    tiles = hidden.reshape(tiles_per, TILE, width)
    placed = jnp.einsum("kt,tif->kif", select, tiles, preferred_element_type=jnp.float32)
    result = lax.all_to_all(
        placed.astype(jnp.bfloat16).reshape(n_bal, capacity * TILE, width),
        "bal",
        split_axis=0,
        concat_axis=2,
        tiled=True,
    )
    return result[None]


def tables(pm_ref, rows_ref, cols_ref, counts_ref, table, slots, cap):
    n_src = rows_ref.shape[0]
    table[...] = jnp.zeros(table.shape, jnp.int32)
    square = (TILE, TILE)
    lane = lax.broadcasted_iota(jnp.int32, square, 1)
    sub = lax.broadcasted_iota(jnp.int32, square, 0)

    def spread(row):
        return jnp.broadcast_to(row, square)

    def total(x):
        return jnp.sum(x, axis=0, keepdims=True)

    def flat(ref):
        return jnp.concatenate([ref[c : c + 1, :] for c in range(n_src)], axis=1)

    pm = pm_ref[...]
    pm = jnp.concatenate([pm, jnp.full((1, TILE - pm.shape[1]), 999, jnp.int32)], axis=1)
    pm_r = spread(pm)
    pm_c = pm_r.T
    earlier = jnp.where((pm_c == pm_r) & (sub < lane), 1, 0)
    place_c = spread(pm * cap + total(earlier)).T
    table[0:1, :] = total(jnp.where(place_c == lane, sub, 0))
    table[8:9, :] = total(jnp.where(pm_c == lane // cap, 1, 0))

    lane_row = lax.broadcasted_iota(jnp.int32, (1, TILE), 1)
    alive = jnp.zeros((1, TILE), jnp.int32)
    for c in range(n_src):
        alive = jnp.where(lane_row // slots == c, counts_ref[0, c], alive)
    rows_r = spread(flat(rows_ref))
    goes = total(jnp.where(rows_r == sub, place_c, 0))
    goes = jnp.where(lane_row % slots < alive, goes, 4096)
    goes_r = spread(goes)
    goes_c = goes_r.T
    rank_c = spread(total(jnp.where(goes_c * TILE + sub < goes_r * TILE + lane, 1, 0))).T
    pick = rank_c == lane
    source = (lane_row // slots) * HALF + flat(cols_ref)
    source_c = spread(source).T
    table[1:2, :] = total(jnp.where(pick, sub, 0))
    table[2:3, :] = total(jnp.where(pick, source_c, 0))
    mine = total(jnp.where(pick, goes_c, 0))
    before = total(jnp.where(rank_c + 1 == lane, goes_c, 0))
    table[3:4, :] = jnp.where((mine == before) & (lane_row % HALF != 0), 1, 0)
    upto = total(jnp.where(goes_c <= lane, 1, 0))
    below = total(jnp.where(goes_c < lane, 1, 0))
    left_end = jnp.minimum(upto, HALF)
    right_from = jnp.maximum(below, HALF)
    table[4:5, :] = jnp.maximum(left_end - 1, 0)
    table[5:6, :] = jnp.where(below < left_end, 1, 0)
    table[6:7, :] = jnp.maximum(upto - 1 - HALF, 0)
    table[7:8, :] = jnp.where(right_from < upto, 1, 0)


def fold(x):
    return jnp.concatenate([x[:HALF], x[HALF:]], axis=1)


def unfold(x):
    return jnp.concatenate([x[:, :HALF], x[:, HALF:]], axis=0)


def layer_kernel(
    cap, slots, n_y, n_q,
    feat, vals_hbm, rows_ref, cols_ref, counts_ref, ws_ref, wn_ref, bias_ref, pm_ref,
    out_hbm,
    vals, own, blocks, sums, degs, f_send, f_recv, m_send, m_recv, joined, pre, out_v,
    table_v, table,
    vals_sem, table_sem, out_sem,
    sib_send, sib_recv, y_send, y_recv, fwd_send, fwd_recv,
    fs_sem, fr_sem, ms_sem, mr_sem,
):
    here = lax.axis_index("blk")
    me = lax.axis_index("bal")
    n_bal = f_recv.shape[0]
    tiles = own.shape[0]
    sibling = here + 1 - 2 * (here % 2)
    across = (here + 2) % 4
    far = (sibling + 2) % 4
    y_tiles = tiles // n_y
    q_tiles = cap // n_q

    load_vals = pltpu.make_async_copy(vals_hbm, vals, vals_sem)
    load_vals.start()

    barrier = pltpu.get_barrier_semaphore()
    for peer in (sibling, across):
        pl.semaphore_signal(barrier, inc=1, device_id={"blk": peer}, device_id_type=MESH)

    def greet(o, _):
        pl.semaphore_signal(
            barrier, inc=1, device_id={"bal": (me + o) % n_bal}, device_id_type=MESH
        )
        return _

    lax.fori_loop(1, n_bal, greet, 0)

    tables(pm_ref, rows_ref, cols_ref, counts_ref, table_v, slots, cap)
    load_table = pltpu.make_async_copy(table_v, table, table_sem)
    load_table.start()

    def pack(t, _):
        x = fold(feat[pl.ds(pl.multiple_of(t * TILE, TILE), TILE), :])
        own[t] = x
        blocks[here * tiles + t] = x
        return _

    lax.fori_loop(0, tiles, pack, 0)
    load_table.wait()
    pl.semaphore_wait(barrier, n_bal + 1)

    def f_copy(o):
        d = (me + o) % n_bal
        return pltpu.make_async_remote_copy(
            f_send.at[o], f_recv.at[me], fs_sem.at[o], fr_sem.at[me],
            device_id={"bal": d}, device_id_type=MESH,
        )

    def f_arrival(o):
        s = (me + o) % n_bal
        return pltpu.make_async_remote_copy(
            f_send.at[o], f_recv.at[s], fs_sem.at[o], fr_sem.at[s],
            device_id={"bal": s}, device_id_type=MESH,
        )

    def y_copy(i):
        span = pl.ds(i * y_tiles, y_tiles)
        return pltpu.make_async_remote_copy(
            own.at[span], blocks.at[pl.ds(here * tiles + i * y_tiles, y_tiles)],
            y_send.at[i], y_recv.at[i],
            device_id={"blk": across}, device_id_type=MESH,
        )

    def y_arrival(i):
        return pltpu.make_async_remote_copy(
            own.at[pl.ds(i * y_tiles, y_tiles)],
            blocks.at[pl.ds(across * tiles + i * y_tiles, y_tiles)],
            y_send.at[i], y_recv.at[i],
            device_id={"blk": across}, device_id_type=MESH,
        )

    def fwd_copy(i):
        span = pl.ds(across * tiles + i * y_tiles, y_tiles)
        return pltpu.make_async_remote_copy(
            blocks.at[span], blocks.at[span], fwd_send.at[i], fwd_recv.at[i],
            device_id={"blk": sibling}, device_id_type=MESH,
        )

    def fwd_arrival(i):
        span = pl.ds(far * tiles + i * y_tiles, y_tiles)
        return pltpu.make_async_remote_copy(
            blocks.at[span], blocks.at[span], fwd_send.at[i], fwd_recv.at[i],
            device_id={"blk": sibling}, device_id_type=MESH,
        )

    sib_copy = pltpu.make_async_remote_copy(
        own, blocks.at[pl.ds(here * tiles, tiles)], sib_send, sib_recv,
        device_id={"blk": sibling}, device_id_type=MESH,
    )
    sib_arrival = pltpu.make_async_remote_copy(
        own, blocks.at[pl.ds(sibling * tiles, tiles)], sib_send, sib_recv,
        device_id={"blk": sibling}, device_id_type=MESH,
    )

    def start_y(i, _):
        y_copy(i).start()
        return _

    lax.fori_loop(0, n_y, start_y, 0)

    def send_f(o, _):
        d = (me + o) % n_bal

        def gather(k, _):
            f_send[o, k] = own[table[0, d * cap + k]]
            return _

        lax.fori_loop(0, cap, gather, 0)
        f_copy(o).start()
        return _

    lax.fori_loop(1, n_bal, send_f, 0)
    sib_copy.start()

    def keep_f(k, _):
        f_recv[me, k] = own[table[0, me * cap + k]]
        return _

    lax.fori_loop(0, cap, keep_f, 0)
    load_vals.wait()

    def pass_on(i, _):
        y_arrival(i).wait_recv()
        fwd_copy(i).start()
        return _

    lax.fori_loop(0, n_y, pass_on, 0)
    sib_arrival.wait_recv()

    def wait_fwd(i, _):
        fwd_arrival(i).wait_recv()
        return _

    lax.fori_loop(0, n_y, wait_fwd, 0)

    zeros = jnp.zeros((TILE, HALF), jnp.bfloat16)
    ones = jnp.ones((TILE, HALF), jnp.bfloat16)
    row_ones = jnp.concatenate(
        [jnp.concatenate([ones, zeros], axis=1), jnp.concatenate([zeros, ones], axis=1)], axis=0
    )
    is_left = lax.broadcasted_iota(jnp.int32, (1, TILE), 1) < HALF

    def absorb(j, carry):
        acc, deg = carry
        a = jnp.concatenate([vals[table[1, j]], vals[table[1, j + HALF]]], axis=1)
        x = unfold(blocks[table[2, j]])
        y = unfold(blocks[table[2, j + HALF]])
        rhs = jnp.concatenate(
            [jnp.concatenate([x, zeros], axis=1), jnp.concatenate([zeros, y], axis=1)], axis=0
        )
        rhs = jnp.concatenate([rhs, row_ones], axis=1)
        prod = jnp.dot(a, rhs, preferred_element_type=jnp.float32)
        keep = jnp.where(is_left, table[3, j], table[3, j + HALF]) > 0
        acc = jnp.where(keep, acc, 0.0) + prod[:, :TILE]
        deg = jnp.where(keep, deg, 0.0) + prod[:, TILE:]
        sums[j] = acc
        degs[j] = deg
        return acc, deg

    empty = jnp.zeros((TILE, TILE), jnp.float32)
    lax.fori_loop(0, HALF, absorb, (empty, empty))

    def mean_piece(p):
        left, right = table[4, p], table[6, p]
        has_left, has_right = table[5, p] > 0, table[7, p] > 0
        agg = jnp.where(has_left, sums[left][:, :HALF], 0.0) + jnp.where(
            has_right, sums[right][:, HALF:], 0.0
        )
        degree = 1.0 + (
            jnp.where(has_left, degs[left][:, :HALF], 0.0)
            + jnp.where(has_right, degs[right][:, HALF:], 0.0)
        )
        return fold((agg / degree).astype(jnp.bfloat16))

    def m_copy(q, o):
        span = pl.ds(q * q_tiles, q_tiles)
        return pltpu.make_async_remote_copy(
            m_send.at[o, span], m_recv.at[me, span], ms_sem.at[q, o], mr_sem.at[q, me],
            device_id={"bal": (me + o) % n_bal}, device_id_type=MESH,
        )

    def m_arrival(q, o):
        s = (me + o) % n_bal
        span = pl.ds(q * q_tiles, q_tiles)
        return pltpu.make_async_remote_copy(
            m_send.at[o, span], m_recv.at[s, span], ms_sem.at[q, o], mr_sem.at[q, s],
            device_id={"bal": s}, device_id_type=MESH,
        )

    def send_m(i, _):
        q = i // (n_bal - 1)
        o = 1 + i % (n_bal - 1)
        d = (me + o) % n_bal

        def fill(k, _):
            m_send[o, q * q_tiles + k] = mean_piece(d * cap + q * q_tiles + k)
            return _

        lax.fori_loop(0, q_tiles, fill, 0)
        m_copy(q, o).start()
        return _

    lax.fori_loop(0, n_q * (n_bal - 1), send_m, 0)

    def keep_m(k, _):
        m_recv[me, k] = mean_piece(me * cap + k)
        return _

    lax.fori_loop(0, cap, keep_m, 0)

    def wait_f(o, _):
        f_arrival(o).wait_recv()
        return _

    lax.fori_loop(1, n_bal, wait_f, 0)

    def join(recv, q):
        def one(kk, _):
            k = q * q_tiles + kk
            parts = [recv[d, k] for d in range(n_bal)]
            top = jnp.concatenate([x[:, :HALF] for x in parts], axis=1)
            bottom = jnp.concatenate([x[:, HALF:] for x in parts], axis=1)
            joined[kk] = jnp.concatenate([top, bottom], axis=0)
            return _

        lax.fori_loop(0, q_tiles, one, 0)
        return joined[...].reshape(q_tiles * TILE, joined.shape[2])

    rows = q_tiles * TILE

    def self_part(q, _):
        part = jnp.dot(join(f_recv, q), ws_ref[...], preferred_element_type=jnp.float32)
        pre[pl.ds(pl.multiple_of(q * rows, rows), rows), :] = part + bias_ref[...]
        return _

    lax.fori_loop(0, n_q, self_part, 0)
    live = table[8, me * cap]

    def out_copy(q):
        span = pl.ds(pl.multiple_of(q * rows, rows), rows)
        return pltpu.make_async_copy(out_v.at[span], out_hbm.at[0, 0, span], out_sem.at[q])

    def finish(q, _):
        def wait_m(o, _):
            m_arrival(q, o).wait_recv()
            return _

        lax.fori_loop(1, n_bal, wait_m, 0)
        span = pl.ds(pl.multiple_of(q * rows, rows), rows)
        part = jnp.dot(join(m_recv, q), wn_ref[...], preferred_element_type=jnp.float32)
        hidden = jnp.maximum(pre[span, :] + part, 0.0)
        row = q * rows + lax.broadcasted_iota(jnp.int32, (rows, 1), 0)
        out_v[span, :] = jnp.where(row < live * TILE, hidden, 0.0).astype(jnp.bfloat16)
        out_copy(q).start()
        return _

    lax.fori_loop(0, n_q, finish, 0)

    def settle_f(o, _):
        f_copy(o).wait_send()
        return _

    def settle_m(i, _):
        m_copy(i // (n_bal - 1), 1 + i % (n_bal - 1)).wait_send()
        return _

    def settle_y(i, _):
        y_copy(i).wait_send()
        fwd_copy(i).wait_send()
        return _

    def settle_out(q, _):
        out_copy(q).wait()
        return _

    lax.fori_loop(1, n_bal, settle_f, 0)
    lax.fori_loop(0, n_q * (n_bal - 1), settle_m, 0)
    lax.fori_loop(0, n_y, settle_y, 0)
    sib_copy.wait_send()
    lax.fori_loop(0, n_q, settle_out, 0)


def layer(
    features, tile_values, tile_rows, tile_cols, tile_counts, w_self, w_neigh, bias, part_map
):
    n_blk = lax.axis_size("blk")
    n_bal = lax.axis_size("bal")
    slots = tile_rows.shape[2]
    tiles = part_map.shape[1]
    cap = 2 * tiles // n_bal
    width = features.shape[1]
    total = w_self.shape[0]
    fits = (
        n_blk == 4 and n_blk * slots == TILE and tiles == HALF and width == HALF
        and n_bal * cap == TILE
    )
    if not fits:
        return on_device(
            features, tile_values, tile_rows, tile_cols, tile_counts, w_self, w_neigh, bias,
            part_map,
        )
    n_y, n_q = 4, 4
    bf16, f32 = jnp.bfloat16, jnp.float32
    vmem = pl.BlockSpec(memory_space=pltpu.VMEM)
    smem = pl.BlockSpec(memory_space=pltpu.SMEM)
    hbm = pl.BlockSpec(memory_space=pl.ANY)
    dma = pltpu.SemaphoreType.DMA
    piece = (HALF, TILE)
    return pl.pallas_call(
        functools.partial(layer_kernel, cap, slots, n_y, n_q),
        out_shape=jax.ShapeDtypeStruct((1, 1, cap * TILE, total), bf16),
        in_specs=[vmem, hbm, vmem, vmem, smem, vmem, vmem, vmem, vmem],
        out_specs=hbm,
        scratch_shapes=[
            pltpu.VMEM((n_blk * slots, TILE, TILE), bf16),
            pltpu.VMEM((tiles,) + piece, bf16),
            pltpu.VMEM((n_blk * tiles,) + piece, bf16),
            pltpu.VMEM((HALF, TILE, TILE), f32),
            pltpu.VMEM((HALF, TILE, TILE), f32),
            pltpu.VMEM((n_bal, cap) + piece, bf16),
            pltpu.VMEM((n_bal, cap) + piece, bf16),
            pltpu.VMEM((n_bal, cap) + piece, bf16),
            pltpu.VMEM((n_bal, cap) + piece, bf16),
            pltpu.VMEM((cap // n_q, TILE, total), bf16),
            pltpu.VMEM((cap * TILE, total), f32),
            pltpu.VMEM((cap * TILE, total), bf16),
            pltpu.VMEM((16, TILE), jnp.int32),
            pltpu.SMEM((16, TILE), jnp.int32),
            dma, dma, dma((n_q,)),
            dma, dma, dma((n_y,)), dma((n_y,)), dma((n_y,)), dma((n_y,)),
            dma((n_bal,)), dma((n_bal,)), dma((n_q, n_bal)), dma((n_q, n_bal)),
        ],
        compiler_params=pltpu.CompilerParams(
            collective_id=0, has_side_effects=True, vmem_limit_bytes=52 * 2**20
        ),
        cost_estimate=pl.CostEstimate(
            flops=4 * cap * TILE * total * total, bytes_accessed=12 * 2**20, transcendentals=0
        ),
    )(
        features,
        tile_values.reshape(n_blk * slots, TILE, TILE),
        tile_rows[0],
        tile_cols[0],
        tile_counts,
        w_self,
        w_neigh,
        bias.reshape(1, total),
        part_map,
    )


def solution(mesh):
    placed = (
        P("blk", "bal"),
        P("blk", None, None, None, None),
        P("blk", None, None),
        P("blk", None, None),
        P("blk", None),
        P(),
        P(),
        P(),
        P("blk", None),
    )
    return jax.shard_map(
        layer,
        mesh=mesh,
        in_specs=placed,
        out_specs=P("blk", "bal", None, None),
        check_vma=False,
    )
```

```python
import functools
import jax
import jax.numpy as jnp
from jax import lax
from jax.experimental import pallas as pl
from jax.experimental.pallas import tpu as pltpu
from jax.sharding import PartitionSpec as P

TILE = 128
HALF = 64
MESH = pl.DeviceIdType.MESH


def from_behind(block, axis, distance):
    devices = range(lax.axis_size(axis))
    route = [((i - distance) % len(devices), i) for i in devices]
    return lax.ppermute(block, axis, route)


def advance(block, steps_by):
    return from_behind(block, "blk", steps_by)


def on_device(
    features, tile_values, tile_rows, tile_cols, tile_counts, w_self, w_neigh, bias, part_map
):
    n_blk = lax.axis_size("blk")
    n_bal = lax.axis_size("bal")
    here = lax.axis_index("blk")
    column = lax.axis_index("bal")
    width = features.shape[1]
    tiles_per = part_map.shape[1]
    values = tile_values[0]
    rows_idx = tile_rows[0]
    cols_idx = tile_cols[0]
    counts = tile_counts[0]
    slots = values.shape[1]
    live = jnp.arange(slots)[None, :] < counts[:, None]
    row_hot = (
        (rows_idx[:, :, None] == jnp.arange(tiles_per)[None, None, :]) & live[:, :, None]
    ).astype(jnp.float32)
    row_mass = jnp.einsum(
        "csij,j->csi", values, jnp.ones((TILE,), jnp.bfloat16), preferred_element_type=jnp.float32
    )
    degree = 1.0 + jnp.einsum("cst,csi->ti", row_hot, row_mass, precision=lax.Precision.HIGHEST)

    def absorb(total, block, source):
        tiles = block.reshape(tiles_per, TILE, width)
        vals = lax.dynamic_index_in_dim(values, source, 0, keepdims=False)
        picks = lax.dynamic_index_in_dim(cols_idx, source, 0, keepdims=False)
        targets = lax.dynamic_index_in_dim(rows_idx, source, 0, keepdims=False)
        alive = lax.dynamic_index_in_dim(live, source, 0, keepdims=False)
        gathered = jnp.take(tiles, picks, axis=0)
        prod = jnp.einsum("sij,sjf->sif", vals, gathered, preferred_element_type=jnp.float32)
        masked = jnp.where(alive[:, None, None], prod, 0.0)
        return total.at[targets].add(masked)

    empty = jnp.zeros((tiles_per, TILE, width), jnp.float32)

    def step_one(index, carry):
        total, block = carry
        total = absorb(total, block, (here - index) % n_blk)
        block = advance(block, 1)
        return (total, block)

    total, block = lax.fori_loop(0, n_blk - 1, step_one, (empty, features))
    total = absorb(total, block, (here - (n_blk - 1)) % n_blk)
    mean_agg = (total / degree[:, :, None]).astype(jnp.bfloat16).reshape(tiles_per * TILE, width)
    capacity = 2 * tiles_per // n_bal
    mapping = part_map[0]
    dest_hot = (mapping[:, None] == jnp.arange(n_bal)[None, :]).astype(jnp.int32)
    ranks = jnp.cumsum(dest_hot, axis=0) - dest_hot
    place = mapping * capacity + jnp.sum(ranks * dest_hot, axis=1)
    select = (jnp.arange(n_bal * capacity)[:, None] == place[None, :]).astype(jnp.bfloat16)
    col_start = column * width
    zeros_out = jnp.zeros((tiles_per * TILE, width), jnp.float32)
    carry = zeros_out
    mean_piece = lax.all_gather(mean_agg, "bal", axis=1, tiled=True)
    feat_piece = lax.all_gather(features, "bal", axis=1, tiled=True)
    count = mean_piece.shape[1]
    neigh_part = lax.dynamic_slice(w_neigh, (0, col_start), (count, width))
    self_part = lax.dynamic_slice(w_self, (0, col_start), (count, width))
    carry = jnp.dot(mean_piece, neigh_part, preferred_element_type=jnp.float32)
    pre = carry + jnp.dot(feat_piece, self_part, preferred_element_type=jnp.float32)
    pre = pre + lax.dynamic_slice_in_dim(bias, col_start, width)
    hidden = jnp.maximum(pre, 0.0).astype(jnp.bfloat16)
    tiles = hidden.reshape(tiles_per, TILE, width)
    placed = jnp.einsum("kt,tif->kif", select, tiles, preferred_element_type=jnp.float32)
    result = lax.all_to_all(
        placed.astype(jnp.bfloat16).reshape(n_bal, capacity * TILE, width),
        "bal",
        split_axis=0,
        concat_axis=2,
        tiled=True,
    )
    return result[None]


def tables(pm_ref, rows_ref, cols_ref, counts_ref, table, slots, cap):
    n_src = rows_ref.shape[0]
    table[...] = jnp.zeros(table.shape, jnp.int32)
    square = (TILE, TILE)
    lane = lax.broadcasted_iota(jnp.int32, square, 1)
    sub = lax.broadcasted_iota(jnp.int32, square, 0)

    def spread(row):
        return jnp.broadcast_to(row, square)

    def total(x):
        return jnp.sum(x, axis=0, keepdims=True)

    def flat(ref):
        return jnp.concatenate([ref[c : c + 1, :] for c in range(n_src)], axis=1)

    pm = pm_ref[...]
    pm = jnp.concatenate([pm, jnp.full((1, TILE - pm.shape[1]), 999, jnp.int32)], axis=1)
    pm_r = spread(pm)
    pm_c = pm_r.T
    earlier = jnp.where((pm_c == pm_r) & (sub < lane), 1, 0)
    place_c = spread(pm * cap + total(earlier)).T
    table[0:1, :] = total(jnp.where(place_c == lane, sub, 0))
    table[8:9, :] = total(jnp.where(pm_c == lane // cap, 1, 0))

    lane_row = lax.broadcasted_iota(jnp.int32, (1, TILE), 1)
    alive = jnp.zeros((1, TILE), jnp.int32)
    for c in range(n_src):
        alive = jnp.where(lane_row // slots == c, counts_ref[0, c], alive)
    rows_r = spread(flat(rows_ref))
    goes = total(jnp.where(rows_r == sub, place_c, 0))
    goes = jnp.where(lane_row % slots < alive, goes, 4096)
    goes_r = spread(goes)
    goes_c = goes_r.T
    rank_c = spread(total(jnp.where(goes_c * TILE + sub < goes_r * TILE + lane, 1, 0))).T
    pick = rank_c == lane
    source = (lane_row // slots) * HALF + flat(cols_ref)
    source_c = spread(source).T
    table[1:2, :] = total(jnp.where(pick, sub, 0))
    table[2:3, :] = total(jnp.where(pick, source_c, 0))
    mine = total(jnp.where(pick, goes_c, 0))
    before = total(jnp.where(rank_c + 1 == lane, goes_c, 0))
    table[3:4, :] = jnp.where((mine == before) & (lane_row % HALF != 0), 1, 0)
    upto = total(jnp.where(goes_c <= lane, 1, 0))
    below = total(jnp.where(goes_c < lane, 1, 0))
    left_end = jnp.minimum(upto, HALF)
    right_from = jnp.maximum(below, HALF)
    table[4:5, :] = jnp.maximum(left_end - 1, 0)
    table[5:6, :] = jnp.where(below < left_end, 1, 0)
    table[6:7, :] = jnp.maximum(upto - 1 - HALF, 0)
    table[7:8, :] = jnp.where(right_from < upto, 1, 0)


def layer_kernel(
    cap, slots, n_y, n_m, n_q, swap,
    feat, vals_hbm, rows_ref, cols_ref, counts_ref, ws_ref, wn_ref, bias_ref, pm_ref,
    out_hbm,
    vals, own, mirror, blocks, sums, f_in, f_out, f_recv, m_in, m_out, m_recv, pre, out_v,
    table_v, table,
    vals_sem, table_sem, mir_sem, out_sem,
    swap_send, swap_recv, sib_send, sib_recv, y_send, y_recv, fwd_send, fwd_recv,
    msib_send, msib_recv, my_send, my_recv, mfwd_send, mfwd_recv,
    fs_sem, fr_sem, fms_sem, fmr_sem, ms_sem, mr_sem, mms_sem, mmr_sem,
):
    here = lax.axis_index("blk")
    me = lax.axis_index("bal")
    tiles, width, _ = own.shape
    wide = width + swap
    stay = width - swap
    n_bal = f_recv.shape[1] // width
    half = n_bal // 2
    base = me // half * half
    partner = (me + half) % n_bal
    sibling = here + 1 - 2 * (here % 2)
    across = (here + 2) % 4
    far = (sibling + 2) % 4
    y_tiles = tiles // n_y
    m_tiles = tiles // n_m
    q_tiles = cap // n_q
    own_rows = pl.ds(pl.multiple_of(me * width, width), width)
    mirror_rows = pl.ds(pl.multiple_of(partner * width + stay, 16), swap)

    def near(o):
        return base + (me + o) % half

    def other(o):
        return (base + half) % n_bal + (me + o) % half

    def each(first, last, body):
        def step(i, carry):
            body(i)
            return carry

        lax.fori_loop(first, last, step, 0)

    def remote(src, dst, send, recv, axis, peer):
        return pltpu.make_async_remote_copy(
            src, dst, send, recv, device_id={axis: peer}, device_id_type=MESH
        )

    load_vals = pltpu.make_async_copy(vals_hbm, vals, vals_sem)
    load_vals.start()

    barrier = pltpu.get_barrier_semaphore()
    for peer in (sibling, across):
        pl.semaphore_signal(barrier, inc=1, device_id={"blk": peer}, device_id_type=MESH)
    each(
        1, n_bal,
        lambda o: pl.semaphore_signal(
            barrier, inc=1, device_id={"bal": (me + o) % n_bal}, device_id_type=MESH
        ),
    )

    def pack(t):
        x = feat[:, pl.ds(pl.multiple_of(t * TILE, TILE), TILE)]
        own[t] = x
        blocks[here * tiles + t, :width, :] = x

    each(0, tiles, pack)
    pl.semaphore_wait(barrier, n_bal + 1)

    def swap_copy(i):
        span = pl.ds(i * m_tiles, m_tiles)
        return remote(
            own.at[span, pl.ds(stay, swap)], mirror.at[span],
            swap_send.at[i], swap_recv.at[i], "bal", partner,
        )

    def y_copy(i, whose):
        return remote(
            own.at[pl.ds(i * y_tiles, y_tiles)],
            blocks.at[pl.ds(whose * tiles + i * y_tiles, y_tiles), pl.ds(0, width)],
            y_send.at[i], y_recv.at[i], "blk", across,
        )

    def fwd_copy(i, whose):
        span = pl.ds(whose * tiles + i * y_tiles, y_tiles)
        part = blocks.at[span, pl.ds(0, width)]
        return remote(part, part, fwd_send.at[i], fwd_recv.at[i], "blk", sibling)

    def sib_copy(whose):
        return remote(
            own, blocks.at[pl.ds(whose * tiles, tiles), pl.ds(0, width)],
            sib_send, sib_recv, "blk", sibling,
        )

    def my_copy(i, whose):
        return remote(
            mirror.at[pl.ds(i * m_tiles, m_tiles)],
            blocks.at[pl.ds(whose * tiles + i * m_tiles, m_tiles), pl.ds(width, swap)],
            my_send.at[i], my_recv.at[i], "blk", across,
        )

    def msib_copy(i, whose):
        return remote(
            mirror.at[pl.ds(i * m_tiles, m_tiles)],
            blocks.at[pl.ds(whose * tiles + i * m_tiles, m_tiles), pl.ds(width, swap)],
            msib_send.at[i], msib_recv.at[i], "blk", sibling,
        )

    def mfwd_copy(i, whose):
        span = pl.ds(whose * tiles + i * m_tiles, m_tiles)
        part = blocks.at[span, pl.ds(width, swap)]
        return remote(part, part, mfwd_send.at[i], mfwd_recv.at[i], "blk", sibling)

    def f_near(o, whose):
        rows = pl.ds(pl.multiple_of(whose * width, width), width)
        return remote(
            f_in.at[o, :, pl.ds(0, width)], f_recv.at[:, rows],
            fs_sem.at[o], fr_sem.at[whose], "bal", near(o),
        )

    def f_near_mirror(o, whose):
        rows = pl.ds(pl.multiple_of((whose + half) % n_bal * width + stay, 16), swap)
        return remote(
            f_in.at[o, :, pl.ds(width, swap)], f_recv.at[:, rows],
            fms_sem.at[o], fmr_sem.at[whose], "bal", near(o),
        )

    def f_other(o, whose):
        rows = pl.ds(pl.multiple_of(whose * width, width), stay)
        return remote(
            f_out.at[o], f_recv.at[:, rows],
            fs_sem.at[half + o], fr_sem.at[whose], "bal", other(o),
        )

    def m_near(q, o, whose):
        span = pl.ds(q * q_tiles, q_tiles)
        rows = pl.ds(pl.multiple_of(whose * width, width), width)
        return remote(
            m_in.at[o, span, pl.ds(0, width)], m_recv.at[span, rows],
            ms_sem.at[q, o], mr_sem.at[q, whose], "bal", near(o),
        )

    def m_near_mirror(q, o, whose):
        span = pl.ds(q * q_tiles, q_tiles)
        rows = pl.ds(pl.multiple_of((whose + half) % n_bal * width + stay, 16), swap)
        return remote(
            m_in.at[o, span, pl.ds(width, swap)], m_recv.at[span, rows],
            mms_sem.at[q, o], mmr_sem.at[q, whose], "bal", near(o),
        )

    def m_other(q, o, whose):
        span = pl.ds(q * q_tiles, q_tiles)
        rows = pl.ds(pl.multiple_of(whose * width, width), stay)
        return remote(
            m_out.at[o, span], m_recv.at[span, rows],
            ms_sem.at[q, half + o], mr_sem.at[q, whose], "bal", other(o),
        )

    each(0, n_m, lambda i: swap_copy(i).start())
    each(0, n_y, lambda i: y_copy(i, here).start())
    sib_copy(here).start()

    tables(pm_ref, rows_ref, cols_ref, counts_ref, table_v, slots, cap)
    load_table = pltpu.make_async_copy(table_v, table, table_sem)
    load_table.start()
    load_table.wait()

    def send_f_near(o):
        def gather(k):
            f_in[o, k, :width, :] = own[table[0, near(o) * cap + k]]

        each(0, cap, gather)
        f_near(o, me).start()

    def fill_f_other(o):
        def gather(k):
            f_out[o, k] = own[table[0, other(o) * cap + k]][:stay]

        each(0, cap, gather)

    def keep_f(k):
        f_recv[k, own_rows, :] = own[table[0, me * cap + k]]

    each(1, half, send_f_near)
    if stay:
        each(0, half, fill_f_other)
    each(0, cap, keep_f)
    load_vals.wait()

    def pass_on(i):
        y_copy(i, across).wait_recv()
        fwd_copy(i, across).start()

    def take_mirror(i):
        swap_copy(i).wait_recv()
        my_copy(i, here).start()
        msib_copy(i, here).start()

    each(0, n_y, pass_on)
    each(0, n_m, take_mirror)
    if stay:
        each(0, half, lambda o: f_other(o, me).start())
    keep_mirror = pltpu.make_async_copy(
        mirror, blocks.at[pl.ds(here * tiles, tiles), pl.ds(width, swap)], mir_sem
    )
    keep_mirror.start()

    def send_f_mirror(o):
        def gather(k):
            f_in[o, k, width:, :] = mirror[table[0, near(o) * cap + k]]

        each(0, cap, gather)
        f_near_mirror(o, me).start()

    def keep_f_mirror(k):
        f_recv[k, mirror_rows, :] = mirror[table[0, me * cap + k]]

    each(1, half, send_f_mirror)
    each(0, cap, keep_f_mirror)

    def pass_mirror_on(i):
        my_copy(i, across).wait_recv()
        mfwd_copy(i, across).start()

    each(0, n_m, pass_mirror_on)
    sib_copy(sibling).wait_recv()
    each(0, n_y, lambda i: fwd_copy(i, far).wait_recv())
    each(0, n_m, lambda i: msib_copy(i, sibling).wait_recv())
    each(0, n_m, lambda i: mfwd_copy(i, far).wait_recv())
    keep_mirror.wait()

    zeros = jnp.zeros((wide, TILE), jnp.bfloat16)
    in_top = lax.broadcasted_iota(jnp.int32, (16, 2 * TILE), 0) < 8
    in_left = lax.broadcasted_iota(jnp.int32, (16, 2 * TILE), 1) < TILE
    ones = jnp.where(in_top == in_left, 1.0, 0.0).astype(jnp.bfloat16)
    deg_left = lax.broadcasted_iota(jnp.int32, (16, TILE), 0) < 8

    def absorb(j, carry):
        left, right, deg = carry
        a = jnp.concatenate([vals[table[1, j]], vals[table[1, j + HALF]]], axis=1)
        x = jnp.concatenate([blocks[table[2, j]], zeros], axis=1)
        y = jnp.concatenate([zeros, blocks[table[2, j + HALF]]], axis=1)
        lhs = jnp.concatenate([x, y, ones], axis=0)
        prod = lax.dot_general(
            lhs, a, (((1,), (1,)), ((), ())), preferred_element_type=jnp.float32
        )
        keep_left, keep_right = table[3, j], table[3, j + HALF]
        left = jnp.where(keep_left > 0, left, 0.0) + prod[:wide]
        right = jnp.where(keep_right > 0, right, 0.0) + prod[wide : 2 * wide]
        deg = jnp.where(jnp.where(deg_left, keep_left, keep_right) > 0, deg, 0.0)
        deg = deg + prod[2 * wide :]
        sums[j, :wide, :] = left
        sums[j, wide : 2 * wide, :] = right
        sums[j, 2 * wide :, :] = deg
        return left, right, deg

    empty = jnp.zeros((wide, TILE), jnp.float32)
    lax.fori_loop(0, HALF, absorb, (empty, empty, jnp.zeros((16, TILE), jnp.float32)))

    def mean_piece(p, rows):
        left, right = sums.at[table[4, p]], sums.at[table[6, p]]
        has_left, has_right = table[5, p] > 0, table[7, p] > 0
        agg = jnp.where(has_left, left[:rows, :], 0.0) + jnp.where(
            has_right, right[wide : wide + rows, :], 0.0
        )
        degree = (
            1.0
            + jnp.where(has_left, left[2 * wide : 2 * wide + 8, :], 0.0)
            + jnp.where(has_right, right[2 * wide + 8 :, :], 0.0)
        )
        return (agg / degree[:1]).astype(jnp.bfloat16)

    def send_m(q):
        def to_other(o):
            def fill(k):
                m_out[o, q * q_tiles + k] = mean_piece(other(o) * cap + q * q_tiles + k, stay)

            each(0, q_tiles, fill)
            m_other(q, o, me).start()

        def to_near(o):
            def fill(k):
                m_in[o, q * q_tiles + k] = mean_piece(near(o) * cap + q * q_tiles + k, wide)

            each(0, q_tiles, fill)
            m_near(q, o, me).start()
            m_near_mirror(q, o, me).start()

        if stay:
            each(0, half, to_other)
        each(1, half, to_near)

    each(0, n_q, send_m)

    def keep_m(k):
        piece = mean_piece(me * cap + k, wide)
        m_recv[k, own_rows, :] = piece[:width]
        m_recv[k, mirror_rows, :] = piece[width:]

    each(0, cap, keep_m)

    def wait_f_near(o):
        f_near(o, near(o)).wait_recv()
        f_near_mirror(o, near(o)).wait_recv()

    each(1, half, wait_f_near)
    if stay:
        each(0, half, lambda o: f_other(o, other(o)).wait_recv())

    rows = q_tiles * TILE

    def times(recv, q, weight):
        x = jnp.concatenate([recv[q * q_tiles + k] for k in range(q_tiles)], axis=1)
        return lax.dot_general(
            x, weight[...], (((0,), (0,)), ((), ())), preferred_element_type=jnp.float32
        )

    def chunk(q):
        return pl.ds(pl.multiple_of(q * rows, rows), rows)

    def self_part(q):
        pre[chunk(q), :] = times(f_recv, q, ws_ref) + bias_ref[...]

    each(0, n_q, self_part)
    live = table[8, me * cap]

    def out_copy(q):
        return pltpu.make_async_copy(
            out_v.at[chunk(q)], out_hbm.at[0, 0, chunk(q)], out_sem.at[q]
        )

    def finish(q):
        def wait_near(o):
            m_near(q, o, near(o)).wait_recv()
            m_near_mirror(q, o, near(o)).wait_recv()

        each(1, half, wait_near)
        if stay:
            each(0, half, lambda o: m_other(q, o, other(o)).wait_recv())
        hidden = jnp.maximum(pre[chunk(q), :] + times(m_recv, q, wn_ref), 0.0)
        row = q * rows + lax.broadcasted_iota(jnp.int32, (rows, 1), 0)
        out_v[chunk(q), :] = jnp.where(row < live * TILE, hidden, 0.0).astype(jnp.bfloat16)
        out_copy(q).start()

    each(0, n_q, finish)

    def settle_near(o):
        f_near(o, me).wait_send()
        f_near_mirror(o, me).wait_send()

        def one(q):
            m_near(q, o, me).wait_send()
            m_near_mirror(q, o, me).wait_send()

        each(0, n_q, one)

    def settle_other(o):
        f_other(o, me).wait_send()
        each(0, n_q, lambda q: m_other(q, o, me).wait_send())

    def settle_y(i):
        y_copy(i, here).wait_send()
        fwd_copy(i, across).wait_send()

    def settle_mirror(i):
        swap_copy(i).wait_send()
        my_copy(i, here).wait_send()
        msib_copy(i, here).wait_send()
        mfwd_copy(i, across).wait_send()

    each(1, half, settle_near)
    if stay:
        each(0, half, settle_other)
    each(0, n_y, settle_y)
    each(0, n_m, settle_mirror)
    sib_copy(here).wait_send()
    each(0, n_q, lambda q: out_copy(q).wait())


def layer(
    features, tile_values, tile_rows, tile_cols, tile_counts, w_self, w_neigh, bias, part_map
):
    n_blk = lax.axis_size("blk")
    n_bal = lax.axis_size("bal")
    slots = tile_rows.shape[2]
    tiles = part_map.shape[1]
    cap = 2 * tiles // n_bal
    width = features.shape[1]
    total = w_self.shape[0]
    fits = (
        n_blk == 4 and n_blk * slots == TILE and tiles == HALF and width == HALF
        and n_bal * cap == TILE
    )
    if not fits:
        return on_device(
            features, tile_values, tile_rows, tile_cols, tile_counts, w_self, w_neigh, bias,
            part_map,
        )
    n_y, n_m, n_q = 4, 2, 4
    swap = width // 2
    wide, stay, half = width + swap, width - swap, n_bal // 2
    bf16, f32 = jnp.bfloat16, jnp.float32
    vmem = pl.BlockSpec(memory_space=pltpu.VMEM)
    smem = pl.BlockSpec(memory_space=pltpu.SMEM)
    hbm = pl.BlockSpec(memory_space=pl.ANY)
    dma = pltpu.SemaphoreType.DMA
    return pl.pallas_call(
        functools.partial(layer_kernel, cap, slots, n_y, n_m, n_q, swap),
        out_shape=jax.ShapeDtypeStruct((1, 1, cap * TILE, total), bf16),
        in_specs=[vmem, hbm, vmem, vmem, smem, vmem, vmem, vmem, vmem],
        out_specs=hbm,
        scratch_shapes=[
            pltpu.VMEM((n_blk * slots, TILE, TILE), bf16),
            pltpu.VMEM((tiles, width, TILE), bf16),
            pltpu.VMEM((tiles, swap, TILE), bf16),
            pltpu.VMEM((n_blk * tiles, wide, TILE), bf16),
            pltpu.VMEM((HALF, 2 * wide + 16, TILE), f32),
            pltpu.VMEM((half, cap, wide, TILE), bf16),
            pltpu.VMEM((half, cap, max(stay, 16), TILE), bf16),
            pltpu.VMEM((cap, total, TILE), bf16),
            pltpu.VMEM((half, cap, wide, TILE), bf16),
            pltpu.VMEM((half, cap, max(stay, 16), TILE), bf16),
            pltpu.VMEM((cap, total, TILE), bf16),
            pltpu.VMEM((cap * TILE, total), f32),
            pltpu.VMEM((cap * TILE, total), bf16),
            pltpu.VMEM((16, TILE), jnp.int32),
            pltpu.SMEM((16, TILE), jnp.int32),
            dma, dma, dma, dma((n_q,)),
            dma((n_m,)), dma((n_m,)), dma, dma, dma((n_y,)), dma((n_y,)), dma((n_y,)), dma((n_y,)),
            dma((n_m,)), dma((n_m,)), dma((n_m,)), dma((n_m,)), dma((n_m,)), dma((n_m,)),
            dma((n_bal,)), dma((n_bal,)), dma((half,)), dma((n_bal,)),
            dma((n_q, n_bal)), dma((n_q, n_bal)), dma((n_q, half)), dma((n_q, n_bal)),
        ],
        compiler_params=pltpu.CompilerParams(
            collective_id=0, has_side_effects=True, vmem_limit_bytes=56 * 2**20
        ),
        cost_estimate=pl.CostEstimate(
            flops=4 * cap * TILE * total * total, bytes_accessed=12 * 2**20, transcendentals=0
        ),
    )(
        features.T,
        tile_values.reshape(n_blk * slots, TILE, TILE),
        tile_rows[0],
        tile_cols[0],
        tile_counts,
        w_self,
        w_neigh,
        bias.reshape(1, total),
        part_map,
    )


def solution(mesh):
    placed = (
        P("blk", "bal"),
        P("blk", None, None, None, None),
        P("blk", None, None),
        P("blk", None, None),
        P("blk", None),
        P(),
        P(),
        P(),
        P("blk", None),
    )
    return jax.shard_map(
        layer,
        mesh=mesh,
        in_specs=placed,
        out_specs=P("blk", "bal", None, None),
        check_vma=False,
    )
```

```python
import functools
import jax
import jax.numpy as jnp
from jax import lax
from jax.experimental import pallas as pl
from jax.experimental.pallas import tpu as pltpu
from jax.sharding import PartitionSpec as P

TILE = 128
HALF = 64
MESH = pl.DeviceIdType.MESH


def from_behind(block, axis, distance):
    devices = range(lax.axis_size(axis))
    route = [((i - distance) % len(devices), i) for i in devices]
    return lax.ppermute(block, axis, route)


def advance(block, steps_by):
    return from_behind(block, "blk", steps_by)


def on_device(
    features, tile_values, tile_rows, tile_cols, tile_counts, w_self, w_neigh, bias, part_map
):
    n_blk = lax.axis_size("blk")
    n_bal = lax.axis_size("bal")
    here = lax.axis_index("blk")
    column = lax.axis_index("bal")
    width = features.shape[1]
    tiles_per = part_map.shape[1]
    values = tile_values[0]
    rows_idx = tile_rows[0]
    cols_idx = tile_cols[0]
    counts = tile_counts[0]
    slots = values.shape[1]
    live = jnp.arange(slots)[None, :] < counts[:, None]
    row_hot = (
        (rows_idx[:, :, None] == jnp.arange(tiles_per)[None, None, :]) & live[:, :, None]
    ).astype(jnp.float32)
    row_mass = jnp.einsum(
        "csij,j->csi", values, jnp.ones((TILE,), jnp.bfloat16), preferred_element_type=jnp.float32
    )
    degree = 1.0 + jnp.einsum("cst,csi->ti", row_hot, row_mass, precision=lax.Precision.HIGHEST)

    def absorb(total, block, source):
        tiles = block.reshape(tiles_per, TILE, width)
        vals = lax.dynamic_index_in_dim(values, source, 0, keepdims=False)
        picks = lax.dynamic_index_in_dim(cols_idx, source, 0, keepdims=False)
        targets = lax.dynamic_index_in_dim(rows_idx, source, 0, keepdims=False)
        alive = lax.dynamic_index_in_dim(live, source, 0, keepdims=False)
        gathered = jnp.take(tiles, picks, axis=0)
        prod = jnp.einsum("sij,sjf->sif", vals, gathered, preferred_element_type=jnp.float32)
        masked = jnp.where(alive[:, None, None], prod, 0.0)
        return total.at[targets].add(masked)

    empty = jnp.zeros((tiles_per, TILE, width), jnp.float32)

    def step_one(index, carry):
        total, block = carry
        total = absorb(total, block, (here - index) % n_blk)
        block = advance(block, 1)
        return (total, block)

    total, block = lax.fori_loop(0, n_blk - 1, step_one, (empty, features))
    total = absorb(total, block, (here - (n_blk - 1)) % n_blk)
    mean_agg = (total / degree[:, :, None]).astype(jnp.bfloat16).reshape(tiles_per * TILE, width)
    capacity = 2 * tiles_per // n_bal
    mapping = part_map[0]
    dest_hot = (mapping[:, None] == jnp.arange(n_bal)[None, :]).astype(jnp.int32)
    ranks = jnp.cumsum(dest_hot, axis=0) - dest_hot
    place = mapping * capacity + jnp.sum(ranks * dest_hot, axis=1)
    select = (jnp.arange(n_bal * capacity)[:, None] == place[None, :]).astype(jnp.bfloat16)
    col_start = column * width
    zeros_out = jnp.zeros((tiles_per * TILE, width), jnp.float32)
    carry = zeros_out
    mean_piece = lax.all_gather(mean_agg, "bal", axis=1, tiled=True)
    feat_piece = lax.all_gather(features, "bal", axis=1, tiled=True)
    count = mean_piece.shape[1]
    neigh_part = lax.dynamic_slice(w_neigh, (0, col_start), (count, width))
    self_part = lax.dynamic_slice(w_self, (0, col_start), (count, width))
    carry = jnp.dot(mean_piece, neigh_part, preferred_element_type=jnp.float32)
    pre = carry + jnp.dot(feat_piece, self_part, preferred_element_type=jnp.float32)
    pre = pre + lax.dynamic_slice_in_dim(bias, col_start, width)
    hidden = jnp.maximum(pre, 0.0).astype(jnp.bfloat16)
    tiles = hidden.reshape(tiles_per, TILE, width)
    placed = jnp.einsum("kt,tif->kif", select, tiles, preferred_element_type=jnp.float32)
    result = lax.all_to_all(
        placed.astype(jnp.bfloat16).reshape(n_bal, capacity * TILE, width),
        "bal",
        split_axis=0,
        concat_axis=2,
        tiled=True,
    )
    return result[None]


def tables(pm_ref, rows_ref, cols_ref, counts_ref, table, slots, cap):
    n_src = rows_ref.shape[0]
    table[...] = jnp.zeros(table.shape, jnp.int32)
    square = (TILE, TILE)
    lane = lax.broadcasted_iota(jnp.int32, square, 1)
    sub = lax.broadcasted_iota(jnp.int32, square, 0)

    def spread(row):
        return jnp.broadcast_to(row, square)

    def total(x):
        return jnp.sum(x, axis=0, keepdims=True)

    def flat(ref):
        return jnp.concatenate([ref[c : c + 1, :] for c in range(n_src)], axis=1)

    pm = pm_ref[...]
    pm = jnp.concatenate([pm, jnp.full((1, TILE - pm.shape[1]), 999, jnp.int32)], axis=1)
    pm_r = spread(pm)
    pm_c = pm_r.T
    earlier = jnp.where((pm_c == pm_r) & (sub < lane), 1, 0)
    place_c = spread(pm * cap + total(earlier)).T
    table[0:1, :] = total(jnp.where(place_c == lane, sub, 0))
    table[8:9, :] = total(jnp.where(pm_c == lane // cap, 1, 0))

    lane_row = lax.broadcasted_iota(jnp.int32, (1, TILE), 1)
    alive = jnp.zeros((1, TILE), jnp.int32)
    for c in range(n_src):
        alive = jnp.where(lane_row // slots == c, counts_ref[0, c], alive)
    rows_r = spread(flat(rows_ref))
    goes = total(jnp.where(rows_r == sub, place_c, 0))
    goes = jnp.where(lane_row % slots < alive, goes, 4096)
    goes_r = spread(goes)
    goes_c = goes_r.T
    rank_c = spread(total(jnp.where(goes_c * TILE + sub < goes_r * TILE + lane, 1, 0))).T
    pick = rank_c == lane
    source = (lane_row // slots) * HALF + flat(cols_ref)
    source_c = spread(source).T
    table[1:2, :] = total(jnp.where(pick, sub, 0))
    table[2:3, :] = total(jnp.where(pick, source_c, 0))
    mine = total(jnp.where(pick, goes_c, 0))
    before = total(jnp.where(rank_c + 1 == lane, goes_c, 0))
    table[3:4, :] = jnp.where((mine == before) & (lane_row % HALF != 0), 1, 0)
    upto = total(jnp.where(goes_c <= lane, 1, 0))
    below = total(jnp.where(goes_c < lane, 1, 0))
    left_end = jnp.minimum(upto, HALF)
    right_from = jnp.maximum(below, HALF)
    table[4:5, :] = jnp.maximum(left_end - 1, 0)
    table[5:6, :] = jnp.where(below < left_end, 1, 0)
    table[6:7, :] = jnp.maximum(upto - 1 - HALF, 0)
    table[7:8, :] = jnp.where(right_from < upto, 1, 0)


def layer_kernel(
    cap, slots, n_y, n_m, n_q, swap,
    feat, vals_hbm, rows_ref, cols_ref, counts_ref, ws_hbm, wn_hbm, bias_ref, pm_ref,
    out_v,
    vals, own, mirror, blocks, mirrors, sums, more, f_in, f_out, f_recv, m_in, m_out, m_recv, pre,
    ws_ref, wn_ref, table_v, table,
    vals_sem, ws_sem, wn_sem, table_sem, mir_sem,
    swap_send, swap_recv, sib_send, sib_recv, y_send, y_recv, fwd_send, fwd_recv,
    msib_send, msib_recv, my_send, my_recv, mfwd_send, mfwd_recv,
    fs_sem, fr_sem, fms_sem, fmr_sem, ms_sem, mr_sem, mms_sem, mmr_sem,
):
    here = lax.axis_index("blk")
    me = lax.axis_index("bal")
    tiles, width, _ = own.shape
    wide = width + swap
    stay = width - swap
    n_bal = f_recv.shape[1] // width
    half = n_bal // 2
    base = me // half * half
    partner = (me + half) % n_bal
    sibling = here + 1 - 2 * (here % 2)
    across = (here + 2) % 4
    far = (sibling + 2) % 4
    y_tiles = tiles // n_y
    m_tiles = tiles // n_m
    q_tiles = cap // n_q
    own_rows = pl.ds(pl.multiple_of(me * width, width), width)
    mirror_rows = pl.ds(pl.multiple_of(partner * width + stay, 16), swap)

    def near(o):
        return base + (me + o) % half

    def other(o):
        return (base + half) % n_bal + (me + o) % half

    def each(first, last, body):
        def step(i, carry):
            body(i)
            return carry

        lax.fori_loop(first, last, step, 0)

    def remote(src, dst, send, recv, axis, peer):
        return pltpu.make_async_remote_copy(
            src, dst, send, recv, device_id={axis: peer}, device_id_type=MESH
        )

    load_vals = pltpu.make_async_copy(vals_hbm, vals, vals_sem)
    load_vals.start()
    load_ws = pltpu.make_async_copy(ws_hbm, ws_ref, ws_sem)
    load_ws.start()
    load_wn = pltpu.make_async_copy(wn_hbm, wn_ref, wn_sem)
    load_wn.start()

    barrier = pltpu.get_barrier_semaphore()
    for peer in (sibling, across):
        pl.semaphore_signal(barrier, inc=1, device_id={"blk": peer}, device_id_type=MESH)
    each(
        1, n_bal,
        lambda o: pl.semaphore_signal(
            barrier, inc=1, device_id={"bal": (me + o) % n_bal}, device_id_type=MESH
        ),
    )

    def pack(t):
        x = feat[:, pl.ds(pl.multiple_of(t * TILE, TILE), TILE)]
        own[t] = x
        blocks[here * tiles + t] = x

    each(0, tiles, pack)
    pl.semaphore_wait(barrier, n_bal + 1)

    def swap_copy(i):
        span = pl.ds(i * m_tiles, m_tiles)
        return remote(
            own.at[span, pl.ds(stay, swap)], mirror.at[span],
            swap_send.at[i], swap_recv.at[i], "bal", partner,
        )

    def y_copy(i, whose):
        return remote(
            own.at[pl.ds(i * y_tiles, y_tiles)],
            blocks.at[pl.ds(whose * tiles + i * y_tiles, y_tiles)],
            y_send.at[i], y_recv.at[i], "blk", across,
        )

    def fwd_copy(i, whose):
        span = pl.ds(whose * tiles + i * y_tiles, y_tiles)
        part = blocks.at[span]
        return remote(part, part, fwd_send.at[i], fwd_recv.at[i], "blk", sibling)

    def sib_copy(whose):
        return remote(
            own, blocks.at[pl.ds(whose * tiles, tiles)],
            sib_send, sib_recv, "blk", sibling,
        )

    def my_copy(i, whose):
        return remote(
            mirror.at[pl.ds(i * m_tiles, m_tiles)],
            mirrors.at[pl.ds(whose * tiles + i * m_tiles, m_tiles)],
            my_send.at[i], my_recv.at[i], "blk", across,
        )

    def msib_copy(i, whose):
        return remote(
            mirror.at[pl.ds(i * m_tiles, m_tiles)],
            mirrors.at[pl.ds(whose * tiles + i * m_tiles, m_tiles)],
            msib_send.at[i], msib_recv.at[i], "blk", sibling,
        )

    def mfwd_copy(i, whose):
        span = pl.ds(whose * tiles + i * m_tiles, m_tiles)
        part = mirrors.at[span]
        return remote(part, part, mfwd_send.at[i], mfwd_recv.at[i], "blk", sibling)

    def f_near(o, whose):
        rows = pl.ds(pl.multiple_of(whose * width, width), width)
        return remote(
            f_in.at[o, :, pl.ds(0, width)], f_recv.at[:, rows],
            fs_sem.at[o], fr_sem.at[whose], "bal", near(o),
        )

    def f_near_mirror(o, whose):
        rows = pl.ds(pl.multiple_of((whose + half) % n_bal * width + stay, 16), swap)
        return remote(
            f_in.at[o, :, pl.ds(width, swap)], f_recv.at[:, rows],
            fms_sem.at[o], fmr_sem.at[whose], "bal", near(o),
        )

    def f_other(o, whose):
        rows = pl.ds(pl.multiple_of(whose * width, width), stay)
        return remote(
            f_out.at[o], f_recv.at[:, rows],
            fs_sem.at[half + o], fr_sem.at[whose], "bal", other(o),
        )

    def m_near(q, o, whose):
        span = pl.ds(q * q_tiles, q_tiles)
        rows = pl.ds(pl.multiple_of(whose * width, width), width)
        return remote(
            m_in.at[o, span, pl.ds(0, width)], m_recv.at[span, rows],
            ms_sem.at[q, o], mr_sem.at[q, whose], "bal", near(o),
        )

    def m_near_mirror(q, o, whose):
        span = pl.ds(q * q_tiles, q_tiles)
        rows = pl.ds(pl.multiple_of((whose + half) % n_bal * width + stay, 16), swap)
        return remote(
            m_in.at[o, span, pl.ds(width, swap)], m_recv.at[span, rows],
            mms_sem.at[q, o], mmr_sem.at[q, whose], "bal", near(o),
        )

    def m_other(q, o, whose):
        span = pl.ds(q * q_tiles, q_tiles)
        rows = pl.ds(pl.multiple_of(whose * width, width), stay)
        return remote(
            m_out.at[o, span], m_recv.at[span, rows],
            ms_sem.at[q, half + o], mr_sem.at[q, whose], "bal", other(o),
        )

    each(0, n_m, lambda i: swap_copy(i).start())
    each(0, n_y, lambda i: y_copy(i, here).start())
    sib_copy(here).start()

    tables(pm_ref, rows_ref, cols_ref, counts_ref, table_v, slots, cap)
    load_table = pltpu.make_async_copy(table_v, table, table_sem)
    load_table.start()
    load_table.wait()

    def send_f_near(o):
        def gather(k):
            f_in[o, k, :width, :] = own[table[0, near(o) * cap + k]]

        each(0, cap, gather)
        f_near(o, me).start()

    def fill_f_other(o):
        def gather(k):
            f_out[o, k] = own[table[0, other(o) * cap + k]][:stay]

        each(0, cap, gather)

    def keep_f(k):
        f_recv[k, own_rows, :] = own[table[0, me * cap + k]]

    each(1, half, send_f_near)
    if stay:
        each(0, half, fill_f_other)
    each(0, cap, keep_f)
    load_vals.wait()

    def pass_on(i):
        y_copy(i, across).wait_recv()
        fwd_copy(i, across).start()

    def take_mirror(i):
        swap_copy(i).wait_recv()
        my_copy(i, here).start()
        msib_copy(i, here).start()

    each(0, n_y, pass_on)
    each(0, n_m, take_mirror)
    if stay:
        each(0, half, lambda o: f_other(o, me).start())
    keep_mirror = pltpu.make_async_copy(
        mirror, mirrors.at[pl.ds(here * tiles, tiles)], mir_sem
    )
    keep_mirror.start()

    def send_f_mirror(o):
        def gather(k):
            f_in[o, k, width:, :] = mirror[table[0, near(o) * cap + k]]

        each(0, cap, gather)
        f_near_mirror(o, me).start()

    def keep_f_mirror(k):
        f_recv[k, mirror_rows, :] = mirror[table[0, me * cap + k]]

    each(1, half, send_f_mirror)
    each(0, cap, keep_f_mirror)

    sib_copy(sibling).wait_recv()
    each(0, n_y, lambda i: fwd_copy(i, far).wait_recv())

    in_top = lax.broadcasted_iota(jnp.int32, (16, 2 * TILE), 0) < 8
    in_left = lax.broadcasted_iota(jnp.int32, (16, 2 * TILE), 1) < TILE
    ones = jnp.where(in_top == in_left, 1.0, 0.0).astype(jnp.bfloat16)
    deg_left = lax.broadcasted_iota(jnp.int32, (16, TILE), 0) < 8

    def products(j, held, count, extra):
        zeros = jnp.zeros((count, TILE), jnp.bfloat16)
        a = jnp.concatenate([vals[table[1, j]], vals[table[1, j + HALF]]], axis=1)
        x = jnp.concatenate([held[table[2, j]], zeros], axis=1)
        y = jnp.concatenate([zeros, held[table[2, j + HALF]]], axis=1)
        lhs = jnp.concatenate([x, y] + extra, axis=0)
        return lax.dot_general(
            lhs, a, (((1,), (1,)), ((), ())), preferred_element_type=jnp.float32
        )

    def absorb(j, carry):
        left, right, deg = carry
        prod = products(j, blocks, width, [ones])
        keep_left, keep_right = table[3, j], table[3, j + HALF]
        left = jnp.where(keep_left > 0, left, 0.0) + prod[:width]
        right = jnp.where(keep_right > 0, right, 0.0) + prod[width : 2 * width]
        deg = jnp.where(jnp.where(deg_left, keep_left, keep_right) > 0, deg, 0.0)
        deg = deg + prod[2 * width :]
        sums[j, :width, :] = left
        sums[j, width : 2 * width, :] = right
        sums[j, 2 * width :, :] = deg
        return left, right, deg

    def absorb_mirror(j, carry):
        left, right = carry
        prod = products(j, mirrors, swap, [])
        left = jnp.where(table[3, j] > 0, left, 0.0) + prod[:swap]
        right = jnp.where(table[3, j + HALF] > 0, right, 0.0) + prod[swap:]
        more[j, :swap, :] = left
        more[j, swap:, :] = right
        return left, right

    empty = jnp.zeros((width, TILE), jnp.float32)
    lax.fori_loop(
        0, HALF, absorb, (empty, empty, jnp.zeros((16, TILE), jnp.float32)), unroll=2
    )

    def inverse_degree(p):
        left, right = sums.at[table[4, p]], sums.at[table[6, p]]
        degree = (
            1.0
            + jnp.where(table[5, p] > 0, left[2 * width : 2 * width + 8, :], 0.0)
            + jnp.where(table[7, p] > 0, right[2 * width + 8 :, :], 0.0)
        )
        return (1.0 / degree)[:1]

    def mean_piece(p, inverse, where, count, right_row):
        left, right = where.at[table[4, p]], where.at[table[6, p]]
        agg = jnp.where(table[5, p] > 0, left[:count, :], 0.0) + jnp.where(
            table[7, p] > 0, right[right_row : right_row + count, :], 0.0
        )
        return (agg * inverse).astype(jnp.bfloat16)

    def send_m_other(q):
        def to_other(o):
            def fill(k):
                p = other(o) * cap + q * q_tiles + k
                m_out[o, q * q_tiles + k] = mean_piece(p, inverse_degree(p), sums, stay, width)

            each(0, q_tiles, fill)
            m_other(q, o, me).start()

        each(0, half, to_other)

    def pass_mirror_on(i):
        my_copy(i, across).wait_recv()
        mfwd_copy(i, across).start()

    if stay:
        each(0, n_q, send_m_other)
    each(0, n_m, pass_mirror_on)
    each(0, n_m, lambda i: msib_copy(i, sibling).wait_recv())
    each(0, n_m, lambda i: mfwd_copy(i, far).wait_recv())
    keep_mirror.wait()
    lax.fori_loop(0, HALF, absorb_mirror, (empty[:swap], empty[:swap]), unroll=2)

    def send_m(q):
        def to_near(o):
            def fill(k):
                p = near(o) * cap + q * q_tiles + k
                inverse = inverse_degree(p)
                at = q * q_tiles + k
                m_in[o, at, :width, :] = mean_piece(p, inverse, sums, width, width)
                m_in[o, at, width:, :] = mean_piece(p, inverse, more, swap, swap)

            each(0, q_tiles, fill)
            m_near(q, o, me).start()
            m_near_mirror(q, o, me).start()

        each(1, half, to_near)

    each(0, n_q, send_m)

    def keep_m(k):
        p = me * cap + k
        inverse = inverse_degree(p)
        m_recv[k, own_rows, :] = mean_piece(p, inverse, sums, width, width)
        m_recv[k, mirror_rows, :] = mean_piece(p, inverse, more, swap, swap)

    each(0, cap, keep_m)
    load_ws.wait()
    load_wn.wait()

    def wait_f_near(o):
        f_near(o, near(o)).wait_recv()
        f_near_mirror(o, near(o)).wait_recv()

    each(1, half, wait_f_near)
    if stay:
        each(0, half, lambda o: f_other(o, other(o)).wait_recv())

    rows = q_tiles * TILE

    def times(recv, q, weight):
        x = jnp.concatenate([recv[q * q_tiles + k] for k in range(q_tiles)], axis=1)
        return lax.dot_general(
            x, weight[...], (((0,), (0,)), ((), ())), preferred_element_type=jnp.float32
        )

    def chunk(q):
        return pl.ds(pl.multiple_of(q * rows, rows), rows)

    def self_part(q):
        pre[chunk(q), :] = times(f_recv, q, ws_ref) + bias_ref[...]

    each(0, n_q, self_part)
    live = table[8, me * cap]

    def finish(q):
        def wait_near(o):
            m_near(q, o, near(o)).wait_recv()
            m_near_mirror(q, o, near(o)).wait_recv()

        each(1, half, wait_near)
        if stay:
            each(0, half, lambda o: m_other(q, o, other(o)).wait_recv())
        hidden = jnp.maximum(pre[chunk(q), :] + times(m_recv, q, wn_ref), 0.0)
        row = q * rows + lax.broadcasted_iota(jnp.int32, (rows, 1), 0)
        out_v[0, 0, chunk(q), :] = jnp.where(row < live * TILE, hidden, 0.0).astype(jnp.bfloat16)

    each(0, n_q, finish)

    def settle_near(o):
        f_near(o, me).wait_send()
        f_near_mirror(o, me).wait_send()

        def one(q):
            m_near(q, o, me).wait_send()
            m_near_mirror(q, o, me).wait_send()

        each(0, n_q, one)

    def settle_other(o):
        f_other(o, me).wait_send()
        each(0, n_q, lambda q: m_other(q, o, me).wait_send())

    def settle_y(i):
        y_copy(i, here).wait_send()
        fwd_copy(i, across).wait_send()

    def settle_mirror(i):
        swap_copy(i).wait_send()
        my_copy(i, here).wait_send()
        msib_copy(i, here).wait_send()
        mfwd_copy(i, across).wait_send()

    each(1, half, settle_near)
    if stay:
        each(0, half, settle_other)
    each(0, n_y, settle_y)
    each(0, n_m, settle_mirror)
    sib_copy(here).wait_send()


def layer(
    features, tile_values, tile_rows, tile_cols, tile_counts, w_self, w_neigh, bias, part_map
):
    n_blk = lax.axis_size("blk")
    n_bal = lax.axis_size("bal")
    slots = tile_rows.shape[2]
    tiles = part_map.shape[1]
    cap = 2 * tiles // n_bal
    width = features.shape[1]
    total = w_self.shape[0]
    fits = (
        n_blk == 4 and n_blk * slots == TILE and tiles == HALF and width == HALF
        and n_bal * cap == TILE
    )
    if not fits:
        return on_device(
            features, tile_values, tile_rows, tile_cols, tile_counts, w_self, w_neigh, bias,
            part_map,
        )
    n_y, n_m, n_q = 4, 2, 4
    swap = width // 2
    wide, stay, half = width + swap, width - swap, n_bal // 2
    bf16, f32 = jnp.bfloat16, jnp.float32
    vmem = pl.BlockSpec(memory_space=pltpu.VMEM)
    smem = pl.BlockSpec(memory_space=pltpu.SMEM)
    hbm = pl.BlockSpec(memory_space=pl.ANY)
    dma = pltpu.SemaphoreType.DMA
    return pl.pallas_call(
        functools.partial(layer_kernel, cap, slots, n_y, n_m, n_q, swap),
        out_shape=pltpu.VMEM((1, 1, cap * TILE, total), bf16),
        in_specs=[vmem, hbm, vmem, vmem, smem, hbm, hbm, vmem, vmem],
        out_specs=vmem,
        scratch_shapes=[
            pltpu.VMEM((n_blk * slots, TILE, TILE), bf16),
            pltpu.VMEM((tiles, width, TILE), bf16),
            pltpu.VMEM((tiles, swap, TILE), bf16),
            pltpu.VMEM((n_blk * tiles, width, TILE), bf16),
            pltpu.VMEM((n_blk * tiles, swap, TILE), bf16),
            pltpu.VMEM((HALF, 2 * width + 16, TILE), f32),
            pltpu.VMEM((HALF, 2 * swap, TILE), f32),
            pltpu.VMEM((half, cap, wide, TILE), bf16),
            pltpu.VMEM((half, cap, max(stay, 16), TILE), bf16),
            pltpu.VMEM((cap, total, TILE), bf16),
            pltpu.VMEM((half, cap, wide, TILE), bf16),
            pltpu.VMEM((half, cap, max(stay, 16), TILE), bf16),
            pltpu.VMEM((cap, total, TILE), bf16),
            pltpu.VMEM((cap * TILE, total), f32),
            pltpu.VMEM((total, total), bf16),
            pltpu.VMEM((total, total), bf16),
            pltpu.VMEM((16, TILE), jnp.int32),
            pltpu.SMEM((16, TILE), jnp.int32),
            dma, dma, dma, dma, dma,
            dma((n_m,)), dma((n_m,)), dma, dma, dma((n_y,)), dma((n_y,)), dma((n_y,)), dma((n_y,)),
            dma((n_m,)), dma((n_m,)), dma((n_m,)), dma((n_m,)), dma((n_m,)), dma((n_m,)),
            dma((n_bal,)), dma((n_bal,)), dma((half,)), dma((n_bal,)),
            dma((n_q, n_bal)), dma((n_q, n_bal)), dma((n_q, half)), dma((n_q, n_bal)),
        ],
        compiler_params=pltpu.CompilerParams(
            collective_id=0, has_side_effects=True, vmem_limit_bytes=56 * 2**20
        ),
        cost_estimate=pl.CostEstimate(
            flops=4 * cap * TILE * total * total, bytes_accessed=12 * 2**20, transcendentals=0
        ),
    )(
        features.T,
        tile_values.reshape(n_blk * slots, TILE, TILE),
        tile_rows[0],
        tile_cols[0],
        tile_counts,
        w_self,
        w_neigh,
        bias.reshape(1, total),
        part_map,
    )


def solution(mesh):
    placed = (
        P("blk", "bal"),
        P("blk", None, None, None, None),
        P("blk", None, None),
        P("blk", None, None),
        P("blk", None),
        P(),
        P(),
        P(),
        P("blk", None),
    )
    return jax.shard_map(
        layer,
        mesh=mesh,
        in_specs=placed,
        out_specs=P("blk", "bal", None, None),
        check_vma=False,
    )
```

```python
import functools
import jax
import jax.numpy as jnp
from jax import lax
from jax.experimental import pallas as pl
from jax.experimental.pallas import tpu as pltpu
from jax.sharding import PartitionSpec as P

TILE = 128
HALF = 64
MESH = pl.DeviceIdType.MESH


def from_behind(block, axis, distance):
    devices = range(lax.axis_size(axis))
    route = [((i - distance) % len(devices), i) for i in devices]
    return lax.ppermute(block, axis, route)


def advance(block, steps_by):
    return from_behind(block, "blk", steps_by)


def on_device(
    features, tile_values, tile_rows, tile_cols, tile_counts, w_self, w_neigh, bias, part_map
):
    n_blk = lax.axis_size("blk")
    n_bal = lax.axis_size("bal")
    here = lax.axis_index("blk")
    column = lax.axis_index("bal")
    width = features.shape[1]
    tiles_per = part_map.shape[1]
    values = tile_values[0]
    rows_idx = tile_rows[0]
    cols_idx = tile_cols[0]
    counts = tile_counts[0]
    slots = values.shape[1]
    live = jnp.arange(slots)[None, :] < counts[:, None]
    row_hot = (
        (rows_idx[:, :, None] == jnp.arange(tiles_per)[None, None, :]) & live[:, :, None]
    ).astype(jnp.float32)
    row_mass = jnp.einsum(
        "csij,j->csi", values, jnp.ones((TILE,), jnp.bfloat16), preferred_element_type=jnp.float32
    )
    degree = 1.0 + jnp.einsum("cst,csi->ti", row_hot, row_mass, precision=lax.Precision.HIGHEST)

    def absorb(total, block, source):
        tiles = block.reshape(tiles_per, TILE, width)
        vals = lax.dynamic_index_in_dim(values, source, 0, keepdims=False)
        picks = lax.dynamic_index_in_dim(cols_idx, source, 0, keepdims=False)
        targets = lax.dynamic_index_in_dim(rows_idx, source, 0, keepdims=False)
        alive = lax.dynamic_index_in_dim(live, source, 0, keepdims=False)
        gathered = jnp.take(tiles, picks, axis=0)
        prod = jnp.einsum("sij,sjf->sif", vals, gathered, preferred_element_type=jnp.float32)
        masked = jnp.where(alive[:, None, None], prod, 0.0)
        return total.at[targets].add(masked)

    empty = jnp.zeros((tiles_per, TILE, width), jnp.float32)

    def step_one(index, carry):
        total, block = carry
        total = absorb(total, block, (here - index) % n_blk)
        block = advance(block, 1)
        return (total, block)

    total, block = lax.fori_loop(0, n_blk - 1, step_one, (empty, features))
    total = absorb(total, block, (here - (n_blk - 1)) % n_blk)
    mean_agg = (total / degree[:, :, None]).astype(jnp.bfloat16).reshape(tiles_per * TILE, width)
    capacity = 2 * tiles_per // n_bal
    mapping = part_map[0]
    dest_hot = (mapping[:, None] == jnp.arange(n_bal)[None, :]).astype(jnp.int32)
    ranks = jnp.cumsum(dest_hot, axis=0) - dest_hot
    place = mapping * capacity + jnp.sum(ranks * dest_hot, axis=1)
    select = (jnp.arange(n_bal * capacity)[:, None] == place[None, :]).astype(jnp.bfloat16)
    col_start = column * width
    zeros_out = jnp.zeros((tiles_per * TILE, width), jnp.float32)
    carry = zeros_out
    mean_piece = lax.all_gather(mean_agg, "bal", axis=1, tiled=True)
    feat_piece = lax.all_gather(features, "bal", axis=1, tiled=True)
    count = mean_piece.shape[1]
    neigh_part = lax.dynamic_slice(w_neigh, (0, col_start), (count, width))
    self_part = lax.dynamic_slice(w_self, (0, col_start), (count, width))
    carry = jnp.dot(mean_piece, neigh_part, preferred_element_type=jnp.float32)
    pre = carry + jnp.dot(feat_piece, self_part, preferred_element_type=jnp.float32)
    pre = pre + lax.dynamic_slice_in_dim(bias, col_start, width)
    hidden = jnp.maximum(pre, 0.0).astype(jnp.bfloat16)
    tiles = hidden.reshape(tiles_per, TILE, width)
    placed = jnp.einsum("kt,tif->kif", select, tiles, preferred_element_type=jnp.float32)
    result = lax.all_to_all(
        placed.astype(jnp.bfloat16).reshape(n_bal, capacity * TILE, width),
        "bal",
        split_axis=0,
        concat_axis=2,
        tiled=True,
    )
    return result[None]


def tables(pm_ref, rows_ref, cols_ref, counts_ref, table, slots, cap):
    n_src = rows_ref.shape[0]
    table[...] = jnp.zeros(table.shape, jnp.int32)
    square = (TILE, TILE)
    lane = lax.broadcasted_iota(jnp.int32, square, 1)
    sub = lax.broadcasted_iota(jnp.int32, square, 0)

    def spread(row):
        return jnp.broadcast_to(row, square)

    def total(x):
        return jnp.sum(x, axis=0, keepdims=True)

    def flat(ref):
        return jnp.concatenate([ref[c : c + 1, :] for c in range(n_src)], axis=1)

    pm = pm_ref[...]
    pm = jnp.concatenate([pm, jnp.full((1, TILE - pm.shape[1]), 999, jnp.int32)], axis=1)
    pm_r = spread(pm)
    pm_c = pm_r.T
    earlier = jnp.where((pm_c == pm_r) & (sub < lane), 1, 0)
    place_c = spread(pm * cap + total(earlier)).T
    table[0:1, :] = total(jnp.where(place_c == lane, sub, 0))
    table[8:9, :] = total(jnp.where(pm_c == lane // cap, 1, 0))

    lane_row = lax.broadcasted_iota(jnp.int32, (1, TILE), 1)
    alive = jnp.zeros((1, TILE), jnp.int32)
    for c in range(n_src):
        alive = jnp.where(lane_row // slots == c, counts_ref[0, c], alive)
    rows_r = spread(flat(rows_ref))
    goes = total(jnp.where(rows_r == sub, place_c, 0))
    goes = jnp.where(lane_row % slots < alive, goes, 4096)
    goes_r = spread(goes)
    goes_c = goes_r.T
    rank_c = spread(total(jnp.where(goes_c * TILE + sub < goes_r * TILE + lane, 1, 0))).T
    pick = rank_c == lane
    source = (lane_row // slots) * HALF + flat(cols_ref)
    source_c = spread(source).T
    table[1:2, :] = total(jnp.where(pick, sub, 0))
    table[2:3, :] = total(jnp.where(pick, source_c, 0))
    mine = total(jnp.where(pick, goes_c, 0))
    before = total(jnp.where(rank_c + 1 == lane, goes_c, 0))
    table[3:4, :] = jnp.where((mine == before) & (lane_row % HALF != 0), 1, 0)
    upto = total(jnp.where(goes_c <= lane, 1, 0))
    below = total(jnp.where(goes_c < lane, 1, 0))
    left_end = jnp.minimum(upto, HALF)
    right_from = jnp.maximum(below, HALF)
    table[4:5, :] = jnp.maximum(left_end - 1, 0)
    table[5:6, :] = jnp.where(below < left_end, 1, 0)
    table[6:7, :] = jnp.maximum(upto - 1 - HALF, 0)
    table[7:8, :] = jnp.where(right_from < upto, 1, 0)


def layer_kernel(
    cap, slots, n_y, n_m, n_q, swap,
    feat, vals_hbm, rows_ref, cols_ref, counts_ref, ws_hbm, wn_hbm, bias_ref, pm_ref,
    out_v,
    vals, own, mirror, blocks, mirrors, sums, more, f_in, f_out, f_recv, m_in, m_out, m_recv, pre,
    ws_ref, wn_ref, table_v, table,
    vals_sem, ws_sem, wn_sem, table_sem, mir_sem,
    swap_send, swap_recv, sib_send, sib_recv, y_send, y_recv, fwd_send, fwd_recv,
    msib_send, msib_recv, my_send, my_recv, mfwd_send, mfwd_recv,
    fs_sem, fr_sem, fms_sem, fmr_sem, ms_sem, mr_sem, mms_sem, mmr_sem,
):
    here = lax.axis_index("blk")
    me = lax.axis_index("bal")
    tiles, width, _ = own.shape
    wide = width + swap
    stay = width - swap
    n_bal = f_recv.shape[1] // width
    half = n_bal // 2
    base = me // half * half
    partner = (me + half) % n_bal
    sibling = here + 1 - 2 * (here % 2)
    across = (here + 2) % 4
    far = (sibling + 2) % 4
    y_tiles = tiles // n_y
    m_tiles = tiles // n_m
    q_tiles = cap // n_q
    own_rows = pl.ds(pl.multiple_of(me * width, width), width)
    mirror_rows = pl.ds(pl.multiple_of(partner * width + stay, 16), swap)

    def near(o):
        return base + (me + o) % half

    def other(o):
        return (base + half) % n_bal + (me + o) % half

    def each(first, last, body):
        def step(i, carry):
            body(i)
            return carry

        lax.fori_loop(first, last, step, 0)

    def remote(src, dst, send, recv, axis, peer):
        return pltpu.make_async_remote_copy(
            src, dst, send, recv, device_id={axis: peer}, device_id_type=MESH
        )

    load_vals = pltpu.make_async_copy(vals_hbm, vals, vals_sem)
    load_vals.start()
    load_ws = pltpu.make_async_copy(ws_hbm, ws_ref, ws_sem)
    load_ws.start()
    load_wn = pltpu.make_async_copy(wn_hbm, wn_ref, wn_sem)
    load_wn.start()

    barrier = pltpu.get_barrier_semaphore()
    for peer in (sibling, across):
        pl.semaphore_signal(barrier, inc=1, device_id={"blk": peer}, device_id_type=MESH)
    each(
        1, n_bal,
        lambda o: pl.semaphore_signal(
            barrier, inc=1, device_id={"bal": (me + o) % n_bal}, device_id_type=MESH
        ),
    )

    def pack(t):
        x = feat[:, pl.ds(pl.multiple_of(t * TILE, TILE), TILE)]
        own[t] = x
        blocks[here * tiles + t] = x

    each(0, tiles, pack)
    pl.semaphore_wait(barrier, n_bal + 1)

    def swap_copy(i):
        span = pl.ds(i * m_tiles, m_tiles)
        return remote(
            own.at[span, pl.ds(stay, swap)], mirror.at[span],
            swap_send.at[i], swap_recv.at[i], "bal", partner,
        )

    def y_copy(i, whose):
        return remote(
            own.at[pl.ds(i * y_tiles, y_tiles)],
            blocks.at[pl.ds(whose * tiles + i * y_tiles, y_tiles)],
            y_send.at[i], y_recv.at[i], "blk", across,
        )

    def fwd_copy(i, whose):
        span = pl.ds(whose * tiles + i * y_tiles, y_tiles)
        part = blocks.at[span]
        return remote(part, part, fwd_send.at[i], fwd_recv.at[i], "blk", sibling)

    def sib_copy(whose):
        return remote(
            own, blocks.at[pl.ds(whose * tiles, tiles)],
            sib_send, sib_recv, "blk", sibling,
        )

    def my_copy(i, whose):
        return remote(
            mirror.at[pl.ds(i * m_tiles, m_tiles)],
            mirrors.at[pl.ds(whose * tiles + i * m_tiles, m_tiles)],
            my_send.at[i], my_recv.at[i], "blk", across,
        )

    def msib_copy(i, whose):
        return remote(
            mirror.at[pl.ds(i * m_tiles, m_tiles)],
            mirrors.at[pl.ds(whose * tiles + i * m_tiles, m_tiles)],
            msib_send.at[i], msib_recv.at[i], "blk", sibling,
        )

    def mfwd_copy(i, whose):
        span = pl.ds(whose * tiles + i * m_tiles, m_tiles)
        part = mirrors.at[span]
        return remote(part, part, mfwd_send.at[i], mfwd_recv.at[i], "blk", sibling)

    def f_near(o, whose):
        rows = pl.ds(pl.multiple_of(whose * width, width), width)
        return remote(
            f_in.at[o, :, pl.ds(0, width)], f_recv.at[:, rows],
            fs_sem.at[o], fr_sem.at[whose], "bal", near(o),
        )

    def f_near_mirror(o, whose):
        rows = pl.ds(pl.multiple_of((whose + half) % n_bal * width + stay, 16), swap)
        return remote(
            f_in.at[o, :, pl.ds(width, swap)], f_recv.at[:, rows],
            fms_sem.at[o], fmr_sem.at[whose], "bal", near(o),
        )

    def f_other(o, whose):
        rows = pl.ds(pl.multiple_of(whose * width, width), stay)
        return remote(
            f_out.at[o], f_recv.at[:, rows],
            fs_sem.at[half + o], fr_sem.at[whose], "bal", other(o),
        )

    def m_near(q, o, whose):
        span = pl.ds(q * q_tiles, q_tiles)
        rows = pl.ds(pl.multiple_of(whose * width, width), width)
        return remote(
            m_in.at[o, span, pl.ds(0, width)], m_recv.at[span, rows],
            ms_sem.at[q, o], mr_sem.at[q, whose], "bal", near(o),
        )

    def m_near_mirror(q, o, whose):
        span = pl.ds(q * q_tiles, q_tiles)
        rows = pl.ds(pl.multiple_of((whose + half) % n_bal * width + stay, 16), swap)
        return remote(
            m_in.at[o, span, pl.ds(width, swap)], m_recv.at[span, rows],
            mms_sem.at[q, o], mmr_sem.at[q, whose], "bal", near(o),
        )

    def m_other(q, o, whose):
        span = pl.ds(q * q_tiles, q_tiles)
        rows = pl.ds(pl.multiple_of(whose * width, width), stay)
        return remote(
            m_out.at[o, span], m_recv.at[span, rows],
            ms_sem.at[q, half + o], mr_sem.at[q, whose], "bal", other(o),
        )

    each(0, n_m, lambda i: swap_copy(i).start())
    each(0, n_y, lambda i: y_copy(i, here).start())
    sib_copy(here).start()

    tables(pm_ref, rows_ref, cols_ref, counts_ref, table_v, slots, cap)
    load_table = pltpu.make_async_copy(table_v, table, table_sem)
    load_table.start()
    load_table.wait()

    def send_f_near(o):
        def gather(k):
            f_in[o, k, :width, :] = own[table[0, near(o) * cap + k]]

        each(0, cap, gather)
        f_near(o, me).start()

    def fill_f_other(o):
        def gather(k):
            f_out[o, k] = own[table[0, other(o) * cap + k]][:stay]

        each(0, cap, gather)

    def keep_f(k):
        f_recv[k, own_rows, :] = own[table[0, me * cap + k]]

    each(1, half, send_f_near)
    if stay:
        each(0, half, fill_f_other)
    each(0, cap, keep_f)
    load_vals.wait()

    def pass_on(i):
        y_copy(i, across).wait_recv()
        fwd_copy(i, across).start()

    def take_mirror(i):
        swap_copy(i).wait_recv()
        my_copy(i, here).start()
        msib_copy(i, here).start()

    each(0, n_y, pass_on)
    each(0, n_m - 1, take_mirror)
    if stay:
        each(0, half, lambda o: f_other(o, me).start())
    each(n_m - 1, n_m, take_mirror)
    keep_mirror = pltpu.make_async_copy(
        mirror, mirrors.at[pl.ds(here * tiles, tiles)], mir_sem
    )
    keep_mirror.start()

    def send_f_mirror(o):
        def gather(k):
            f_in[o, k, width:, :] = mirror[table[0, near(o) * cap + k]]

        each(0, cap, gather)
        f_near_mirror(o, me).start()

    def keep_f_mirror(k):
        f_recv[k, mirror_rows, :] = mirror[table[0, me * cap + k]]

    each(1, half, send_f_mirror)
    each(0, cap, keep_f_mirror)

    sib_copy(sibling).wait_recv()
    each(0, n_y, lambda i: fwd_copy(i, far).wait_recv())

    in_top = lax.broadcasted_iota(jnp.int32, (16, 2 * TILE), 0) < 8
    in_left = lax.broadcasted_iota(jnp.int32, (16, 2 * TILE), 1) < TILE
    ones = jnp.where(in_top == in_left, 1.0, 0.0).astype(jnp.bfloat16)
    deg_left = lax.broadcasted_iota(jnp.int32, (16, TILE), 0) < 8

    def products(j, held, count, extra):
        zeros = jnp.zeros((count, TILE), jnp.bfloat16)
        a = jnp.concatenate([vals[table[1, j]], vals[table[1, j + HALF]]], axis=1)
        x = jnp.concatenate([held[table[2, j]], zeros], axis=1)
        y = jnp.concatenate([zeros, held[table[2, j + HALF]]], axis=1)
        lhs = jnp.concatenate([x, y] + extra, axis=0)
        return lax.dot_general(
            lhs, a, (((1,), (1,)), ((), ())), preferred_element_type=jnp.float32
        )

    def absorb(j, carry):
        left, right, deg = carry
        prod = products(j, blocks, width, [ones])
        keep_left, keep_right = table[3, j], table[3, j + HALF]
        left = jnp.where(keep_left > 0, left, 0.0) + prod[:width]
        right = jnp.where(keep_right > 0, right, 0.0) + prod[width : 2 * width]
        deg = jnp.where(jnp.where(deg_left, keep_left, keep_right) > 0, deg, 0.0)
        deg = deg + prod[2 * width :]
        sums[j, :width, :] = left
        sums[j, width : 2 * width, :] = right
        sums[j, 2 * width :, :] = deg
        return left, right, deg

    def absorb_mirror(j, carry):
        left, right = carry
        prod = products(j, mirrors, swap, [])
        left = jnp.where(table[3, j] > 0, left, 0.0) + prod[:swap]
        right = jnp.where(table[3, j + HALF] > 0, right, 0.0) + prod[swap:]
        more[j, :swap, :] = left
        more[j, swap:, :] = right
        return left, right

    empty = jnp.zeros((width, TILE), jnp.float32)
    lax.fori_loop(
        0, HALF, absorb, (empty, empty, jnp.zeros((16, TILE), jnp.float32)), unroll=2
    )

    def inverse_degree(p):
        left, right = sums.at[table[4, p]], sums.at[table[6, p]]
        degree = (
            1.0
            + jnp.where(table[5, p] > 0, left[2 * width : 2 * width + 8, :], 0.0)
            + jnp.where(table[7, p] > 0, right[2 * width + 8 :, :], 0.0)
        )
        return (1.0 / degree)[:1]

    def mean_piece(p, inverse, where, count, right_row):
        left, right = where.at[table[4, p]], where.at[table[6, p]]
        agg = jnp.where(table[5, p] > 0, left[:count, :], 0.0) + jnp.where(
            table[7, p] > 0, right[right_row : right_row + count, :], 0.0
        )
        return (agg * inverse).astype(jnp.bfloat16)

    def send_m_other(q):
        def to_other(o):
            def fill(k):
                p = other(o) * cap + q * q_tiles + k
                m_out[o, q * q_tiles + k] = mean_piece(p, inverse_degree(p), sums, stay, width)

            each(0, q_tiles, fill)
            m_other(q, o, me).start()

        each(0, half, to_other)

    def send_m_near(q):
        def to_near(o):
            def fill(k):
                p = near(o) * cap + q * q_tiles + k
                m_in[o, q * q_tiles + k, :width, :] = mean_piece(
                    p, inverse_degree(p), sums, width, width
                )

            each(0, q_tiles, fill)
            m_near(q, o, me).start()

        each(1, half, to_near)

    def pass_mirror_on(i):
        my_copy(i, across).wait_recv()
        mfwd_copy(i, across).start()

    if stay:
        each(0, n_q, send_m_other)
    each(0, n_m, pass_mirror_on)
    each(0, n_q, send_m_near)
    each(0, n_m, lambda i: msib_copy(i, sibling).wait_recv())
    each(0, n_m, lambda i: mfwd_copy(i, far).wait_recv())
    keep_mirror.wait()
    lax.fori_loop(0, HALF, absorb_mirror, (empty[:swap], empty[:swap]), unroll=2)

    def send_m_mirror(q):
        def to_near(o):
            def fill(k):
                p = near(o) * cap + q * q_tiles + k
                m_in[o, q * q_tiles + k, width:, :] = mean_piece(
                    p, inverse_degree(p), more, swap, swap
                )

            each(0, q_tiles, fill)
            m_near_mirror(q, o, me).start()

        each(1, half, to_near)

    each(0, n_q, send_m_mirror)

    def keep_m(k):
        p = me * cap + k
        inverse = inverse_degree(p)
        m_recv[k, own_rows, :] = mean_piece(p, inverse, sums, width, width)
        m_recv[k, mirror_rows, :] = mean_piece(p, inverse, more, swap, swap)

    each(0, cap, keep_m)
    load_ws.wait()
    load_wn.wait()

    def wait_f_near(o):
        f_near(o, near(o)).wait_recv()
        f_near_mirror(o, near(o)).wait_recv()

    each(1, half, wait_f_near)
    if stay:
        each(0, half, lambda o: f_other(o, other(o)).wait_recv())

    rows = q_tiles * TILE

    def times(recv, q, weight):
        x = jnp.concatenate([recv[q * q_tiles + k] for k in range(q_tiles)], axis=1)
        return lax.dot_general(
            x, weight[...], (((0,), (0,)), ((), ())), preferred_element_type=jnp.float32
        )

    def chunk(q):
        return pl.ds(pl.multiple_of(q * rows, rows), rows)

    def self_part(q):
        pre[chunk(q), :] = times(f_recv, q, ws_ref) + bias_ref[...]

    each(0, n_q, self_part)
    live = table[8, me * cap]

    def finish(q):
        def wait_near(o):
            m_near(q, o, near(o)).wait_recv()
            m_near_mirror(q, o, near(o)).wait_recv()

        each(1, half, wait_near)
        if stay:
            each(0, half, lambda o: m_other(q, o, other(o)).wait_recv())
        hidden = jnp.maximum(pre[chunk(q), :] + times(m_recv, q, wn_ref), 0.0)
        row = q * rows + lax.broadcasted_iota(jnp.int32, (rows, 1), 0)
        out_v[0, 0, chunk(q), :] = jnp.where(row < live * TILE, hidden, 0.0).astype(jnp.bfloat16)

    each(0, n_q, finish)

    def settle_near(o):
        f_near(o, me).wait_send()
        f_near_mirror(o, me).wait_send()

        def one(q):
            m_near(q, o, me).wait_send()
            m_near_mirror(q, o, me).wait_send()

        each(0, n_q, one)

    def settle_other(o):
        f_other(o, me).wait_send()
        each(0, n_q, lambda q: m_other(q, o, me).wait_send())

    def settle_y(i):
        y_copy(i, here).wait_send()
        fwd_copy(i, across).wait_send()

    def settle_mirror(i):
        swap_copy(i).wait_send()
        my_copy(i, here).wait_send()
        msib_copy(i, here).wait_send()
        mfwd_copy(i, across).wait_send()

    each(1, half, settle_near)
    if stay:
        each(0, half, settle_other)
    each(0, n_y, settle_y)
    each(0, n_m, settle_mirror)
    sib_copy(here).wait_send()


def layer(
    features, tile_values, tile_rows, tile_cols, tile_counts, w_self, w_neigh, bias, part_map
):
    n_blk = lax.axis_size("blk")
    n_bal = lax.axis_size("bal")
    slots = tile_rows.shape[2]
    tiles = part_map.shape[1]
    cap = 2 * tiles // n_bal
    width = features.shape[1]
    total = w_self.shape[0]
    fits = (
        n_blk == 4 and n_blk * slots == TILE and tiles == HALF and width == HALF
        and n_bal * cap == TILE
    )
    if not fits:
        return on_device(
            features, tile_values, tile_rows, tile_cols, tile_counts, w_self, w_neigh, bias,
            part_map,
        )
    n_y, n_m, n_q = 4, 4, 4
    swap = width // 2
    wide, stay, half = width + swap, width - swap, n_bal // 2
    bf16, f32 = jnp.bfloat16, jnp.float32
    vmem = pl.BlockSpec(memory_space=pltpu.VMEM)
    smem = pl.BlockSpec(memory_space=pltpu.SMEM)
    hbm = pl.BlockSpec(memory_space=pl.ANY)
    dma = pltpu.SemaphoreType.DMA
    return pl.pallas_call(
        functools.partial(layer_kernel, cap, slots, n_y, n_m, n_q, swap),
        out_shape=pltpu.VMEM((1, 1, cap * TILE, total), bf16),
        in_specs=[vmem, hbm, vmem, vmem, smem, hbm, hbm, vmem, vmem],
        out_specs=vmem,
        scratch_shapes=[
            pltpu.VMEM((n_blk * slots, TILE, TILE), bf16),
            pltpu.VMEM((tiles, width, TILE), bf16),
            pltpu.VMEM((tiles, swap, TILE), bf16),
            pltpu.VMEM((n_blk * tiles, width, TILE), bf16),
            pltpu.VMEM((n_blk * tiles, swap, TILE), bf16),
            pltpu.VMEM((HALF, 2 * width + 16, TILE), f32),
            pltpu.VMEM((HALF, 2 * swap, TILE), f32),
            pltpu.VMEM((half, cap, wide, TILE), bf16),
            pltpu.VMEM((half, cap, max(stay, 16), TILE), bf16),
            pltpu.VMEM((cap, total, TILE), bf16),
            pltpu.VMEM((half, cap, wide, TILE), bf16),
            pltpu.VMEM((half, cap, max(stay, 16), TILE), bf16),
            pltpu.VMEM((cap, total, TILE), bf16),
            pltpu.VMEM((cap * TILE, total), f32),
            pltpu.VMEM((total, total), bf16),
            pltpu.VMEM((total, total), bf16),
            pltpu.VMEM((16, TILE), jnp.int32),
            pltpu.SMEM((16, TILE), jnp.int32),
            dma, dma, dma, dma, dma,
            dma((n_m,)), dma((n_m,)), dma, dma, dma((n_y,)), dma((n_y,)), dma((n_y,)), dma((n_y,)),
            dma((n_m,)), dma((n_m,)), dma((n_m,)), dma((n_m,)), dma((n_m,)), dma((n_m,)),
            dma((n_bal,)), dma((n_bal,)), dma((half,)), dma((n_bal,)),
            dma((n_q, n_bal)), dma((n_q, n_bal)), dma((n_q, half)), dma((n_q, n_bal)),
        ],
        compiler_params=pltpu.CompilerParams(
            collective_id=0, has_side_effects=True, vmem_limit_bytes=56 * 2**20
        ),
        cost_estimate=pl.CostEstimate(
            flops=4 * cap * TILE * total * total, bytes_accessed=12 * 2**20, transcendentals=0
        ),
    )(
        features.T,
        tile_values.reshape(n_blk * slots, TILE, TILE),
        tile_rows[0],
        tile_cols[0],
        tile_counts,
        w_self,
        w_neigh,
        bias.reshape(1, total),
        part_map,
    )


def solution(mesh):
    placed = (
        P("blk", "bal"),
        P("blk", None, None, None, None),
        P("blk", None, None),
        P("blk", None, None),
        P("blk", None),
        P(),
        P(),
        P(),
        P("blk", None),
    )
    return jax.shard_map(
        layer,
        mesh=mesh,
        in_specs=placed,
        out_specs=P("blk", "bal", None, None),
        check_vma=False,
    )
```

```python
import functools
import jax
import jax.numpy as jnp
from jax import lax
from jax.experimental import pallas as pl
from jax.experimental.pallas import tpu as pltpu
from jax.sharding import PartitionSpec as P

TILE = 128
HALF = 64
MESH = pl.DeviceIdType.MESH


def from_behind(block, axis, distance):
    devices = range(lax.axis_size(axis))
    route = [((i - distance) % len(devices), i) for i in devices]
    return lax.ppermute(block, axis, route)


def advance(block, steps_by):
    return from_behind(block, "blk", steps_by)


def on_device(
    features, tile_values, tile_rows, tile_cols, tile_counts, w_self, w_neigh, bias, part_map
):
    n_blk = lax.axis_size("blk")
    n_bal = lax.axis_size("bal")
    here = lax.axis_index("blk")
    column = lax.axis_index("bal")
    width = features.shape[1]
    tiles_per = part_map.shape[1]
    values = tile_values[0]
    rows_idx = tile_rows[0]
    cols_idx = tile_cols[0]
    counts = tile_counts[0]
    slots = values.shape[1]
    live = jnp.arange(slots)[None, :] < counts[:, None]
    row_hot = (
        (rows_idx[:, :, None] == jnp.arange(tiles_per)[None, None, :]) & live[:, :, None]
    ).astype(jnp.float32)
    row_mass = jnp.einsum(
        "csij,j->csi", values, jnp.ones((TILE,), jnp.bfloat16), preferred_element_type=jnp.float32
    )
    degree = 1.0 + jnp.einsum("cst,csi->ti", row_hot, row_mass, precision=lax.Precision.HIGHEST)

    def absorb(total, block, source):
        tiles = block.reshape(tiles_per, TILE, width)
        vals = lax.dynamic_index_in_dim(values, source, 0, keepdims=False)
        picks = lax.dynamic_index_in_dim(cols_idx, source, 0, keepdims=False)
        targets = lax.dynamic_index_in_dim(rows_idx, source, 0, keepdims=False)
        alive = lax.dynamic_index_in_dim(live, source, 0, keepdims=False)
        gathered = jnp.take(tiles, picks, axis=0)
        prod = jnp.einsum("sij,sjf->sif", vals, gathered, preferred_element_type=jnp.float32)
        masked = jnp.where(alive[:, None, None], prod, 0.0)
        return total.at[targets].add(masked)

    empty = jnp.zeros((tiles_per, TILE, width), jnp.float32)

    def step_one(index, carry):
        total, block = carry
        total = absorb(total, block, (here - index) % n_blk)
        block = advance(block, 1)
        return (total, block)

    total, block = lax.fori_loop(0, n_blk - 1, step_one, (empty, features))
    total = absorb(total, block, (here - (n_blk - 1)) % n_blk)
    mean_agg = (total / degree[:, :, None]).astype(jnp.bfloat16).reshape(tiles_per * TILE, width)
    capacity = 2 * tiles_per // n_bal
    mapping = part_map[0]
    dest_hot = (mapping[:, None] == jnp.arange(n_bal)[None, :]).astype(jnp.int32)
    ranks = jnp.cumsum(dest_hot, axis=0) - dest_hot
    place = mapping * capacity + jnp.sum(ranks * dest_hot, axis=1)
    select = (jnp.arange(n_bal * capacity)[:, None] == place[None, :]).astype(jnp.bfloat16)
    col_start = column * width
    zeros_out = jnp.zeros((tiles_per * TILE, width), jnp.float32)
    carry = zeros_out
    mean_piece = lax.all_gather(mean_agg, "bal", axis=1, tiled=True)
    feat_piece = lax.all_gather(features, "bal", axis=1, tiled=True)
    count = mean_piece.shape[1]
    neigh_part = lax.dynamic_slice(w_neigh, (0, col_start), (count, width))
    self_part = lax.dynamic_slice(w_self, (0, col_start), (count, width))
    carry = jnp.dot(mean_piece, neigh_part, preferred_element_type=jnp.float32)
    pre = carry + jnp.dot(feat_piece, self_part, preferred_element_type=jnp.float32)
    pre = pre + lax.dynamic_slice_in_dim(bias, col_start, width)
    hidden = jnp.maximum(pre, 0.0).astype(jnp.bfloat16)
    tiles = hidden.reshape(tiles_per, TILE, width)
    placed = jnp.einsum("kt,tif->kif", select, tiles, preferred_element_type=jnp.float32)
    result = lax.all_to_all(
        placed.astype(jnp.bfloat16).reshape(n_bal, capacity * TILE, width),
        "bal",
        split_axis=0,
        concat_axis=2,
        tiled=True,
    )
    return result[None]


def tables(pm_ref, rows_ref, cols_ref, counts_ref, table, slots, cap):
    n_src = rows_ref.shape[0]
    table[...] = jnp.zeros(table.shape, jnp.int32)
    square = (TILE, TILE)
    lane = lax.broadcasted_iota(jnp.int32, square, 1)
    sub = lax.broadcasted_iota(jnp.int32, square, 0)

    def spread(row):
        return jnp.broadcast_to(row, square)

    def total(x):
        return jnp.sum(x, axis=0, keepdims=True)

    def flat(ref):
        return jnp.concatenate([ref[c : c + 1, :] for c in range(n_src)], axis=1)

    pm = pm_ref[...]
    pm = jnp.concatenate([pm, jnp.full((1, TILE - pm.shape[1]), 999, jnp.int32)], axis=1)
    pm_r = spread(pm)
    pm_c = pm_r.T
    earlier = jnp.where((pm_c == pm_r) & (sub < lane), 1, 0)
    place_c = spread(pm * cap + total(earlier)).T
    table[0:1, :] = total(jnp.where(place_c == lane, sub, 0))
    table[8:9, :] = total(jnp.where(pm_c == lane // cap, 1, 0))

    lane_row = lax.broadcasted_iota(jnp.int32, (1, TILE), 1)
    alive = jnp.zeros((1, TILE), jnp.int32)
    for c in range(n_src):
        alive = jnp.where(lane_row // slots == c, counts_ref[0, c], alive)
    rows_r = spread(flat(rows_ref))
    goes = total(jnp.where(rows_r == sub, place_c, 0))
    goes = jnp.where(lane_row % slots < alive, goes, 4096)
    goes_r = spread(goes)
    goes_c = goes_r.T
    rank_c = spread(total(jnp.where(goes_c * TILE + sub < goes_r * TILE + lane, 1, 0))).T
    pick = rank_c == lane
    source = (lane_row // slots) * HALF + flat(cols_ref)
    source_c = spread(source).T
    table[1:2, :] = total(jnp.where(pick, sub, 0))
    table[2:3, :] = total(jnp.where(pick, source_c, 0))
    mine = total(jnp.where(pick, goes_c, 0))
    before = total(jnp.where(rank_c + 1 == lane, goes_c, 0))
    table[3:4, :] = jnp.where((mine == before) & (lane_row % HALF != 0), 1, 0)
    upto = total(jnp.where(goes_c <= lane, 1, 0))
    below = total(jnp.where(goes_c < lane, 1, 0))
    left_end = jnp.minimum(upto, HALF)
    right_from = jnp.maximum(below, HALF)
    table[4:5, :] = jnp.maximum(left_end - 1, 0)
    table[5:6, :] = jnp.where(below < left_end, 1, 0)
    table[6:7, :] = jnp.maximum(upto - 1 - HALF, 0)
    table[7:8, :] = jnp.where(right_from < upto, 1, 0)


def layer_kernel(
    cap, slots, n_y, n_m, n_q, swap,
    feat, vals_hbm, rows_ref, cols_ref, counts_ref, ws_hbm, wn_hbm, bias_ref, pm_ref,
    out_v,
    vals, own, mirror, blocks, mirrors, sums, more, f_in, f_out, f_recv, m_in, m_out, m_recv, pre,
    ws_ref, wn_ref, ws_t, wn_t, bias_t, table_v, table,
    vals_sem, ws_sem, wn_sem, table_sem, mir_sem,
    swap_send, swap_recv, sib_send, sib_recv, y_send, y_recv, fwd_send, fwd_recv,
    msib_send, msib_recv, my_send, my_recv, mfwd_send, mfwd_recv,
    fs_sem, fr_sem, fms_sem, fmr_sem, ms_sem, mr_sem, mms_sem, mmr_sem,
):
    here = lax.axis_index("blk")
    me = lax.axis_index("bal")
    tiles, width, _ = own.shape
    wide = width + swap
    stay = width - swap
    n_bal = f_recv.shape[1] // width
    half = n_bal // 2
    base = me // half * half
    partner = (me + half) % n_bal
    sibling = here + 1 - 2 * (here % 2)
    across = (here + 2) % 4
    far = (sibling + 2) % 4
    y_tiles = tiles // n_y
    m_tiles = tiles // n_m
    q_tiles = cap // n_q
    own_rows = pl.ds(pl.multiple_of(me * width, width), width)
    mirror_rows = pl.ds(pl.multiple_of(partner * width + stay, 16), swap)

    def near(o):
        return base + (me + o) % half

    def other(o):
        return (base + half) % n_bal + (me + o) % half

    def each(first, last, body, unroll=1):
        def step(i, carry):
            body(i)
            return carry

        lax.fori_loop(first, last, step, 0, unroll=unroll)

    def remote(src, dst, send, recv, axis, peer):
        return pltpu.make_async_remote_copy(
            src, dst, send, recv, device_id={axis: peer}, device_id_type=MESH
        )

    load_vals = pltpu.make_async_copy(vals_hbm, vals, vals_sem)
    load_vals.start()
    load_ws = pltpu.make_async_copy(ws_hbm, ws_ref, ws_sem)
    load_ws.start()
    load_wn = pltpu.make_async_copy(wn_hbm, wn_ref, wn_sem)
    load_wn.start()

    barrier = pltpu.get_barrier_semaphore()
    for peer in (sibling, across):
        pl.semaphore_signal(barrier, inc=1, device_id={"blk": peer}, device_id_type=MESH)
    each(
        1, n_bal,
        lambda o: pl.semaphore_signal(
            barrier, inc=1, device_id={"bal": (me + o) % n_bal}, device_id_type=MESH
        ),
    )

    def pack(t):
        x = feat[:, pl.ds(pl.multiple_of(t * TILE, TILE), TILE)]
        own[t] = x
        blocks[here * tiles + t] = x

    each(0, tiles, pack, 4)
    pl.semaphore_wait(barrier, n_bal + 1)

    def swap_copy(i):
        span = pl.ds(i * m_tiles, m_tiles)
        return remote(
            own.at[span, pl.ds(stay, swap)], mirror.at[span],
            swap_send.at[i], swap_recv.at[i], "bal", partner,
        )

    def y_copy(i, whose):
        return remote(
            own.at[pl.ds(i * y_tiles, y_tiles)],
            blocks.at[pl.ds(whose * tiles + i * y_tiles, y_tiles)],
            y_send.at[i], y_recv.at[i], "blk", across,
        )

    def fwd_copy(i, whose):
        span = pl.ds(whose * tiles + i * y_tiles, y_tiles)
        part = blocks.at[span]
        return remote(part, part, fwd_send.at[i], fwd_recv.at[i], "blk", sibling)

    def sib_copy(whose):
        return remote(
            own, blocks.at[pl.ds(whose * tiles, tiles)],
            sib_send, sib_recv, "blk", sibling,
        )

    def my_copy(i, whose):
        return remote(
            mirror.at[pl.ds(i * m_tiles, m_tiles)],
            mirrors.at[pl.ds(whose * tiles + i * m_tiles, m_tiles)],
            my_send.at[i], my_recv.at[i], "blk", across,
        )

    def msib_copy(i, whose):
        return remote(
            mirror.at[pl.ds(i * m_tiles, m_tiles)],
            mirrors.at[pl.ds(whose * tiles + i * m_tiles, m_tiles)],
            msib_send.at[i], msib_recv.at[i], "blk", sibling,
        )

    def mfwd_copy(i, whose):
        span = pl.ds(whose * tiles + i * m_tiles, m_tiles)
        part = mirrors.at[span]
        return remote(part, part, mfwd_send.at[i], mfwd_recv.at[i], "blk", sibling)

    def f_near(o, whose):
        rows = pl.ds(pl.multiple_of(whose * width, width), width)
        return remote(
            f_in.at[o, :, pl.ds(0, width)], f_recv.at[:, rows],
            fs_sem.at[o], fr_sem.at[whose], "bal", near(o),
        )

    def f_near_mirror(o, whose):
        rows = pl.ds(pl.multiple_of((whose + half) % n_bal * width + stay, 16), swap)
        return remote(
            f_in.at[o, :, pl.ds(width, swap)], f_recv.at[:, rows],
            fms_sem.at[o], fmr_sem.at[whose], "bal", near(o),
        )

    def f_other(o, whose):
        rows = pl.ds(pl.multiple_of(whose * width, width), stay)
        return remote(
            f_out.at[o], f_recv.at[:, rows],
            fs_sem.at[half + o], fr_sem.at[whose], "bal", other(o),
        )

    def m_near(q, o, whose):
        span = pl.ds(q * q_tiles, q_tiles)
        rows = pl.ds(pl.multiple_of(whose * width, width), width)
        return remote(
            m_in.at[o, span, pl.ds(0, width)], m_recv.at[span, rows],
            ms_sem.at[q, o], mr_sem.at[q, whose], "bal", near(o),
        )

    def m_near_mirror(q, o, whose):
        span = pl.ds(q * q_tiles, q_tiles)
        rows = pl.ds(pl.multiple_of((whose + half) % n_bal * width + stay, 16), swap)
        return remote(
            m_in.at[o, span, pl.ds(width, swap)], m_recv.at[span, rows],
            mms_sem.at[q, o], mmr_sem.at[q, whose], "bal", near(o),
        )

    def m_other(q, o, whose):
        span = pl.ds(q * q_tiles, q_tiles)
        rows = pl.ds(pl.multiple_of(whose * width, width), stay)
        return remote(
            m_out.at[o, span], m_recv.at[span, rows],
            ms_sem.at[q, half + o], mr_sem.at[q, whose], "bal", other(o),
        )

    each(0, n_m, lambda i: swap_copy(i).start())
    each(0, n_y, lambda i: y_copy(i, here).start())
    sib_copy(here).start()

    tables(pm_ref, rows_ref, cols_ref, counts_ref, table_v, slots, cap)
    load_table = pltpu.make_async_copy(table_v, table, table_sem)
    load_table.start()
    load_table.wait()

    def send_f_near(o):
        def gather(k):
            f_in[o, k, :width, :] = own[table[0, near(o) * cap + k]]

        each(0, cap, gather, 4)
        f_near(o, me).start()

    def fill_f_other(o):
        def gather(k):
            f_out[o, k] = own[table[0, other(o) * cap + k]][:stay]

        each(0, cap, gather, 4)

    def keep_f(k):
        f_recv[k, own_rows, :] = own[table[0, me * cap + k]]

    each(1, half, send_f_near)
    if stay:
        each(0, half, fill_f_other)
    each(0, cap, keep_f, 4)
    load_vals.wait()
    load_ws.wait()
    ws_t[...] = ws_ref[...].T
    load_wn.wait()
    wn_t[...] = wn_ref[...].T
    bias_t[...] = jnp.broadcast_to(bias_ref[...], (TILE, bias_ref.shape[1])).T

    def pass_on(i):
        y_copy(i, across).wait_recv()
        fwd_copy(i, across).start()

    def take_mirror(i):
        swap_copy(i).wait_recv()
        my_copy(i, here).start()
        msib_copy(i, here).start()

    each(0, n_y, pass_on)
    each(0, n_m - 1, take_mirror)
    if stay:
        each(0, half, lambda o: f_other(o, me).start())
    each(n_m - 1, n_m, take_mirror)
    keep_mirror = pltpu.make_async_copy(
        mirror, mirrors.at[pl.ds(here * tiles, tiles)], mir_sem
    )
    keep_mirror.start()

    def send_f_mirror(o):
        def gather(k):
            f_in[o, k, width:, :] = mirror[table[0, near(o) * cap + k]]

        each(0, cap, gather, 4)
        f_near_mirror(o, me).start()

    def keep_f_mirror(k):
        f_recv[k, mirror_rows, :] = mirror[table[0, me * cap + k]]

    each(1, half, send_f_mirror)

    sib_copy(sibling).wait_recv()
    each(0, n_y, lambda i: fwd_copy(i, far).wait_recv())

    in_top = lax.broadcasted_iota(jnp.int32, (16, 2 * TILE), 0) < 8
    in_left = lax.broadcasted_iota(jnp.int32, (16, 2 * TILE), 1) < TILE
    ones = jnp.where(in_top == in_left, 1.0, 0.0).astype(jnp.bfloat16)
    deg_left = lax.broadcasted_iota(jnp.int32, (16, TILE), 0) < 8

    def products(j, held, count, extra):
        zeros = jnp.zeros((count, TILE), jnp.bfloat16)
        a = jnp.concatenate([vals[table[1, j]], vals[table[1, j + HALF]]], axis=1)
        x = jnp.concatenate([held[table[2, j]], zeros], axis=1)
        y = jnp.concatenate([zeros, held[table[2, j + HALF]]], axis=1)
        lhs = jnp.concatenate([x, y] + extra, axis=0)
        return lax.dot_general(
            lhs, a, (((1,), (1,)), ((), ())), preferred_element_type=jnp.float32
        )

    def absorb(j, carry):
        left, right, deg = carry
        prod = products(j, blocks, width, [ones])
        keep_left, keep_right = table[3, j], table[3, j + HALF]
        left = jnp.where(keep_left > 0, left, 0.0) + prod[:width]
        right = jnp.where(keep_right > 0, right, 0.0) + prod[width : 2 * width]
        deg = jnp.where(jnp.where(deg_left, keep_left, keep_right) > 0, deg, 0.0)
        deg = deg + prod[2 * width :]
        sums[j, :width, :] = left
        sums[j, width : 2 * width, :] = right
        sums[j, 2 * width :, :] = deg
        return left, right, deg

    def absorb_mirror(j, carry):
        left, right = carry
        prod = products(j, mirrors, swap, [])
        left = jnp.where(table[3, j] > 0, left, 0.0) + prod[:swap]
        right = jnp.where(table[3, j + HALF] > 0, right, 0.0) + prod[swap:]
        more[j, :swap, :] = left
        more[j, swap:, :] = right
        return left, right

    empty = jnp.zeros((width, TILE), jnp.float32)
    lax.fori_loop(
        0, HALF, absorb, (empty, empty, jnp.zeros((16, TILE), jnp.float32)), unroll=2
    )

    def inverse_degree(p):
        left, right = sums.at[table[4, p]], sums.at[table[6, p]]
        degree = (
            1.0
            + jnp.where(table[5, p] > 0, left[2 * width : 2 * width + 8, :], 0.0)
            + jnp.where(table[7, p] > 0, right[2 * width + 8 :, :], 0.0)
        )
        return (1.0 / degree)[:1]

    def mean_piece(p, inverse, where, count, right_row):
        left, right = where.at[table[4, p]], where.at[table[6, p]]
        agg = jnp.where(table[5, p] > 0, left[:count, :], 0.0) + jnp.where(
            table[7, p] > 0, right[right_row : right_row + count, :], 0.0
        )
        return (agg * inverse).astype(jnp.bfloat16)

    def send_m_other(q):
        def to_other(o):
            def fill(k):
                p = other(o) * cap + q * q_tiles + k
                m_out[o, q * q_tiles + k] = mean_piece(p, inverse_degree(p), sums, stay, width)

            each(0, q_tiles, fill, q_tiles)
            m_other(q, o, me).start()

        each(0, half, to_other)

    def send_m_near(q):
        def to_near(o):
            def fill(k):
                p = near(o) * cap + q * q_tiles + k
                m_in[o, q * q_tiles + k, :width, :] = mean_piece(
                    p, inverse_degree(p), sums, width, width
                )

            each(0, q_tiles, fill, q_tiles)
            m_near(q, o, me).start()

        each(1, half, to_near)

    def pass_mirror_on(i):
        my_copy(i, across).wait_recv()
        mfwd_copy(i, across).start()

    if stay:
        each(0, n_q, send_m_other)
    each(0, n_m, pass_mirror_on)
    each(0, n_q, send_m_near)
    each(0, n_m, lambda i: msib_copy(i, sibling).wait_recv())
    each(0, n_m, lambda i: mfwd_copy(i, far).wait_recv())
    keep_mirror.wait()
    lax.fori_loop(0, HALF, absorb_mirror, (empty[:swap], empty[:swap]), unroll=2)

    def send_m_mirror(q):
        def to_near(o):
            def fill(k):
                p = near(o) * cap + q * q_tiles + k
                m_in[o, q * q_tiles + k, width:, :] = mean_piece(
                    p, inverse_degree(p), more, swap, swap
                )

            each(0, q_tiles, fill, q_tiles)
            m_near_mirror(q, o, me).start()

        each(1, half, to_near)

    each(0, n_q, send_m_mirror)

    def keep_m(k):
        p = me * cap + k
        inverse = inverse_degree(p)
        m_recv[k, own_rows, :] = mean_piece(p, inverse, sums, width, width)
        m_recv[k, mirror_rows, :] = mean_piece(p, inverse, more, swap, swap)

    each(0, cap, keep_m, 4)
    each(0, cap, keep_f_mirror, 4)

    def wait_f_near(o):
        f_near(o, near(o)).wait_recv()
        f_near_mirror(o, near(o)).wait_recv()

    each(1, half, wait_f_near)
    if stay:
        each(0, half, lambda o: f_other(o, other(o)).wait_recv())

    rows = q_tiles * TILE

    def times(weight, recv, q):
        x = jnp.concatenate([recv[q * q_tiles + k] for k in range(q_tiles)], axis=1)
        return jnp.dot(weight[...], x, preferred_element_type=jnp.float32)

    def self_part(q):
        pre[q] = times(ws_t, f_recv, q) + jnp.concatenate([bias_t[...]] * q_tiles, axis=1)

    each(0, n_q, self_part)
    live = table[8, me * cap]

    def finish(q):
        def wait_near(o):
            m_near(q, o, near(o)).wait_recv()
            m_near_mirror(q, o, near(o)).wait_recv()

        each(1, half, wait_near)
        if stay:
            each(0, half, lambda o: m_other(q, o, other(o)).wait_recv())
        hidden = jnp.maximum(pre[q] + times(wn_t, m_recv, q), 0.0)
        row = q * rows + lax.broadcasted_iota(jnp.int32, (1, rows), 1)
        hidden = jnp.where(row < live * TILE, hidden, 0.0).astype(jnp.bfloat16)
        out_v[0, 0, pl.ds(pl.multiple_of(q * rows, rows), rows), :] = hidden.T

    each(0, n_q, finish)

    def settle_near(o):
        f_near(o, me).wait_send()
        f_near_mirror(o, me).wait_send()

        def one(q):
            m_near(q, o, me).wait_send()
            m_near_mirror(q, o, me).wait_send()

        each(0, n_q, one)

    def settle_other(o):
        f_other(o, me).wait_send()
        each(0, n_q, lambda q: m_other(q, o, me).wait_send())

    def settle_y(i):
        y_copy(i, here).wait_send()
        fwd_copy(i, across).wait_send()

    def settle_mirror(i):
        swap_copy(i).wait_send()
        my_copy(i, here).wait_send()
        msib_copy(i, here).wait_send()
        mfwd_copy(i, across).wait_send()

    each(1, half, settle_near)
    if stay:
        each(0, half, settle_other)
    each(0, n_y, settle_y)
    each(0, n_m, settle_mirror)
    sib_copy(here).wait_send()


def layer(
    features, tile_values, tile_rows, tile_cols, tile_counts, w_self, w_neigh, bias, part_map
):
    n_blk = lax.axis_size("blk")
    n_bal = lax.axis_size("bal")
    slots = tile_rows.shape[2]
    tiles = part_map.shape[1]
    cap = 2 * tiles // n_bal
    width = features.shape[1]
    total = w_self.shape[0]
    fits = (
        n_blk == 4 and n_blk * slots == TILE and tiles == HALF and width == HALF
        and n_bal * cap == TILE
    )
    if not fits:
        return on_device(
            features, tile_values, tile_rows, tile_cols, tile_counts, w_self, w_neigh, bias,
            part_map,
        )
    n_y, n_m, n_q = 4, 4, 4
    swap = width // 2
    wide, stay, half = width + swap, width - swap, n_bal // 2
    bf16, f32 = jnp.bfloat16, jnp.float32
    vmem = pl.BlockSpec(memory_space=pltpu.VMEM)
    smem = pl.BlockSpec(memory_space=pltpu.SMEM)
    hbm = pl.BlockSpec(memory_space=pl.ANY)
    dma = pltpu.SemaphoreType.DMA
    return pl.pallas_call(
        functools.partial(layer_kernel, cap, slots, n_y, n_m, n_q, swap),
        out_shape=pltpu.VMEM((1, 1, cap * TILE, total), bf16),
        in_specs=[vmem, hbm, vmem, vmem, smem, hbm, hbm, vmem, vmem],
        out_specs=vmem,
        scratch_shapes=[
            pltpu.VMEM((n_blk * slots, TILE, TILE), bf16),
            pltpu.VMEM((tiles, width, TILE), bf16),
            pltpu.VMEM((tiles, swap, TILE), bf16),
            pltpu.VMEM((n_blk * tiles, width, TILE), bf16),
            pltpu.VMEM((n_blk * tiles, swap, TILE), bf16),
            pltpu.VMEM((HALF, 2 * width + 16, TILE), f32),
            pltpu.VMEM((HALF, 2 * swap, TILE), f32),
            pltpu.VMEM((half, cap, wide, TILE), bf16),
            pltpu.VMEM((half, cap, max(stay, 16), TILE), bf16),
            pltpu.VMEM((cap, total, TILE), bf16),
            pltpu.VMEM((half, cap, wide, TILE), bf16),
            pltpu.VMEM((half, cap, max(stay, 16), TILE), bf16),
            pltpu.VMEM((cap, total, TILE), bf16),
            pltpu.VMEM((n_q, total, cap // n_q * TILE), f32),
            pltpu.VMEM((total, total), bf16),
            pltpu.VMEM((total, total), bf16),
            pltpu.VMEM((total, total), bf16),
            pltpu.VMEM((total, total), bf16),
            pltpu.VMEM((total, TILE), f32),
            pltpu.VMEM((16, TILE), jnp.int32),
            pltpu.SMEM((16, TILE), jnp.int32),
            dma, dma, dma, dma, dma,
            dma((n_m,)), dma((n_m,)), dma, dma, dma((n_y,)), dma((n_y,)), dma((n_y,)), dma((n_y,)),
            dma((n_m,)), dma((n_m,)), dma((n_m,)), dma((n_m,)), dma((n_m,)), dma((n_m,)),
            dma((n_bal,)), dma((n_bal,)), dma((half,)), dma((n_bal,)),
            dma((n_q, n_bal)), dma((n_q, n_bal)), dma((n_q, half)), dma((n_q, n_bal)),
        ],
        compiler_params=pltpu.CompilerParams(
            collective_id=0, has_side_effects=True, vmem_limit_bytes=56 * 2**20
        ),
        cost_estimate=pl.CostEstimate(
            flops=4 * cap * TILE * total * total, bytes_accessed=12 * 2**20, transcendentals=0
        ),
    )(
        features.T,
        tile_values.reshape(n_blk * slots, TILE, TILE),
        tile_rows[0],
        tile_cols[0],
        tile_counts,
        w_self,
        w_neigh,
        bias.reshape(1, total),
        part_map,
    )


def solution(mesh):
    placed = (
        P("blk", "bal"),
        P("blk", None, None, None, None),
        P("blk", None, None),
        P("blk", None, None),
        P("blk", None),
        P(),
        P(),
        P(),
        P("blk", None),
    )
    return jax.shard_map(
        layer,
        mesh=mesh,
        in_specs=placed,
        out_specs=P("blk", "bal", None, None),
        check_vma=False,
    )
```

```python
import functools
import jax
import jax.numpy as jnp
from jax import lax
from jax.experimental import pallas as pl
from jax.experimental.pallas import tpu as pltpu
from jax.sharding import PartitionSpec as P

TILE = 128
HALF = 64
MESH = pl.DeviceIdType.MESH


def from_behind(block, axis, distance):
    devices = range(lax.axis_size(axis))
    route = [((i - distance) % len(devices), i) for i in devices]
    return lax.ppermute(block, axis, route)


def advance(block, steps_by):
    return from_behind(block, "blk", steps_by)


def on_device(
    features, tile_values, tile_rows, tile_cols, tile_counts, w_self, w_neigh, bias, part_map
):
    n_blk = lax.axis_size("blk")
    n_bal = lax.axis_size("bal")
    here = lax.axis_index("blk")
    column = lax.axis_index("bal")
    width = features.shape[1]
    tiles_per = part_map.shape[1]
    values = tile_values[0]
    rows_idx = tile_rows[0]
    cols_idx = tile_cols[0]
    counts = tile_counts[0]
    slots = values.shape[1]
    live = jnp.arange(slots)[None, :] < counts[:, None]
    row_hot = (
        (rows_idx[:, :, None] == jnp.arange(tiles_per)[None, None, :]) & live[:, :, None]
    ).astype(jnp.float32)
    row_mass = jnp.einsum(
        "csij,j->csi", values, jnp.ones((TILE,), jnp.bfloat16), preferred_element_type=jnp.float32
    )
    degree = 1.0 + jnp.einsum("cst,csi->ti", row_hot, row_mass, precision=lax.Precision.HIGHEST)

    def absorb(total, block, source):
        tiles = block.reshape(tiles_per, TILE, width)
        vals = lax.dynamic_index_in_dim(values, source, 0, keepdims=False)
        picks = lax.dynamic_index_in_dim(cols_idx, source, 0, keepdims=False)
        targets = lax.dynamic_index_in_dim(rows_idx, source, 0, keepdims=False)
        alive = lax.dynamic_index_in_dim(live, source, 0, keepdims=False)
        gathered = jnp.take(tiles, picks, axis=0)
        prod = jnp.einsum("sij,sjf->sif", vals, gathered, preferred_element_type=jnp.float32)
        masked = jnp.where(alive[:, None, None], prod, 0.0)
        return total.at[targets].add(masked)

    empty = jnp.zeros((tiles_per, TILE, width), jnp.float32)

    def step_one(index, carry):
        total, block = carry
        total = absorb(total, block, (here - index) % n_blk)
        block = advance(block, 1)
        return (total, block)

    total, block = lax.fori_loop(0, n_blk - 1, step_one, (empty, features))
    total = absorb(total, block, (here - (n_blk - 1)) % n_blk)
    mean_agg = (total / degree[:, :, None]).astype(jnp.bfloat16).reshape(tiles_per * TILE, width)
    capacity = 2 * tiles_per // n_bal
    mapping = part_map[0]
    dest_hot = (mapping[:, None] == jnp.arange(n_bal)[None, :]).astype(jnp.int32)
    ranks = jnp.cumsum(dest_hot, axis=0) - dest_hot
    place = mapping * capacity + jnp.sum(ranks * dest_hot, axis=1)
    select = (jnp.arange(n_bal * capacity)[:, None] == place[None, :]).astype(jnp.bfloat16)
    col_start = column * width
    zeros_out = jnp.zeros((tiles_per * TILE, width), jnp.float32)
    carry = zeros_out
    mean_piece = lax.all_gather(mean_agg, "bal", axis=1, tiled=True)
    feat_piece = lax.all_gather(features, "bal", axis=1, tiled=True)
    count = mean_piece.shape[1]
    neigh_part = lax.dynamic_slice(w_neigh, (0, col_start), (count, width))
    self_part = lax.dynamic_slice(w_self, (0, col_start), (count, width))
    carry = jnp.dot(mean_piece, neigh_part, preferred_element_type=jnp.float32)
    pre = carry + jnp.dot(feat_piece, self_part, preferred_element_type=jnp.float32)
    pre = pre + lax.dynamic_slice_in_dim(bias, col_start, width)
    hidden = jnp.maximum(pre, 0.0).astype(jnp.bfloat16)
    tiles = hidden.reshape(tiles_per, TILE, width)
    placed = jnp.einsum("kt,tif->kif", select, tiles, preferred_element_type=jnp.float32)
    result = lax.all_to_all(
        placed.astype(jnp.bfloat16).reshape(n_bal, capacity * TILE, width),
        "bal",
        split_axis=0,
        concat_axis=2,
        tiled=True,
    )
    return result[None]


def tables(pm_ref, rows_ref, cols_ref, counts_ref, table, slots, cap):
    n_src = rows_ref.shape[0]
    table[...] = jnp.zeros(table.shape, jnp.int32)
    square = (TILE, TILE)
    lane = lax.broadcasted_iota(jnp.int32, square, 1)
    sub = lax.broadcasted_iota(jnp.int32, square, 0)

    def spread(row):
        return jnp.broadcast_to(row, square)

    def total(x):
        return jnp.sum(x, axis=0, keepdims=True)

    def flat(ref):
        return jnp.concatenate([ref[c : c + 1, :] for c in range(n_src)], axis=1)

    pm = pm_ref[...]
    pm = jnp.concatenate([pm, jnp.full((1, TILE - pm.shape[1]), 999, jnp.int32)], axis=1)
    pm_r = spread(pm)
    pm_c = pm_r.T
    earlier = jnp.where((pm_c == pm_r) & (sub < lane), 1, 0)
    place_c = spread(pm * cap + total(earlier)).T
    table[0:1, :] = total(jnp.where(place_c == lane, sub, 0))
    table[8:9, :] = total(jnp.where(pm_c == lane // cap, 1, 0))

    lane_row = lax.broadcasted_iota(jnp.int32, (1, TILE), 1)
    alive = jnp.zeros((1, TILE), jnp.int32)
    for c in range(n_src):
        alive = jnp.where(lane_row // slots == c, counts_ref[0, c], alive)
    rows_r = spread(flat(rows_ref))
    goes = total(jnp.where(rows_r == sub, place_c, 0))
    goes = jnp.where(lane_row % slots < alive, goes, 4096)
    goes_r = spread(goes)
    goes_c = goes_r.T
    rank_c = spread(total(jnp.where(goes_c * TILE + sub < goes_r * TILE + lane, 1, 0))).T
    pick = rank_c == lane
    source = (lane_row // slots) * HALF + flat(cols_ref)
    source_c = spread(source).T
    table[1:2, :] = total(jnp.where(pick, sub, 0))
    table[2:3, :] = total(jnp.where(pick, source_c, 0))
    mine = total(jnp.where(pick, goes_c, 0))
    before = total(jnp.where(rank_c + 1 == lane, goes_c, 0))
    table[3:4, :] = jnp.where((mine == before) & (lane_row % HALF != 0), 1, 0)
    upto = total(jnp.where(goes_c <= lane, 1, 0))
    below = total(jnp.where(goes_c < lane, 1, 0))
    left_end = jnp.minimum(upto, HALF)
    right_from = jnp.maximum(below, HALF)
    table[4:5, :] = jnp.maximum(left_end - 1, 0)
    table[5:6, :] = jnp.where(below < left_end, 1, 0)
    table[6:7, :] = jnp.maximum(upto - 1 - HALF, 0)
    table[7:8, :] = jnp.where(right_from < upto, 1, 0)


def layer_kernel(
    cap, slots, n_y, n_m, n_q, swap,
    feat_hbm, vals_hbm, rows_ref, cols_ref, counts_ref, ws_hbm, wn_hbm, bias_ref, pm_ref,
    out_v,
    feat, vals, own, mirror, blocks, mirrors, sums, more, f_in, f_out, f_recv, m_in, m_out, m_recv, pre,
    ws_ref, wn_ref, ws_t, wn_t, bias_t, table_v, table,
    feat_sem, vals_sem, ws_sem, wn_sem, table_sem, mir_sem,
    swap_send, swap_recv, sib_send, sib_recv, y_send, y_recv, fwd_send, fwd_recv,
    msib_send, msib_recv, my_send, my_recv, mfwd_send, mfwd_recv,
    fs_sem, fr_sem, fms_sem, fmr_sem, ms_sem, mr_sem, mms_sem, mmr_sem,
):
    here = lax.axis_index("blk")
    me = lax.axis_index("bal")
    tiles, width, _ = own.shape
    wide = width + swap
    stay = width - swap
    n_bal = f_recv.shape[1] // width
    half = n_bal // 2
    at_end = (me % half < half // 2) == (me // half == 0)
    base = me // half * half
    partner = (me + half) % n_bal
    sibling = here + 1 - 2 * (here % 2)
    across = (here + 2) % 4
    far = (sibling + 2) % 4
    y_tiles = tiles // n_y
    m_tiles = tiles // n_m
    q_tiles = cap // n_q
    own_rows = pl.ds(pl.multiple_of(me * width, width), width)
    mirror_rows = pl.ds(pl.multiple_of(partner * width + stay, 16), swap)

    def near(o):
        return base + (me + o) % half

    def other(o):
        return (base + half) % n_bal + (me + o) % half

    def each(first, last, body, unroll=1):
        def step(i, carry):
            body(i)
            return carry

        lax.fori_loop(first, last, step, 0, unroll=unroll)

    def remote(src, dst, send, recv, axis, peer):
        return pltpu.make_async_remote_copy(
            src, dst, send, recv, device_id={axis: peer}, device_id_type=MESH
        )

    barrier = pltpu.get_barrier_semaphore()
    for peer in (sibling, across):
        pl.semaphore_signal(barrier, inc=1, device_id={"blk": peer}, device_id_type=MESH)
    each(
        1, n_bal,
        lambda o: pl.semaphore_signal(
            barrier, inc=1, device_id={"bal": (me + o) % n_bal}, device_id_type=MESH
        ),
    )

    span_y = y_tiles * TILE

    def load_feat(i):
        part = pl.ds(pl.multiple_of(i * span_y, span_y), span_y)
        return pltpu.make_async_copy(feat_hbm.at[:, part], feat.at[:, part], feat_sem.at[i])

    each(0, n_y, lambda i: load_feat(i).start())
    load_vals = pltpu.make_async_copy(vals_hbm, vals, vals_sem)
    load_ws = pltpu.make_async_copy(ws_hbm, ws_ref, ws_sem)
    load_wn = pltpu.make_async_copy(wn_hbm, wn_ref, wn_sem)

    def pack(t):
        x = feat[:, pl.ds(pl.multiple_of(t * TILE, TILE), TILE)]
        own[t] = x
        blocks[here * tiles + t] = x

    def pack_part(i):
        load_feat(i).wait()
        each(0, y_tiles, lambda t: pack(i * y_tiles + t), 4)

    each(0, n_y, pack_part)
    pl.semaphore_wait(barrier, n_bal + 1)

    def swap_copy(i):
        span = pl.ds(i * m_tiles, m_tiles)
        return remote(
            own.at[span, pl.ds(stay, swap)], mirror.at[span],
            swap_send.at[i], swap_recv.at[i], "bal", partner,
        )

    def y_copy(i, whose):
        return remote(
            own.at[pl.ds(i * y_tiles, y_tiles)],
            blocks.at[pl.ds(whose * tiles + i * y_tiles, y_tiles)],
            y_send.at[i], y_recv.at[i], "blk", across,
        )

    def fwd_copy(i, whose):
        span = pl.ds(whose * tiles + i * y_tiles, y_tiles)
        part = blocks.at[span]
        return remote(part, part, fwd_send.at[i], fwd_recv.at[i], "blk", sibling)

    def sib_copy(whose):
        return remote(
            own, blocks.at[pl.ds(whose * tiles, tiles)],
            sib_send, sib_recv, "blk", sibling,
        )

    def my_copy(i, whose):
        return remote(
            mirror.at[pl.ds(i * m_tiles, m_tiles)],
            mirrors.at[pl.ds(whose * tiles + i * m_tiles, m_tiles)],
            my_send.at[i], my_recv.at[i], "blk", across,
        )

    def msib_copy(i, whose):
        return remote(
            mirror.at[pl.ds(i * m_tiles, m_tiles)],
            mirrors.at[pl.ds(whose * tiles + i * m_tiles, m_tiles)],
            msib_send.at[i], msib_recv.at[i], "blk", sibling,
        )

    def mfwd_copy(i, whose):
        span = pl.ds(whose * tiles + i * m_tiles, m_tiles)
        part = mirrors.at[span]
        return remote(part, part, mfwd_send.at[i], mfwd_recv.at[i], "blk", sibling)

    def f_near(o, whose):
        rows = pl.ds(pl.multiple_of(whose * width, width), width)
        return remote(
            f_in.at[o, :, pl.ds(0, width)], f_recv.at[:, rows],
            fs_sem.at[o], fr_sem.at[whose], "bal", near(o),
        )

    def f_near_mirror(o, whose):
        rows = pl.ds(pl.multiple_of((whose + half) % n_bal * width + stay, 16), swap)
        return remote(
            f_in.at[o, :, pl.ds(width, swap)], f_recv.at[:, rows],
            fms_sem.at[o], fmr_sem.at[whose], "bal", near(o),
        )

    def f_other(o, whose):
        rows = pl.ds(pl.multiple_of(whose * width, width), stay)
        return remote(
            f_out.at[o], f_recv.at[:, rows],
            fs_sem.at[half + o], fr_sem.at[whose], "bal", other(o),
        )

    def m_near(q, o, whose):
        span = pl.ds(q * q_tiles, q_tiles)
        rows = pl.ds(pl.multiple_of(whose * width, width), width)
        return remote(
            m_in.at[o, span, pl.ds(0, width)], m_recv.at[span, rows],
            ms_sem.at[q, o], mr_sem.at[q, whose], "bal", near(o),
        )

    def m_near_mirror(q, o, whose):
        span = pl.ds(q * q_tiles, q_tiles)
        rows = pl.ds(pl.multiple_of((whose + half) % n_bal * width + stay, 16), swap)
        return remote(
            m_in.at[o, span, pl.ds(width, swap)], m_recv.at[span, rows],
            mms_sem.at[q, o], mmr_sem.at[q, whose], "bal", near(o),
        )

    def m_other(q, o, whose):
        span = pl.ds(q * q_tiles, q_tiles)
        rows = pl.ds(pl.multiple_of(whose * width, width), stay)
        return remote(
            m_out.at[o, span], m_recv.at[span, rows],
            ms_sem.at[q, half + o], mr_sem.at[q, whose], "bal", other(o),
        )

    each(0, n_m, lambda i: swap_copy(i).start())
    each(0, n_y, lambda i: y_copy(i, here).start())
    sib_copy(here).start()

    load_vals.start()
    load_ws.start()
    load_wn.start()
    tables(pm_ref, rows_ref, cols_ref, counts_ref, table_v, slots, cap)
    load_table = pltpu.make_async_copy(table_v, table, table_sem)
    load_table.start()
    load_table.wait()

    def send_f_near(o):
        def gather(k):
            f_in[o, k, :width, :] = own[table[0, near(o) * cap + k]]

        each(0, cap, gather, 4)
        f_near(o, me).start()

    def fill_f_other(o):
        def gather(k):
            f_out[o, k] = own[table[0, other(o) * cap + k]][:stay]

        each(0, cap, gather, 4)

    def keep_f(k):
        f_recv[k, own_rows, :] = own[table[0, me * cap + k]]

    each(1, half, send_f_near)
    if stay:
        each(0, half, fill_f_other)
    each(0, cap, keep_f, 4)
    load_vals.wait()
    load_ws.wait()
    ws_t[...] = ws_ref[...].T
    load_wn.wait()
    wn_t[...] = wn_ref[...].T
    bias_t[...] = jnp.broadcast_to(bias_ref[...], (TILE, bias_ref.shape[1])).T

    def pass_on(i):
        y_copy(i, across).wait_recv()
        fwd_copy(i, across).start()

    def take_mirror(i):
        swap_copy(i).wait_recv()
        my_copy(i, here).start()
        msib_copy(i, here).start()

    each(0, n_y, pass_on)
    each(0, n_m - 1, take_mirror)

    def send_f_other():
        each(0, half, lambda o: f_other(o, me).start())

    if stay:
        pl.when(at_end)(send_f_other)
    each(n_m - 1, n_m, take_mirror)
    keep_mirror = pltpu.make_async_copy(
        mirror, mirrors.at[pl.ds(here * tiles, tiles)], mir_sem
    )
    keep_mirror.start()

    def send_f_mirror(o):
        def gather(k):
            f_in[o, k, width:, :] = mirror[table[0, near(o) * cap + k]]

        each(0, cap, gather, 4)
        f_near_mirror(o, me).start()

    def keep_f_mirror(k):
        f_recv[k, mirror_rows, :] = mirror[table[0, me * cap + k]]

    each(1, half, send_f_mirror)
    if stay:
        pl.when(jnp.logical_not(at_end))(send_f_other)

    sib_copy(sibling).wait_recv()
    each(0, n_y, lambda i: fwd_copy(i, far).wait_recv())

    in_top = lax.broadcasted_iota(jnp.int32, (16, 2 * TILE), 0) < 8
    in_left = lax.broadcasted_iota(jnp.int32, (16, 2 * TILE), 1) < TILE
    ones = jnp.where(in_top == in_left, 1.0, 0.0).astype(jnp.bfloat16)
    deg_left = lax.broadcasted_iota(jnp.int32, (16, TILE), 0) < 8

    def products(j, held, count, extra):
        zeros = jnp.zeros((count, TILE), jnp.bfloat16)
        a = jnp.concatenate([vals[table[1, j]], vals[table[1, j + HALF]]], axis=1)
        x = jnp.concatenate([held[table[2, j]], zeros], axis=1)
        y = jnp.concatenate([zeros, held[table[2, j + HALF]]], axis=1)
        lhs = jnp.concatenate([x, y] + extra, axis=0)
        return lax.dot_general(
            lhs, a, (((1,), (1,)), ((), ())), preferred_element_type=jnp.float32
        )

    def absorb(j, carry):
        left, right, deg = carry
        prod = products(j, blocks, width, [ones])
        keep_left, keep_right = table[3, j], table[3, j + HALF]
        left = jnp.where(keep_left > 0, left, 0.0) + prod[:width]
        right = jnp.where(keep_right > 0, right, 0.0) + prod[width : 2 * width]
        deg = jnp.where(jnp.where(deg_left, keep_left, keep_right) > 0, deg, 0.0)
        deg = deg + prod[2 * width :]
        sums[j, :width, :] = left
        sums[j, width : 2 * width, :] = right
        sums[j, 2 * width :, :] = deg
        return left, right, deg

    def absorb_mirror(j, carry):
        left, right = carry
        prod = products(j, mirrors, swap, [])
        left = jnp.where(table[3, j] > 0, left, 0.0) + prod[:swap]
        right = jnp.where(table[3, j + HALF] > 0, right, 0.0) + prod[swap:]
        more[j, :swap, :] = left
        more[j, swap:, :] = right
        return left, right

    empty = jnp.zeros((width, TILE), jnp.float32)
    lax.fori_loop(
        0, HALF, absorb, (empty, empty, jnp.zeros((16, TILE), jnp.float32)), unroll=2
    )

    def inverse_degree(p):
        left, right = sums.at[table[4, p]], sums.at[table[6, p]]
        degree = (
            1.0
            + jnp.where(table[5, p] > 0, left[2 * width : 2 * width + 8, :], 0.0)
            + jnp.where(table[7, p] > 0, right[2 * width + 8 :, :], 0.0)
        )
        return (1.0 / degree)[:1]

    def mean_piece(p, inverse, where, count, right_row):
        left, right = where.at[table[4, p]], where.at[table[6, p]]
        agg = jnp.where(table[5, p] > 0, left[:count, :], 0.0) + jnp.where(
            table[7, p] > 0, right[right_row : right_row + count, :], 0.0
        )
        return (agg * inverse).astype(jnp.bfloat16)

    def send_m_other(q):
        def to_other(o):
            def fill(k):
                p = other(o) * cap + q * q_tiles + k
                m_out[o, q * q_tiles + k] = mean_piece(p, inverse_degree(p), sums, stay, width)

            each(0, q_tiles, fill, q_tiles)
            m_other(q, o, me).start()

        each(0, half, to_other)

    def send_m_near(q):
        def to_near(o):
            def fill(k):
                p = near(o) * cap + q * q_tiles + k
                m_in[o, q * q_tiles + k, :width, :] = mean_piece(
                    p, inverse_degree(p), sums, width, width
                )

            each(0, q_tiles, fill, q_tiles)
            m_near(q, o, me).start()

        each(1, half, to_near)

    def pass_mirror_on(i):
        my_copy(i, across).wait_recv()
        mfwd_copy(i, across).start()

    def send_all_m_other():
        each(0, n_q, send_m_other)

    if stay:
        pl.when(at_end)(send_all_m_other)
    each(0, n_m, pass_mirror_on)
    each(0, n_q, send_m_near)
    if stay:
        pl.when(jnp.logical_not(at_end))(send_all_m_other)
    each(0, n_m, lambda i: msib_copy(i, sibling).wait_recv())
    each(0, n_m, lambda i: mfwd_copy(i, far).wait_recv())
    keep_mirror.wait()
    lax.fori_loop(0, HALF, absorb_mirror, (empty[:swap], empty[:swap]), unroll=2)

    def send_m_mirror(q):
        def to_near(o):
            def fill(k):
                p = near(o) * cap + q * q_tiles + k
                m_in[o, q * q_tiles + k, width:, :] = mean_piece(
                    p, inverse_degree(p), more, swap, swap
                )

            each(0, q_tiles, fill, q_tiles)
            m_near_mirror(q, o, me).start()

        each(1, half, to_near)

    each(0, n_q, send_m_mirror)

    def keep_m(k):
        p = me * cap + k
        inverse = inverse_degree(p)
        m_recv[k, own_rows, :] = mean_piece(p, inverse, sums, width, width)
        m_recv[k, mirror_rows, :] = mean_piece(p, inverse, more, swap, swap)

    each(0, cap, keep_m, 4)
    each(0, cap, keep_f_mirror, 4)

    def wait_f_near(o):
        f_near(o, near(o)).wait_recv()
        f_near_mirror(o, near(o)).wait_recv()

    each(1, half, wait_f_near)
    if stay:
        each(0, half, lambda o: f_other(o, other(o)).wait_recv())

    rows = q_tiles * TILE

    def times(weight, recv, q):
        x = jnp.concatenate([recv[q * q_tiles + k] for k in range(q_tiles)], axis=1)
        return jnp.dot(weight[...], x, preferred_element_type=jnp.float32)

    def self_part(q):
        pre[q] = times(ws_t, f_recv, q) + jnp.concatenate([bias_t[...]] * q_tiles, axis=1)

    each(0, n_q, self_part)
    live = table[8, me * cap]

    def finish(q):
        def wait_near(o):
            m_near(q, o, near(o)).wait_recv()
            m_near_mirror(q, o, near(o)).wait_recv()

        each(1, half, wait_near)
        if stay:
            each(0, half, lambda o: m_other(q, o, other(o)).wait_recv())
        hidden = jnp.maximum(pre[q] + times(wn_t, m_recv, q), 0.0)
        row = q * rows + lax.broadcasted_iota(jnp.int32, (1, rows), 1)
        hidden = jnp.where(row < live * TILE, hidden, 0.0).astype(jnp.bfloat16)
        out_v[0, 0, pl.ds(pl.multiple_of(q * rows, rows), rows), :] = hidden.T

    each(0, n_q, finish)

    def settle_near(o):
        f_near(o, me).wait_send()
        f_near_mirror(o, me).wait_send()

        def one(q):
            m_near(q, o, me).wait_send()
            m_near_mirror(q, o, me).wait_send()

        each(0, n_q, one)

    def settle_other(o):
        f_other(o, me).wait_send()
        each(0, n_q, lambda q: m_other(q, o, me).wait_send())

    def settle_y(i):
        y_copy(i, here).wait_send()
        fwd_copy(i, across).wait_send()

    def settle_mirror(i):
        swap_copy(i).wait_send()
        my_copy(i, here).wait_send()
        msib_copy(i, here).wait_send()
        mfwd_copy(i, across).wait_send()

    each(1, half, settle_near)
    if stay:
        each(0, half, settle_other)
    each(0, n_y, settle_y)
    each(0, n_m, settle_mirror)
    sib_copy(here).wait_send()


def layer(
    features, tile_values, tile_rows, tile_cols, tile_counts, w_self, w_neigh, bias, part_map
):
    n_blk = lax.axis_size("blk")
    n_bal = lax.axis_size("bal")
    slots = tile_rows.shape[2]
    tiles = part_map.shape[1]
    cap = 2 * tiles // n_bal
    width = features.shape[1]
    total = w_self.shape[0]
    fits = (
        n_blk == 4 and n_blk * slots == TILE and tiles == HALF and width == HALF
        and n_bal * cap == TILE
    )
    if not fits:
        return on_device(
            features, tile_values, tile_rows, tile_cols, tile_counts, w_self, w_neigh, bias,
            part_map,
        )
    n_y, n_m, n_q = 4, 4, 4
    swap = width // 2
    wide, stay, half = width + swap, width - swap, n_bal // 2
    bf16, f32 = jnp.bfloat16, jnp.float32
    vmem = pl.BlockSpec(memory_space=pltpu.VMEM)
    smem = pl.BlockSpec(memory_space=pltpu.SMEM)
    hbm = pl.BlockSpec(memory_space=pl.ANY)
    dma = pltpu.SemaphoreType.DMA
    return pl.pallas_call(
        functools.partial(layer_kernel, cap, slots, n_y, n_m, n_q, swap),
        out_shape=pltpu.VMEM((1, 1, cap * TILE, total), bf16),
        in_specs=[hbm, hbm, vmem, vmem, smem, hbm, hbm, vmem, vmem],
        out_specs=vmem,
        scratch_shapes=[
            pltpu.VMEM((width, tiles * TILE), bf16),
            pltpu.VMEM((n_blk * slots, TILE, TILE), bf16),
            pltpu.VMEM((tiles, width, TILE), bf16),
            pltpu.VMEM((tiles, swap, TILE), bf16),
            pltpu.VMEM((n_blk * tiles, width, TILE), bf16),
            pltpu.VMEM((n_blk * tiles, swap, TILE), bf16),
            pltpu.VMEM((HALF, 2 * width + 16, TILE), f32),
            pltpu.VMEM((HALF, 2 * swap, TILE), f32),
            pltpu.VMEM((half, cap, wide, TILE), bf16),
            pltpu.VMEM((half, cap, max(stay, 16), TILE), bf16),
            pltpu.VMEM((cap, total, TILE), bf16),
            pltpu.VMEM((half, cap, wide, TILE), bf16),
            pltpu.VMEM((half, cap, max(stay, 16), TILE), bf16),
            pltpu.VMEM((cap, total, TILE), bf16),
            pltpu.VMEM((n_q, total, cap // n_q * TILE), f32),
            pltpu.VMEM((total, total), bf16),
            pltpu.VMEM((total, total), bf16),
            pltpu.VMEM((total, total), bf16),
            pltpu.VMEM((total, total), bf16),
            pltpu.VMEM((total, TILE), f32),
            pltpu.VMEM((16, TILE), jnp.int32),
            pltpu.SMEM((16, TILE), jnp.int32),
            dma((n_y,)), dma, dma, dma, dma, dma,
            dma((n_m,)), dma((n_m,)), dma, dma, dma((n_y,)), dma((n_y,)), dma((n_y,)), dma((n_y,)),
            dma((n_m,)), dma((n_m,)), dma((n_m,)), dma((n_m,)), dma((n_m,)), dma((n_m,)),
            dma((n_bal,)), dma((n_bal,)), dma((half,)), dma((n_bal,)),
            dma((n_q, n_bal)), dma((n_q, n_bal)), dma((n_q, half)), dma((n_q, n_bal)),
        ],
        compiler_params=pltpu.CompilerParams(
            collective_id=0, has_side_effects=True, vmem_limit_bytes=56 * 2**20
        ),
        cost_estimate=pl.CostEstimate(
            flops=4 * cap * TILE * total * total, bytes_accessed=12 * 2**20, transcendentals=0
        ),
    )(
        features.T,
        tile_values.reshape(n_blk * slots, TILE, TILE),
        tile_rows[0],
        tile_cols[0],
        tile_counts,
        w_self,
        w_neigh,
        bias.reshape(1, total),
        part_map,
    )


def solution(mesh):
    placed = (
        P("blk", "bal"),
        P("blk", None, None, None, None),
        P("blk", None, None),
        P("blk", None, None),
        P("blk", None),
        P(),
        P(),
        P(),
        P("blk", None),
    )
    return jax.shard_map(
        layer,
        mesh=mesh,
        in_specs=placed,
        out_specs=P("blk", "bal", None, None),
        check_vma=False,
    )
```

```python
import functools
import jax
import jax.numpy as jnp
from jax import lax
from jax.experimental import pallas as pl
from jax.experimental.pallas import tpu as pltpu
from jax.sharding import PartitionSpec as P

TILE = 128
HALF = 64
MESH = pl.DeviceIdType.MESH


def from_behind(block, axis, distance):
    devices = range(lax.axis_size(axis))
    route = [((i - distance) % len(devices), i) for i in devices]
    return lax.ppermute(block, axis, route)


def advance(block, steps_by):
    return from_behind(block, "blk", steps_by)


def on_device(
    features, tile_values, tile_rows, tile_cols, tile_counts, w_self, w_neigh, bias, part_map
):
    n_blk = lax.axis_size("blk")
    n_bal = lax.axis_size("bal")
    here = lax.axis_index("blk")
    column = lax.axis_index("bal")
    width = features.shape[1]
    tiles_per = part_map.shape[1]
    values = tile_values[0]
    rows_idx = tile_rows[0]
    cols_idx = tile_cols[0]
    counts = tile_counts[0]
    slots = values.shape[1]
    live = jnp.arange(slots)[None, :] < counts[:, None]
    row_hot = (
        (rows_idx[:, :, None] == jnp.arange(tiles_per)[None, None, :]) & live[:, :, None]
    ).astype(jnp.float32)
    row_mass = jnp.einsum(
        "csij,j->csi", values, jnp.ones((TILE,), jnp.bfloat16), preferred_element_type=jnp.float32
    )
    degree = 1.0 + jnp.einsum("cst,csi->ti", row_hot, row_mass, precision=lax.Precision.HIGHEST)

    def absorb(total, block, source):
        tiles = block.reshape(tiles_per, TILE, width)
        vals = lax.dynamic_index_in_dim(values, source, 0, keepdims=False)
        picks = lax.dynamic_index_in_dim(cols_idx, source, 0, keepdims=False)
        targets = lax.dynamic_index_in_dim(rows_idx, source, 0, keepdims=False)
        alive = lax.dynamic_index_in_dim(live, source, 0, keepdims=False)
        gathered = jnp.take(tiles, picks, axis=0)
        prod = jnp.einsum("sij,sjf->sif", vals, gathered, preferred_element_type=jnp.float32)
        masked = jnp.where(alive[:, None, None], prod, 0.0)
        return total.at[targets].add(masked)

    empty = jnp.zeros((tiles_per, TILE, width), jnp.float32)

    def step_one(index, carry):
        total, block = carry
        total = absorb(total, block, (here - index) % n_blk)
        block = advance(block, 1)
        return (total, block)

    total, block = lax.fori_loop(0, n_blk - 1, step_one, (empty, features))
    total = absorb(total, block, (here - (n_blk - 1)) % n_blk)
    mean_agg = (total / degree[:, :, None]).astype(jnp.bfloat16).reshape(tiles_per * TILE, width)
    capacity = 2 * tiles_per // n_bal
    mapping = part_map[0]
    dest_hot = (mapping[:, None] == jnp.arange(n_bal)[None, :]).astype(jnp.int32)
    ranks = jnp.cumsum(dest_hot, axis=0) - dest_hot
    place = mapping * capacity + jnp.sum(ranks * dest_hot, axis=1)
    select = (jnp.arange(n_bal * capacity)[:, None] == place[None, :]).astype(jnp.bfloat16)
    col_start = column * width
    zeros_out = jnp.zeros((tiles_per * TILE, width), jnp.float32)
    carry = zeros_out
    mean_piece = lax.all_gather(mean_agg, "bal", axis=1, tiled=True)
    feat_piece = lax.all_gather(features, "bal", axis=1, tiled=True)
    count = mean_piece.shape[1]
    neigh_part = lax.dynamic_slice(w_neigh, (0, col_start), (count, width))
    self_part = lax.dynamic_slice(w_self, (0, col_start), (count, width))
    carry = jnp.dot(mean_piece, neigh_part, preferred_element_type=jnp.float32)
    pre = carry + jnp.dot(feat_piece, self_part, preferred_element_type=jnp.float32)
    pre = pre + lax.dynamic_slice_in_dim(bias, col_start, width)
    hidden = jnp.maximum(pre, 0.0).astype(jnp.bfloat16)
    tiles = hidden.reshape(tiles_per, TILE, width)
    placed = jnp.einsum("kt,tif->kif", select, tiles, preferred_element_type=jnp.float32)
    result = lax.all_to_all(
        placed.astype(jnp.bfloat16).reshape(n_bal, capacity * TILE, width),
        "bal",
        split_axis=0,
        concat_axis=2,
        tiled=True,
    )
    return result[None]


def tables(pm_ref, rows_ref, cols_ref, counts_ref, table, slots, cap):
    n_src = rows_ref.shape[0]
    table[...] = jnp.zeros(table.shape, jnp.int32)
    square = (TILE, TILE)
    lane = lax.broadcasted_iota(jnp.int32, square, 1)
    sub = lax.broadcasted_iota(jnp.int32, square, 0)

    def spread(row):
        return jnp.broadcast_to(row, square)

    def total(x):
        return jnp.sum(x, axis=0, keepdims=True)

    def flat(ref):
        return jnp.concatenate([ref[c : c + 1, :] for c in range(n_src)], axis=1)

    pm = pm_ref[...]
    pm = jnp.concatenate([pm, jnp.full((1, TILE - pm.shape[1]), 999, jnp.int32)], axis=1)
    pm_r = spread(pm)
    pm_c = pm_r.T
    earlier = jnp.where((pm_c == pm_r) & (sub < lane), 1, 0)
    place_c = spread(pm * cap + total(earlier)).T
    table[0:1, :] = total(jnp.where(place_c == lane, sub, 0))
    table[8:9, :] = total(jnp.where(pm_c == lane // cap, 1, 0))

    lane_row = lax.broadcasted_iota(jnp.int32, (1, TILE), 1)
    alive = jnp.zeros((1, TILE), jnp.int32)
    for c in range(n_src):
        alive = jnp.where(lane_row // slots == c, counts_ref[0, c], alive)
    rows_r = spread(flat(rows_ref))
    goes = total(jnp.where(rows_r == sub, place_c, 0))
    goes = jnp.where(lane_row % slots < alive, goes, 4096)
    goes_r = spread(goes)
    goes_c = goes_r.T
    rank_c = spread(total(jnp.where(goes_c * TILE + sub < goes_r * TILE + lane, 1, 0))).T
    pick = rank_c == lane
    source = (lane_row // slots) * HALF + flat(cols_ref)
    source_c = spread(source).T
    table[1:2, :] = total(jnp.where(pick, sub, 0))
    table[2:3, :] = total(jnp.where(pick, source_c, 0))
    mine = total(jnp.where(pick, goes_c, 0))
    before = total(jnp.where(rank_c + 1 == lane, goes_c, 0))
    table[3:4, :] = jnp.where((mine == before) & (lane_row % HALF != 0), 1, 0)
    upto = total(jnp.where(goes_c <= lane, 1, 0))
    below = total(jnp.where(goes_c < lane, 1, 0))
    left_end = jnp.minimum(upto, HALF)
    right_from = jnp.maximum(below, HALF)
    table[4:5, :] = jnp.maximum(left_end - 1, 0)
    table[5:6, :] = jnp.where(below < left_end, 1, 0)
    table[6:7, :] = jnp.maximum(upto - 1 - HALF, 0)
    table[7:8, :] = jnp.where(right_from < upto, 1, 0)


def layer_kernel(
    cap, slots, n_y, n_m, n_q, swap,
    feat_hbm, vals_hbm, rows_ref, cols_ref, counts_ref, ws_hbm, wn_hbm, bias_ref, pm_ref,
    out_v,
    feat, vals, own, mirror, blocks, mirrors, sums, more, f_in, f_out, f_recv, m_in, m_out, m_recv, pre,
    ws_ref, wn_ref, ws_t, wn_t, bias_t, table_v, table,
    feat_sem, vals_sem, ws_sem, wn_sem, table_sem, mir_sem,
    swap_send, swap_recv, sib_send, sib_recv, y_send, y_recv, fwd_send, fwd_recv,
    msib_send, msib_recv, my_send, my_recv, mfwd_send, mfwd_recv,
    fs_sem, fr_sem, fms_sem, fmr_sem, ms_sem, mr_sem, mms_sem, mmr_sem,
):
    here = lax.axis_index("blk")
    me = lax.axis_index("bal")
    tiles, width, _ = own.shape
    wide = width + swap
    stay = width - swap
    n_bal = f_recv.shape[1] // width
    half = n_bal // 2
    at_end = (me % half < half // 2) == (me // half == 0)
    base = me // half * half
    partner = (me + half) % n_bal
    sibling = here + 1 - 2 * (here % 2)
    across = (here + 2) % 4
    far = (sibling + 2) % 4
    y_tiles = tiles // n_y
    m_tiles = tiles // n_m
    q_tiles = cap // n_q
    own_rows = pl.ds(pl.multiple_of(me * width, width), width)
    mirror_rows = pl.ds(pl.multiple_of(partner * width + stay, 16), swap)

    def near(o):
        return base + (me + o) % half

    def other(o):
        return (base + half) % n_bal + (me + o) % half

    def each(first, last, body, unroll=1):
        def step(i, carry):
            body(i)
            return carry

        lax.fori_loop(first, last, step, 0, unroll=unroll)

    def remote(src, dst, send, recv, axis, peer):
        return pltpu.make_async_remote_copy(
            src, dst, send, recv, device_id={axis: peer}, device_id_type=MESH
        )

    barrier = pltpu.get_barrier_semaphore()
    for peer in (sibling, across):
        pl.semaphore_signal(barrier, inc=1, device_id={"blk": peer}, device_id_type=MESH)
    each(
        1, n_bal,
        lambda o: pl.semaphore_signal(
            barrier, inc=1, device_id={"bal": (me + o) % n_bal}, device_id_type=MESH
        ),
    )

    span_y = y_tiles * TILE

    def load_feat(i):
        part = pl.ds(pl.multiple_of(i * span_y, span_y), span_y)
        return pltpu.make_async_copy(feat_hbm.at[:, part], feat.at[:, part], feat_sem.at[i])

    each(0, n_y, lambda i: load_feat(i).start())
    load_vals = pltpu.make_async_copy(vals_hbm, vals, vals_sem)
    load_ws = pltpu.make_async_copy(ws_hbm, ws_ref, ws_sem)
    load_wn = pltpu.make_async_copy(wn_hbm, wn_ref, wn_sem)

    def pack(t):
        x = feat[:, pl.ds(pl.multiple_of(t * TILE, TILE), TILE)]
        own[t] = x
        blocks[here * tiles + t] = x

    def pack_part(i):
        load_feat(i).wait()
        each(0, y_tiles, lambda t: pack(i * y_tiles + t), 4)

    each(0, n_y, pack_part)
    pl.semaphore_wait(barrier, n_bal + 1)

    def swap_copy(i):
        span = pl.ds(i * m_tiles, m_tiles)
        return remote(
            own.at[span, pl.ds(stay, swap)], mirror.at[span],
            swap_send.at[i], swap_recv.at[i], "bal", partner,
        )

    def y_copy(i, whose):
        return remote(
            own.at[pl.ds(i * y_tiles, y_tiles)],
            blocks.at[pl.ds(whose * tiles + i * y_tiles, y_tiles)],
            y_send.at[i], y_recv.at[i], "blk", across,
        )

    def fwd_copy(i, whose):
        span = pl.ds(whose * tiles + i * y_tiles, y_tiles)
        part = blocks.at[span]
        return remote(part, part, fwd_send.at[i], fwd_recv.at[i], "blk", sibling)

    def sib_copy(whose):
        return remote(
            own, blocks.at[pl.ds(whose * tiles, tiles)],
            sib_send, sib_recv, "blk", sibling,
        )

    def my_copy(i, whose):
        return remote(
            mirror.at[pl.ds(i * m_tiles, m_tiles)],
            mirrors.at[pl.ds(whose * tiles + i * m_tiles, m_tiles)],
            my_send.at[i], my_recv.at[i], "blk", across,
        )

    def msib_copy(i, whose):
        return remote(
            mirror.at[pl.ds(i * m_tiles, m_tiles)],
            mirrors.at[pl.ds(whose * tiles + i * m_tiles, m_tiles)],
            msib_send.at[i], msib_recv.at[i], "blk", sibling,
        )

    def mfwd_copy(i, whose):
        span = pl.ds(whose * tiles + i * m_tiles, m_tiles)
        part = mirrors.at[span]
        return remote(part, part, mfwd_send.at[i], mfwd_recv.at[i], "blk", sibling)

    def f_near(o, whose):
        rows = pl.ds(pl.multiple_of(whose * width, width), width)
        return remote(
            f_in.at[o, :, pl.ds(0, width)], f_recv.at[:, rows],
            fs_sem.at[o], fr_sem.at[whose], "bal", near(o),
        )

    def f_near_mirror(o, whose):
        rows = pl.ds(pl.multiple_of((whose + half) % n_bal * width + stay, 16), swap)
        return remote(
            f_in.at[o, :, pl.ds(width, swap)], f_recv.at[:, rows],
            fms_sem.at[o], fmr_sem.at[whose], "bal", near(o),
        )

    def f_other(o, whose):
        rows = pl.ds(pl.multiple_of(whose * width, width), stay)
        return remote(
            f_out.at[o], f_recv.at[:, rows],
            fs_sem.at[half + o], fr_sem.at[whose], "bal", other(o),
        )

    def m_near(q, o, whose):
        span = pl.ds(q * q_tiles, q_tiles)
        rows = pl.ds(pl.multiple_of(whose * width, width), width)
        return remote(
            m_in.at[o, span, pl.ds(0, width)], m_recv.at[span, rows],
            ms_sem.at[q, o], mr_sem.at[q, whose], "bal", near(o),
        )

    def m_near_mirror(q, o, whose):
        span = pl.ds(q * q_tiles, q_tiles)
        rows = pl.ds(pl.multiple_of((whose + half) % n_bal * width + stay, 16), swap)
        return remote(
            m_in.at[o, span, pl.ds(width, swap)], m_recv.at[span, rows],
            mms_sem.at[q, o], mmr_sem.at[q, whose], "bal", near(o),
        )

    def m_other(q, o, whose):
        span = pl.ds(q * q_tiles, q_tiles)
        rows = pl.ds(pl.multiple_of(whose * width, width), stay)
        return remote(
            m_out.at[o, span], m_recv.at[span, rows],
            ms_sem.at[q, half + o], mr_sem.at[q, whose], "bal", other(o),
        )

    each(0, n_m, lambda i: swap_copy(i).start())
    each(0, n_y, lambda i: y_copy(i, here).start())
    sib_copy(here).start()

    load_vals.start()
    load_ws.start()
    load_wn.start()
    tables(pm_ref, rows_ref, cols_ref, counts_ref, table_v, slots, cap)
    load_table = pltpu.make_async_copy(table_v, table, table_sem)
    load_table.start()
    load_table.wait()

    def send_f_near(o):
        def gather(k):
            f_in[o, k, :width, :] = own[table[0, near(o) * cap + k]]

        each(0, cap, gather, 4)
        f_near(o, me).start()

    def fill_f_other(o):
        def gather(k):
            f_out[o, k] = own[table[0, other(o) * cap + k]][:stay]

        each(0, cap, gather, 4)

    def keep_f(k):
        f_recv[k, own_rows, :] = own[table[0, me * cap + k]]

    each(1, half, send_f_near)
    if stay:
        each(0, half, fill_f_other)
    each(0, cap, keep_f, 4)
    load_vals.wait()
    load_ws.wait()
    ws_t[...] = ws_ref[...].T
    load_wn.wait()
    wn_t[...] = wn_ref[...].T
    bias_t[...] = jnp.broadcast_to(bias_ref[...], (TILE, bias_ref.shape[1])).T

    def pass_on(i):
        y_copy(i, across).wait_recv()
        fwd_copy(i, across).start()

    def take_mirror(i):
        swap_copy(i).wait_recv()
        my_copy(i, here).start()
        msib_copy(i, here).start()

    each(0, n_y, pass_on)
    each(0, n_m - 1, take_mirror)

    def send_f_other():
        each(0, half, lambda o: f_other(o, me).start())

    if stay:
        send_f_other()
    sib_copy(sibling).wait_recv()
    each(0, n_y, lambda i: fwd_copy(i, far).wait_recv())

    in_top = lax.broadcasted_iota(jnp.int32, (16, 2 * TILE), 0) < 8
    in_left = lax.broadcasted_iota(jnp.int32, (16, 2 * TILE), 1) < TILE
    ones = jnp.where(in_top == in_left, 1.0, 0.0).astype(jnp.bfloat16)
    deg_left = lax.broadcasted_iota(jnp.int32, (16, TILE), 0) < 8

    def products(j, held, count, extra):
        zeros = jnp.zeros((count, TILE), jnp.bfloat16)
        a = jnp.concatenate([vals[table[1, j]], vals[table[1, j + HALF]]], axis=1)
        x = jnp.concatenate([held[table[2, j]], zeros], axis=1)
        y = jnp.concatenate([zeros, held[table[2, j + HALF]]], axis=1)
        lhs = jnp.concatenate([x, y] + extra, axis=0)
        return lax.dot_general(
            lhs, a, (((1,), (1,)), ((), ())), preferred_element_type=jnp.float32
        )

    def absorb(j, carry):
        left, right, deg = carry
        prod = products(j, blocks, width, [ones])
        keep_left, keep_right = table[3, j], table[3, j + HALF]
        left = jnp.where(keep_left > 0, left, 0.0) + prod[:width]
        right = jnp.where(keep_right > 0, right, 0.0) + prod[width : 2 * width]
        deg = jnp.where(jnp.where(deg_left, keep_left, keep_right) > 0, deg, 0.0)
        deg = deg + prod[2 * width :]
        sums[j, :width, :] = left
        sums[j, width : 2 * width, :] = right
        sums[j, 2 * width :, :] = deg
        return left, right, deg

    def absorb_mirror(j, carry):
        left, right = carry
        prod = products(j, mirrors, swap, [])
        left = jnp.where(table[3, j] > 0, left, 0.0) + prod[:swap]
        right = jnp.where(table[3, j + HALF] > 0, right, 0.0) + prod[swap:]
        more[j, :swap, :] = left
        more[j, swap:, :] = right
        return left, right

    empty = jnp.zeros((width, TILE), jnp.float32)
    lax.fori_loop(
        0, HALF, absorb, (empty, empty, jnp.zeros((16, TILE), jnp.float32)), unroll=2
    )

    each(n_m - 1, n_m, take_mirror)
    keep_mirror = pltpu.make_async_copy(
        mirror, mirrors.at[pl.ds(here * tiles, tiles)], mir_sem
    )
    keep_mirror.start()

    def send_f_mirror(o):
        def gather(k):
            f_in[o, k, width:, :] = mirror[table[0, near(o) * cap + k]]

        each(0, cap, gather, 4)
        f_near_mirror(o, me).start()

    def keep_f_mirror(k):
        f_recv[k, mirror_rows, :] = mirror[table[0, me * cap + k]]

    each(1, half, send_f_mirror)

    def inverse_degree(p):
        left, right = sums.at[table[4, p]], sums.at[table[6, p]]
        degree = (
            1.0
            + jnp.where(table[5, p] > 0, left[2 * width : 2 * width + 8, :], 0.0)
            + jnp.where(table[7, p] > 0, right[2 * width + 8 :, :], 0.0)
        )
        return (1.0 / degree)[:1]

    def mean_piece(p, inverse, where, count, right_row):
        left, right = where.at[table[4, p]], where.at[table[6, p]]
        agg = jnp.where(table[5, p] > 0, left[:count, :], 0.0) + jnp.where(
            table[7, p] > 0, right[right_row : right_row + count, :], 0.0
        )
        return (agg * inverse).astype(jnp.bfloat16)

    def send_m_other(q):
        def to_other(o):
            def fill(k):
                p = other(o) * cap + q * q_tiles + k
                m_out[o, q * q_tiles + k] = mean_piece(p, inverse_degree(p), sums, stay, width)

            each(0, q_tiles, fill, q_tiles)
            m_other(q, o, me).start()

        each(0, half, to_other)

    def send_m_near(q):
        def to_near(o):
            def fill(k):
                p = near(o) * cap + q * q_tiles + k
                m_in[o, q * q_tiles + k, :width, :] = mean_piece(
                    p, inverse_degree(p), sums, width, width
                )

            each(0, q_tiles, fill, q_tiles)
            m_near(q, o, me).start()

        each(1, half, to_near)

    def pass_mirror_on(i):
        my_copy(i, across).wait_recv()
        mfwd_copy(i, across).start()

    def send_all_m_other():
        each(0, n_q, send_m_other)

    if stay:
        pl.when(at_end)(send_all_m_other)
    each(0, n_m, pass_mirror_on)
    each(0, n_q, send_m_near)
    if stay:
        pl.when(jnp.logical_not(at_end))(send_all_m_other)
    each(0, n_m, lambda i: msib_copy(i, sibling).wait_recv())
    each(0, n_m, lambda i: mfwd_copy(i, far).wait_recv())
    keep_mirror.wait()
    lax.fori_loop(0, HALF, absorb_mirror, (empty[:swap], empty[:swap]), unroll=2)

    def send_m_mirror(q):
        def to_near(o):
            def fill(k):
                p = near(o) * cap + q * q_tiles + k
                m_in[o, q * q_tiles + k, width:, :] = mean_piece(
                    p, inverse_degree(p), more, swap, swap
                )

            each(0, q_tiles, fill, q_tiles)
            m_near_mirror(q, o, me).start()

        each(1, half, to_near)

    each(0, n_q, send_m_mirror)

    def keep_m(k):
        p = me * cap + k
        inverse = inverse_degree(p)
        m_recv[k, own_rows, :] = mean_piece(p, inverse, sums, width, width)
        m_recv[k, mirror_rows, :] = mean_piece(p, inverse, more, swap, swap)

    each(0, cap, keep_m, 4)
    each(0, cap, keep_f_mirror, 4)

    def wait_f_near(o):
        f_near(o, near(o)).wait_recv()
        f_near_mirror(o, near(o)).wait_recv()

    each(1, half, wait_f_near)
    if stay:
        each(0, half, lambda o: f_other(o, other(o)).wait_recv())

    rows = q_tiles * TILE

    def times(weight, recv, q):
        x = jnp.concatenate([recv[q * q_tiles + k] for k in range(q_tiles)], axis=1)
        return jnp.dot(weight[...], x, preferred_element_type=jnp.float32)

    def self_part(q):
        pre[q] = times(ws_t, f_recv, q) + jnp.concatenate([bias_t[...]] * q_tiles, axis=1)

    each(0, n_q, self_part)
    live = table[8, me * cap]

    def finish(q):
        def wait_near(o):
            m_near(q, o, near(o)).wait_recv()
            m_near_mirror(q, o, near(o)).wait_recv()

        each(1, half, wait_near)
        if stay:
            each(0, half, lambda o: m_other(q, o, other(o)).wait_recv())
        hidden = jnp.maximum(pre[q] + times(wn_t, m_recv, q), 0.0)
        row = q * rows + lax.broadcasted_iota(jnp.int32, (1, rows), 1)
        hidden = jnp.where(row < live * TILE, hidden, 0.0).astype(jnp.bfloat16)
        out_v[0, 0, pl.ds(pl.multiple_of(q * rows, rows), rows), :] = hidden.T

    each(0, n_q, finish)

    def settle_near(o):
        f_near(o, me).wait_send()
        f_near_mirror(o, me).wait_send()

        def one(q):
            m_near(q, o, me).wait_send()
            m_near_mirror(q, o, me).wait_send()

        each(0, n_q, one)

    def settle_other(o):
        f_other(o, me).wait_send()
        each(0, n_q, lambda q: m_other(q, o, me).wait_send())

    def settle_y(i):
        y_copy(i, here).wait_send()
        fwd_copy(i, across).wait_send()

    def settle_mirror(i):
        swap_copy(i).wait_send()
        my_copy(i, here).wait_send()
        msib_copy(i, here).wait_send()
        mfwd_copy(i, across).wait_send()

    each(1, half, settle_near)
    if stay:
        each(0, half, settle_other)
    each(0, n_y, settle_y)
    each(0, n_m, settle_mirror)
    sib_copy(here).wait_send()


def layer(
    features, tile_values, tile_rows, tile_cols, tile_counts, w_self, w_neigh, bias, part_map
):
    n_blk = lax.axis_size("blk")
    n_bal = lax.axis_size("bal")
    slots = tile_rows.shape[2]
    tiles = part_map.shape[1]
    cap = 2 * tiles // n_bal
    width = features.shape[1]
    total = w_self.shape[0]
    fits = (
        n_blk == 4 and n_blk * slots == TILE and tiles == HALF and width == HALF
        and n_bal * cap == TILE
    )
    if not fits:
        return on_device(
            features, tile_values, tile_rows, tile_cols, tile_counts, w_self, w_neigh, bias,
            part_map,
        )
    n_y, n_m, n_q = 4, 4, 4
    swap = 3 * width // 4
    wide, stay, half = width + swap, width - swap, n_bal // 2
    bf16, f32 = jnp.bfloat16, jnp.float32
    vmem = pl.BlockSpec(memory_space=pltpu.VMEM)
    smem = pl.BlockSpec(memory_space=pltpu.SMEM)
    hbm = pl.BlockSpec(memory_space=pl.ANY)
    dma = pltpu.SemaphoreType.DMA
    return pl.pallas_call(
        functools.partial(layer_kernel, cap, slots, n_y, n_m, n_q, swap),
        out_shape=pltpu.VMEM((1, 1, cap * TILE, total), bf16),
        in_specs=[hbm, hbm, vmem, vmem, smem, hbm, hbm, vmem, vmem],
        out_specs=vmem,
        scratch_shapes=[
            pltpu.VMEM((width, tiles * TILE), bf16),
            pltpu.VMEM((n_blk * slots, TILE, TILE), bf16),
            pltpu.VMEM((tiles, width, TILE), bf16),
            pltpu.VMEM((tiles, swap, TILE), bf16),
            pltpu.VMEM((n_blk * tiles, width, TILE), bf16),
            pltpu.VMEM((n_blk * tiles, swap, TILE), bf16),
            pltpu.VMEM((HALF, 2 * width + 16, TILE), f32),
            pltpu.VMEM((HALF, 2 * swap, TILE), f32),
            pltpu.VMEM((half, cap, wide, TILE), bf16),
            pltpu.VMEM((half, cap, max(stay, 16), TILE), bf16),
            pltpu.VMEM((cap, total, TILE), bf16),
            pltpu.VMEM((half, cap, wide, TILE), bf16),
            pltpu.VMEM((half, cap, max(stay, 16), TILE), bf16),
            pltpu.VMEM((cap, total, TILE), bf16),
            pltpu.VMEM((n_q, total, cap // n_q * TILE), f32),
            pltpu.VMEM((total, total), bf16),
            pltpu.VMEM((total, total), bf16),
            pltpu.VMEM((total, total), bf16),
            pltpu.VMEM((total, total), bf16),
            pltpu.VMEM((total, TILE), f32),
            pltpu.VMEM((16, TILE), jnp.int32),
            pltpu.SMEM((16, TILE), jnp.int32),
            dma((n_y,)), dma, dma, dma, dma, dma,
            dma((n_m,)), dma((n_m,)), dma, dma, dma((n_y,)), dma((n_y,)), dma((n_y,)), dma((n_y,)),
            dma((n_m,)), dma((n_m,)), dma((n_m,)), dma((n_m,)), dma((n_m,)), dma((n_m,)),
            dma((n_bal,)), dma((n_bal,)), dma((half,)), dma((n_bal,)),
            dma((n_q, n_bal)), dma((n_q, n_bal)), dma((n_q, half)), dma((n_q, n_bal)),
        ],
        compiler_params=pltpu.CompilerParams(
            collective_id=0, has_side_effects=True, vmem_limit_bytes=56 * 2**20
        ),
        cost_estimate=pl.CostEstimate(
            flops=4 * cap * TILE * total * total, bytes_accessed=12 * 2**20, transcendentals=0
        ),
    )(
        features.T,
        tile_values.reshape(n_blk * slots, TILE, TILE),
        tile_rows[0],
        tile_cols[0],
        tile_counts,
        w_self,
        w_neigh,
        bias.reshape(1, total),
        part_map,
    )


def solution(mesh):
    placed = (
        P("blk", "bal"),
        P("blk", None, None, None, None),
        P("blk", None, None),
        P("blk", None, None),
        P("blk", None),
        P(),
        P(),
        P(),
        P("blk", None),
    )
    return jax.shard_map(
        layer,
        mesh=mesh,
        in_specs=placed,
        out_specs=P("blk", "bal", None, None),
        check_vma=False,
    )
```

```python
import functools
import jax
import jax.numpy as jnp
from jax import lax
from jax.experimental import pallas as pl
from jax.experimental.pallas import tpu as pltpu
from jax.sharding import PartitionSpec as P

TILE = 128
HALF = 64
MESH = pl.DeviceIdType.MESH


def from_behind(block, axis, distance):
    devices = range(lax.axis_size(axis))
    route = [((i - distance) % len(devices), i) for i in devices]
    return lax.ppermute(block, axis, route)


def advance(block, steps_by):
    return from_behind(block, "blk", steps_by)


def on_device(
    features, tile_values, tile_rows, tile_cols, tile_counts, w_self, w_neigh, bias, part_map
):
    n_blk = lax.axis_size("blk")
    n_bal = lax.axis_size("bal")
    here = lax.axis_index("blk")
    column = lax.axis_index("bal")
    width = features.shape[1]
    tiles_per = part_map.shape[1]
    values = tile_values[0]
    rows_idx = tile_rows[0]
    cols_idx = tile_cols[0]
    counts = tile_counts[0]
    slots = values.shape[1]
    live = jnp.arange(slots)[None, :] < counts[:, None]
    row_hot = (
        (rows_idx[:, :, None] == jnp.arange(tiles_per)[None, None, :]) & live[:, :, None]
    ).astype(jnp.float32)
    row_mass = jnp.einsum(
        "csij,j->csi", values, jnp.ones((TILE,), jnp.bfloat16), preferred_element_type=jnp.float32
    )
    degree = 1.0 + jnp.einsum("cst,csi->ti", row_hot, row_mass, precision=lax.Precision.HIGHEST)

    def absorb(total, block, source):
        tiles = block.reshape(tiles_per, TILE, width)
        vals = lax.dynamic_index_in_dim(values, source, 0, keepdims=False)
        picks = lax.dynamic_index_in_dim(cols_idx, source, 0, keepdims=False)
        targets = lax.dynamic_index_in_dim(rows_idx, source, 0, keepdims=False)
        alive = lax.dynamic_index_in_dim(live, source, 0, keepdims=False)
        gathered = jnp.take(tiles, picks, axis=0)
        prod = jnp.einsum("sij,sjf->sif", vals, gathered, preferred_element_type=jnp.float32)
        masked = jnp.where(alive[:, None, None], prod, 0.0)
        return total.at[targets].add(masked)

    empty = jnp.zeros((tiles_per, TILE, width), jnp.float32)

    def step_one(index, carry):
        total, block = carry
        total = absorb(total, block, (here - index) % n_blk)
        block = advance(block, 1)
        return (total, block)

    total, block = lax.fori_loop(0, n_blk - 1, step_one, (empty, features))
    total = absorb(total, block, (here - (n_blk - 1)) % n_blk)
    mean_agg = (total / degree[:, :, None]).astype(jnp.bfloat16).reshape(tiles_per * TILE, width)
    capacity = 2 * tiles_per // n_bal
    mapping = part_map[0]
    dest_hot = (mapping[:, None] == jnp.arange(n_bal)[None, :]).astype(jnp.int32)
    ranks = jnp.cumsum(dest_hot, axis=0) - dest_hot
    place = mapping * capacity + jnp.sum(ranks * dest_hot, axis=1)
    select = (jnp.arange(n_bal * capacity)[:, None] == place[None, :]).astype(jnp.bfloat16)
    col_start = column * width
    zeros_out = jnp.zeros((tiles_per * TILE, width), jnp.float32)
    carry = zeros_out
    mean_piece = lax.all_gather(mean_agg, "bal", axis=1, tiled=True)
    feat_piece = lax.all_gather(features, "bal", axis=1, tiled=True)
    count = mean_piece.shape[1]
    neigh_part = lax.dynamic_slice(w_neigh, (0, col_start), (count, width))
    self_part = lax.dynamic_slice(w_self, (0, col_start), (count, width))
    carry = jnp.dot(mean_piece, neigh_part, preferred_element_type=jnp.float32)
    pre = carry + jnp.dot(feat_piece, self_part, preferred_element_type=jnp.float32)
    pre = pre + lax.dynamic_slice_in_dim(bias, col_start, width)
    hidden = jnp.maximum(pre, 0.0).astype(jnp.bfloat16)
    tiles = hidden.reshape(tiles_per, TILE, width)
    placed = jnp.einsum("kt,tif->kif", select, tiles, preferred_element_type=jnp.float32)
    result = lax.all_to_all(
        placed.astype(jnp.bfloat16).reshape(n_bal, capacity * TILE, width),
        "bal",
        split_axis=0,
        concat_axis=2,
        tiled=True,
    )
    return result[None]


def tables(pm_ref, rows_ref, cols_ref, counts_ref, table, slots, cap):
    n_src = rows_ref.shape[0]
    table[...] = jnp.zeros(table.shape, jnp.int32)
    square = (TILE, TILE)
    lane = lax.broadcasted_iota(jnp.int32, square, 1)
    sub = lax.broadcasted_iota(jnp.int32, square, 0)

    def spread(row):
        return jnp.broadcast_to(row, square)

    def total(x):
        return jnp.sum(x, axis=0, keepdims=True)

    def flat(ref):
        return jnp.concatenate([ref[c : c + 1, :] for c in range(n_src)], axis=1)

    pm = pm_ref[...]
    pm = jnp.concatenate([pm, jnp.full((1, TILE - pm.shape[1]), 999, jnp.int32)], axis=1)
    pm_r = spread(pm)
    pm_c = pm_r.T
    earlier = jnp.where((pm_c == pm_r) & (sub < lane), 1, 0)
    place_c = spread(pm * cap + total(earlier)).T
    table[0:1, :] = total(jnp.where(place_c == lane, sub, 0))
    table[8:9, :] = total(jnp.where(pm_c == lane // cap, 1, 0))

    lane_row = lax.broadcasted_iota(jnp.int32, (1, TILE), 1)
    alive = jnp.zeros((1, TILE), jnp.int32)
    for c in range(n_src):
        alive = jnp.where(lane_row // slots == c, counts_ref[0, c], alive)
    rows_r = spread(flat(rows_ref))
    goes = total(jnp.where(rows_r == sub, place_c, 0))
    goes = jnp.where(lane_row % slots < alive, goes, 4096)
    goes_r = spread(goes)
    goes_c = goes_r.T
    rank_c = spread(total(jnp.where(goes_c * TILE + sub < goes_r * TILE + lane, 1, 0))).T
    pick = rank_c == lane
    source = (lane_row // slots) * HALF + flat(cols_ref)
    source_c = spread(source).T
    table[1:2, :] = total(jnp.where(pick, sub, 0))
    table[2:3, :] = total(jnp.where(pick, source_c, 0))
    mine = total(jnp.where(pick, goes_c, 0))
    before = total(jnp.where(rank_c + 1 == lane, goes_c, 0))
    table[3:4, :] = jnp.where((mine == before) & (lane_row % HALF != 0), 1, 0)
    upto = total(jnp.where(goes_c <= lane, 1, 0))
    below = total(jnp.where(goes_c < lane, 1, 0))
    left_end = jnp.minimum(upto, HALF)
    right_from = jnp.maximum(below, HALF)
    table[4:5, :] = jnp.maximum(left_end - 1, 0)
    table[5:6, :] = jnp.where(below < left_end, 1, 0)
    table[6:7, :] = jnp.maximum(upto - 1 - HALF, 0)
    table[7:8, :] = jnp.where(right_from < upto, 1, 0)


def layer_kernel(
    cap, slots, n_y, n_m, n_q, swap,
    feat_hbm, vals_hbm, rows_ref, cols_ref, counts_ref, ws_hbm, wn_hbm, bias_ref, pm_ref,
    out_v,
    feat, vals, own, mirror, blocks, mirrors, sums, more, f_in, f_out, f_recv, m_in, m_out, m_recv, pre,
    ws_ref, wn_ref, ws_t, wn_t, bias_t, table_v, table,
    feat_sem, vals_sem, ws_sem, wn_sem, table_sem, mir_sem,
    swap_send, swap_recv, sib_send, sib_recv, y_send, y_recv, fwd_send, fwd_recv,
    msib_send, msib_recv, my_send, my_recv, mfwd_send, mfwd_recv,
    fs_sem, fr_sem, fms_sem, fmr_sem, ms_sem, mr_sem, mms_sem, mmr_sem,
):
    here = lax.axis_index("blk")
    me = lax.axis_index("bal")
    tiles, width, _ = own.shape
    wide = width + swap
    stay = width - swap
    n_bal = f_recv.shape[1] // width
    half = n_bal // 2
    at_end = (me % half < half // 2) == (me // half == 0)
    base = me // half * half
    partner = (me + half) % n_bal
    sibling = here + 1 - 2 * (here % 2)
    across = (here + 2) % 4
    far = (sibling + 2) % 4
    y_tiles = tiles // n_y
    m_tiles = tiles // n_m
    q_tiles = cap // n_q
    own_rows = pl.ds(pl.multiple_of(me * width, width), width)
    mirror_rows = pl.ds(pl.multiple_of(partner * width + stay, 16), swap)

    def near(o):
        return base + (me + o) % half

    def other(o):
        return (base + half) % n_bal + (me + o) % half

    def each(first, last, body, unroll=1):
        def step(i, carry):
            body(i)
            return carry

        lax.fori_loop(first, last, step, 0, unroll=unroll)

    def remote(src, dst, send, recv, axis, peer):
        return pltpu.make_async_remote_copy(
            src, dst, send, recv, device_id={axis: peer}, device_id_type=MESH
        )

    barrier = pltpu.get_barrier_semaphore()
    for peer in (sibling, across):
        pl.semaphore_signal(barrier, inc=1, device_id={"blk": peer}, device_id_type=MESH)
    each(
        1, n_bal,
        lambda o: pl.semaphore_signal(
            barrier, inc=1, device_id={"bal": (me + o) % n_bal}, device_id_type=MESH
        ),
    )

    span_y = y_tiles * TILE

    def load_feat(i):
        part = pl.ds(pl.multiple_of(i * span_y, span_y), span_y)
        return pltpu.make_async_copy(feat_hbm.at[:, part], feat.at[:, part], feat_sem.at[i])

    each(0, n_y, lambda i: load_feat(i).start())
    load_vals = pltpu.make_async_copy(vals_hbm, vals, vals_sem)
    load_ws = pltpu.make_async_copy(ws_hbm, ws_ref, ws_sem)
    load_wn = pltpu.make_async_copy(wn_hbm, wn_ref, wn_sem)

    def pack(t):
        x = feat[:, pl.ds(pl.multiple_of(t * TILE, TILE), TILE)]
        own[t] = x
        blocks[here * tiles + t] = x

    def pack_part(i):
        load_feat(i).wait()
        each(0, y_tiles, lambda t: pack(i * y_tiles + t), 4)

    tables(pm_ref, rows_ref, cols_ref, counts_ref, table_v, slots, cap)
    load_table = pltpu.make_async_copy(table_v, table, table_sem)
    load_table.start()
    each(0, n_y, pack_part)
    pl.semaphore_wait(barrier, n_bal + 1)

    def swap_copy(i):
        span = pl.ds(i * m_tiles, m_tiles)
        return remote(
            own.at[span, pl.ds(stay, swap)], mirror.at[span],
            swap_send.at[i], swap_recv.at[i], "bal", partner,
        )

    def y_copy(i, whose):
        return remote(
            own.at[pl.ds(i * y_tiles, y_tiles)],
            blocks.at[pl.ds(whose * tiles + i * y_tiles, y_tiles)],
            y_send.at[i], y_recv.at[i], "blk", across,
        )

    def fwd_copy(i, whose):
        span = pl.ds(whose * tiles + i * y_tiles, y_tiles)
        part = blocks.at[span]
        return remote(part, part, fwd_send.at[i], fwd_recv.at[i], "blk", sibling)

    def sib_copy(whose):
        return remote(
            own, blocks.at[pl.ds(whose * tiles, tiles)],
            sib_send, sib_recv, "blk", sibling,
        )

    def my_copy(i, whose):
        return remote(
            mirror.at[pl.ds(i * m_tiles, m_tiles)],
            mirrors.at[pl.ds(whose * tiles + i * m_tiles, m_tiles)],
            my_send.at[i], my_recv.at[i], "blk", across,
        )

    def msib_copy(i, whose):
        return remote(
            mirror.at[pl.ds(i * m_tiles, m_tiles)],
            mirrors.at[pl.ds(whose * tiles + i * m_tiles, m_tiles)],
            msib_send.at[i], msib_recv.at[i], "blk", sibling,
        )

    def mfwd_copy(i, whose):
        span = pl.ds(whose * tiles + i * m_tiles, m_tiles)
        part = mirrors.at[span]
        return remote(part, part, mfwd_send.at[i], mfwd_recv.at[i], "blk", sibling)

    def f_near(o, whose):
        rows = pl.ds(pl.multiple_of(whose * width, width), width)
        return remote(
            f_in.at[o, :, pl.ds(0, width)], f_recv.at[:, rows],
            fs_sem.at[o], fr_sem.at[whose], "bal", near(o),
        )

    def f_near_mirror(o, whose):
        rows = pl.ds(pl.multiple_of((whose + half) % n_bal * width + stay, 16), swap)
        return remote(
            f_in.at[o, :, pl.ds(width, swap)], f_recv.at[:, rows],
            fms_sem.at[o], fmr_sem.at[whose], "bal", near(o),
        )

    def f_other(o, whose):
        rows = pl.ds(pl.multiple_of(whose * width, width), stay)
        return remote(
            f_out.at[o], f_recv.at[:, rows],
            fs_sem.at[half + o], fr_sem.at[whose], "bal", other(o),
        )

    def m_near(q, o, whose):
        span = pl.ds(q * q_tiles, q_tiles)
        rows = pl.ds(pl.multiple_of(whose * width, width), width)
        return remote(
            m_in.at[o, span, pl.ds(0, width)], m_recv.at[span, rows],
            ms_sem.at[q, o], mr_sem.at[q, whose], "bal", near(o),
        )

    def m_near_mirror(q, o, whose):
        span = pl.ds(q * q_tiles, q_tiles)
        rows = pl.ds(pl.multiple_of((whose + half) % n_bal * width + stay, 16), swap)
        return remote(
            m_in.at[o, span, pl.ds(width, swap)], m_recv.at[span, rows],
            mms_sem.at[q, o], mmr_sem.at[q, whose], "bal", near(o),
        )

    def m_other(q, o, whose):
        span = pl.ds(q * q_tiles, q_tiles)
        rows = pl.ds(pl.multiple_of(whose * width, width), stay)
        return remote(
            m_out.at[o, span], m_recv.at[span, rows],
            ms_sem.at[q, half + o], mr_sem.at[q, whose], "bal", other(o),
        )

    each(0, n_m, lambda i: swap_copy(i).start())
    each(0, n_y, lambda i: y_copy(i, here).start())
    sib_copy(here).start()

    load_vals.start()
    load_ws.start()
    load_wn.start()
    load_table.wait()

    def send_f_near(o):
        def gather(k):
            f_in[o, k, :width, :] = own[table[0, near(o) * cap + k]]

        each(0, cap, gather, 4)
        f_near(o, me).start()

    def fill_f_other(o):
        def gather(k):
            f_out[o, k] = own[table[0, other(o) * cap + k]][:stay]

        each(0, cap, gather, 4)

    def keep_f(k):
        f_recv[k, own_rows, :] = own[table[0, me * cap + k]]

    each(1, half, send_f_near)
    if stay:
        each(0, half, fill_f_other)
    each(0, cap, keep_f, 4)
    load_vals.wait()
    load_ws.wait()
    ws_t[...] = ws_ref[...].T
    load_wn.wait()
    wn_t[...] = wn_ref[...].T
    bias_t[...] = jnp.broadcast_to(bias_ref[...], (TILE, bias_ref.shape[1])).T

    def pass_on(i):
        y_copy(i, across).wait_recv()
        fwd_copy(i, across).start()

    def take_mirror(i):
        swap_copy(i).wait_recv()
        my_copy(i, here).start()
        msib_copy(i, here).start()

    each(0, n_y, pass_on)
    each(0, n_m - 1, take_mirror)

    def send_f_other():
        each(0, half, lambda o: f_other(o, me).start())

    if stay:
        pl.when(at_end)(send_f_other)
    each(n_m - 1, n_m, take_mirror)
    keep_mirror = pltpu.make_async_copy(
        mirror, mirrors.at[pl.ds(here * tiles, tiles)], mir_sem
    )
    keep_mirror.start()

    def send_f_mirror(o):
        def gather(k):
            f_in[o, k, width:, :] = mirror[table[0, near(o) * cap + k]]

        each(0, cap, gather, 4)
        f_near_mirror(o, me).start()

    def keep_f_mirror(k):
        f_recv[k, mirror_rows, :] = mirror[table[0, me * cap + k]]

    each(1, half, send_f_mirror)
    if stay:
        pl.when(jnp.logical_not(at_end))(send_f_other)

    sib_copy(sibling).wait_recv()
    each(0, n_y, lambda i: fwd_copy(i, far).wait_recv())

    in_top = lax.broadcasted_iota(jnp.int32, (16, 2 * TILE), 0) < 8
    in_left = lax.broadcasted_iota(jnp.int32, (16, 2 * TILE), 1) < TILE
    ones = jnp.where(in_top == in_left, 1.0, 0.0).astype(jnp.bfloat16)
    deg_left = lax.broadcasted_iota(jnp.int32, (16, TILE), 0) < 8

    def products(j, held, count, extra):
        zeros = jnp.zeros((count, TILE), jnp.bfloat16)
        a = jnp.concatenate([vals[table[1, j]], vals[table[1, j + HALF]]], axis=1)
        x = jnp.concatenate([held[table[2, j]], zeros], axis=1)
        y = jnp.concatenate([zeros, held[table[2, j + HALF]]], axis=1)
        lhs = jnp.concatenate([x, y] + extra, axis=0)
        return lax.dot_general(
            lhs, a, (((1,), (1,)), ((), ())), preferred_element_type=jnp.float32
        )

    def absorb(j, carry):
        left, right, deg = carry
        prod = products(j, blocks, width, [ones])
        keep_left, keep_right = table[3, j], table[3, j + HALF]
        left = jnp.where(keep_left > 0, left, 0.0) + prod[:width]
        right = jnp.where(keep_right > 0, right, 0.0) + prod[width : 2 * width]
        deg = jnp.where(jnp.where(deg_left, keep_left, keep_right) > 0, deg, 0.0)
        deg = deg + prod[2 * width :]
        sums[j, :width, :] = left
        sums[j, width : 2 * width, :] = right
        sums[j, 2 * width :, :] = deg
        return left, right, deg

    def absorb_mirror(j, carry):
        left, right = carry
        prod = products(j, mirrors, swap, [])
        left = jnp.where(table[3, j] > 0, left, 0.0) + prod[:swap]
        right = jnp.where(table[3, j + HALF] > 0, right, 0.0) + prod[swap:]
        more[j, :swap, :] = left
        more[j, swap:, :] = right
        return left, right

    empty = jnp.zeros((width, TILE), jnp.float32)
    lax.fori_loop(
        0, HALF, absorb, (empty, empty, jnp.zeros((16, TILE), jnp.float32)), unroll=2
    )

    def inverse_degree(p):
        left, right = sums.at[table[4, p]], sums.at[table[6, p]]
        degree = (
            1.0
            + jnp.where(table[5, p] > 0, left[2 * width : 2 * width + 8, :], 0.0)
            + jnp.where(table[7, p] > 0, right[2 * width + 8 :, :], 0.0)
        )
        return (1.0 / degree)[:1]

    def mean_piece(p, inverse, where, count, right_row):
        left, right = where.at[table[4, p]], where.at[table[6, p]]
        agg = jnp.where(table[5, p] > 0, left[:count, :], 0.0) + jnp.where(
            table[7, p] > 0, right[right_row : right_row + count, :], 0.0
        )
        return (agg * inverse).astype(jnp.bfloat16)

    def send_m_other(q):
        def to_other(o):
            def fill(k):
                p = other(o) * cap + q * q_tiles + k
                m_out[o, q * q_tiles + k] = mean_piece(p, inverse_degree(p), sums, stay, width)

            each(0, q_tiles, fill, q_tiles)
            m_other(q, o, me).start()

        each(0, half, to_other)

    def send_m_near(q):
        def to_near(o):
            def fill(k):
                p = near(o) * cap + q * q_tiles + k
                m_in[o, q * q_tiles + k, :width, :] = mean_piece(
                    p, inverse_degree(p), sums, width, width
                )

            each(0, q_tiles, fill, q_tiles)
            m_near(q, o, me).start()

        each(1, half, to_near)

    def pass_mirror_on(i):
        my_copy(i, across).wait_recv()
        mfwd_copy(i, across).start()

    def send_all_m_other():
        each(0, n_q, send_m_other)

    if stay:
        pl.when(at_end)(send_all_m_other)
    each(0, n_m, pass_mirror_on)
    each(0, n_q, send_m_near)
    if stay:
        pl.when(jnp.logical_not(at_end))(send_all_m_other)
    each(0, n_m, lambda i: msib_copy(i, sibling).wait_recv())
    each(0, n_m, lambda i: mfwd_copy(i, far).wait_recv())
    keep_mirror.wait()
    lax.fori_loop(0, HALF, absorb_mirror, (empty[:swap], empty[:swap]), unroll=2)

    def send_m_mirror(q):
        def to_near(o):
            def fill(k):
                p = near(o) * cap + q * q_tiles + k
                m_in[o, q * q_tiles + k, width:, :] = mean_piece(
                    p, inverse_degree(p), more, swap, swap
                )

            each(0, q_tiles, fill, q_tiles)
            m_near_mirror(q, o, me).start()

        each(1, half, to_near)

    each(0, n_q, send_m_mirror)

    def keep_m(k):
        p = me * cap + k
        inverse = inverse_degree(p)
        m_recv[k, own_rows, :] = mean_piece(p, inverse, sums, width, width)
        m_recv[k, mirror_rows, :] = mean_piece(p, inverse, more, swap, swap)

    each(0, cap, keep_m, 4)
    each(0, cap, keep_f_mirror, 4)

    def wait_f_near(o):
        f_near(o, near(o)).wait_recv()
        f_near_mirror(o, near(o)).wait_recv()

    each(1, half, wait_f_near)
    if stay:
        each(0, half, lambda o: f_other(o, other(o)).wait_recv())

    rows = q_tiles * TILE

    def times(weight, recv, q):
        x = jnp.concatenate([recv[q * q_tiles + k] for k in range(q_tiles)], axis=1)
        return jnp.dot(weight[...], x, preferred_element_type=jnp.float32)

    def self_part(q):
        pre[q] = times(ws_t, f_recv, q) + jnp.concatenate([bias_t[...]] * q_tiles, axis=1)

    each(0, n_q, self_part)
    live = table[8, me * cap]

    def finish(q):
        def wait_near(o):
            m_near(q, o, near(o)).wait_recv()
            m_near_mirror(q, o, near(o)).wait_recv()

        each(1, half, wait_near)
        if stay:
            each(0, half, lambda o: m_other(q, o, other(o)).wait_recv())
        hidden = jnp.maximum(pre[q] + times(wn_t, m_recv, q), 0.0)
        row = q * rows + lax.broadcasted_iota(jnp.int32, (1, rows), 1)
        hidden = jnp.where(row < live * TILE, hidden, 0.0).astype(jnp.bfloat16)
        out_v[0, 0, pl.ds(pl.multiple_of(q * rows, rows), rows), :] = hidden.T

    each(0, n_q, finish)

    def settle_near(o):
        f_near(o, me).wait_send()
        f_near_mirror(o, me).wait_send()

        def one(q):
            m_near(q, o, me).wait_send()
            m_near_mirror(q, o, me).wait_send()

        each(0, n_q, one)

    def settle_other(o):
        f_other(o, me).wait_send()
        each(0, n_q, lambda q: m_other(q, o, me).wait_send())

    def settle_y(i):
        y_copy(i, here).wait_send()
        fwd_copy(i, across).wait_send()

    def settle_mirror(i):
        swap_copy(i).wait_send()
        my_copy(i, here).wait_send()
        msib_copy(i, here).wait_send()
        mfwd_copy(i, across).wait_send()

    each(1, half, settle_near)
    if stay:
        each(0, half, settle_other)
    each(0, n_y, settle_y)
    each(0, n_m, settle_mirror)
    sib_copy(here).wait_send()


def layer(
    features, tile_values, tile_rows, tile_cols, tile_counts, w_self, w_neigh, bias, part_map
):
    n_blk = lax.axis_size("blk")
    n_bal = lax.axis_size("bal")
    slots = tile_rows.shape[2]
    tiles = part_map.shape[1]
    cap = 2 * tiles // n_bal
    width = features.shape[1]
    total = w_self.shape[0]
    fits = (
        n_blk == 4 and n_blk * slots == TILE and tiles == HALF and width == HALF
        and n_bal * cap == TILE
    )
    if not fits:
        return on_device(
            features, tile_values, tile_rows, tile_cols, tile_counts, w_self, w_neigh, bias,
            part_map,
        )
    n_y, n_m, n_q = 4, 4, 4
    swap = width // 2
    wide, stay, half = width + swap, width - swap, n_bal // 2
    bf16, f32 = jnp.bfloat16, jnp.float32
    vmem = pl.BlockSpec(memory_space=pltpu.VMEM)
    smem = pl.BlockSpec(memory_space=pltpu.SMEM)
    hbm = pl.BlockSpec(memory_space=pl.ANY)
    dma = pltpu.SemaphoreType.DMA
    return pl.pallas_call(
        functools.partial(layer_kernel, cap, slots, n_y, n_m, n_q, swap),
        out_shape=pltpu.VMEM((1, 1, cap * TILE, total), bf16),
        in_specs=[hbm, hbm, vmem, vmem, smem, hbm, hbm, vmem, vmem],
        out_specs=vmem,
        scratch_shapes=[
            pltpu.VMEM((width, tiles * TILE), bf16),
            pltpu.VMEM((n_blk * slots, TILE, TILE), bf16),
            pltpu.VMEM((tiles, width, TILE), bf16),
            pltpu.VMEM((tiles, swap, TILE), bf16),
            pltpu.VMEM((n_blk * tiles, width, TILE), bf16),
            pltpu.VMEM((n_blk * tiles, swap, TILE), bf16),
            pltpu.VMEM((HALF, 2 * width + 16, TILE), f32),
            pltpu.VMEM((HALF, 2 * swap, TILE), f32),
            pltpu.VMEM((half, cap, wide, TILE), bf16),
            pltpu.VMEM((half, cap, max(stay, 16), TILE), bf16),
            pltpu.VMEM((cap, total, TILE), bf16),
            pltpu.VMEM((half, cap, wide, TILE), bf16),
            pltpu.VMEM((half, cap, max(stay, 16), TILE), bf16),
            pltpu.VMEM((cap, total, TILE), bf16),
            pltpu.VMEM((n_q, total, cap // n_q * TILE), f32),
            pltpu.VMEM((total, total), bf16),
            pltpu.VMEM((total, total), bf16),
            pltpu.VMEM((total, total), bf16),
            pltpu.VMEM((total, total), bf16),
            pltpu.VMEM((total, TILE), f32),
            pltpu.VMEM((16, TILE), jnp.int32),
            pltpu.SMEM((16, TILE), jnp.int32),
            dma((n_y,)), dma, dma, dma, dma, dma,
            dma((n_m,)), dma((n_m,)), dma, dma, dma((n_y,)), dma((n_y,)), dma((n_y,)), dma((n_y,)),
            dma((n_m,)), dma((n_m,)), dma((n_m,)), dma((n_m,)), dma((n_m,)), dma((n_m,)),
            dma((n_bal,)), dma((n_bal,)), dma((half,)), dma((n_bal,)),
            dma((n_q, n_bal)), dma((n_q, n_bal)), dma((n_q, half)), dma((n_q, n_bal)),
        ],
        compiler_params=pltpu.CompilerParams(
            collective_id=0, has_side_effects=True, vmem_limit_bytes=56 * 2**20
        ),
        cost_estimate=pl.CostEstimate(
            flops=4 * cap * TILE * total * total, bytes_accessed=12 * 2**20, transcendentals=0
        ),
    )(
        features.T,
        tile_values.reshape(n_blk * slots, TILE, TILE),
        tile_rows[0],
        tile_cols[0],
        tile_counts,
        w_self,
        w_neigh,
        bias.reshape(1, total),
        part_map,
    )


def solution(mesh):
    placed = (
        P("blk", "bal"),
        P("blk", None, None, None, None),
        P("blk", None, None),
        P("blk", None, None),
        P("blk", None),
        P(),
        P(),
        P(),
        P("blk", None),
    )
    return jax.shard_map(
        layer,
        mesh=mesh,
        in_specs=placed,
        out_specs=P("blk", "bal", None, None),
        check_vma=False,
    )
```

```python
import functools
import jax
import jax.numpy as jnp
from jax import lax
from jax.experimental import pallas as pl
from jax.experimental.pallas import tpu as pltpu
from jax.sharding import PartitionSpec as P

TILE = 128
HALF = 64
MESH = pl.DeviceIdType.MESH


def from_behind(block, axis, distance):
    devices = range(lax.axis_size(axis))
    route = [((i - distance) % len(devices), i) for i in devices]
    return lax.ppermute(block, axis, route)


def advance(block, steps_by):
    return from_behind(block, "blk", steps_by)


def on_device(
    features, tile_values, tile_rows, tile_cols, tile_counts, w_self, w_neigh, bias, part_map
):
    n_blk = lax.axis_size("blk")
    n_bal = lax.axis_size("bal")
    here = lax.axis_index("blk")
    column = lax.axis_index("bal")
    width = features.shape[1]
    tiles_per = part_map.shape[1]
    values = tile_values[0]
    rows_idx = tile_rows[0]
    cols_idx = tile_cols[0]
    counts = tile_counts[0]
    slots = values.shape[1]
    live = jnp.arange(slots)[None, :] < counts[:, None]
    row_hot = (
        (rows_idx[:, :, None] == jnp.arange(tiles_per)[None, None, :]) & live[:, :, None]
    ).astype(jnp.float32)
    row_mass = jnp.einsum(
        "csij,j->csi", values, jnp.ones((TILE,), jnp.bfloat16), preferred_element_type=jnp.float32
    )
    degree = 1.0 + jnp.einsum("cst,csi->ti", row_hot, row_mass, precision=lax.Precision.HIGHEST)

    def absorb(total, block, source):
        tiles = block.reshape(tiles_per, TILE, width)
        vals = lax.dynamic_index_in_dim(values, source, 0, keepdims=False)
        picks = lax.dynamic_index_in_dim(cols_idx, source, 0, keepdims=False)
        targets = lax.dynamic_index_in_dim(rows_idx, source, 0, keepdims=False)
        alive = lax.dynamic_index_in_dim(live, source, 0, keepdims=False)
        gathered = jnp.take(tiles, picks, axis=0)
        prod = jnp.einsum("sij,sjf->sif", vals, gathered, preferred_element_type=jnp.float32)
        masked = jnp.where(alive[:, None, None], prod, 0.0)
        return total.at[targets].add(masked)

    empty = jnp.zeros((tiles_per, TILE, width), jnp.float32)

    def step_one(index, carry):
        total, block = carry
        total = absorb(total, block, (here - index) % n_blk)
        block = advance(block, 1)
        return (total, block)

    total, block = lax.fori_loop(0, n_blk - 1, step_one, (empty, features))
    total = absorb(total, block, (here - (n_blk - 1)) % n_blk)
    mean_agg = (total / degree[:, :, None]).astype(jnp.bfloat16).reshape(tiles_per * TILE, width)
    capacity = 2 * tiles_per // n_bal
    mapping = part_map[0]
    dest_hot = (mapping[:, None] == jnp.arange(n_bal)[None, :]).astype(jnp.int32)
    ranks = jnp.cumsum(dest_hot, axis=0) - dest_hot
    place = mapping * capacity + jnp.sum(ranks * dest_hot, axis=1)
    select = (jnp.arange(n_bal * capacity)[:, None] == place[None, :]).astype(jnp.bfloat16)
    col_start = column * width
    zeros_out = jnp.zeros((tiles_per * TILE, width), jnp.float32)
    carry = zeros_out
    mean_piece = lax.all_gather(mean_agg, "bal", axis=1, tiled=True)
    feat_piece = lax.all_gather(features, "bal", axis=1, tiled=True)
    count = mean_piece.shape[1]
    neigh_part = lax.dynamic_slice(w_neigh, (0, col_start), (count, width))
    self_part = lax.dynamic_slice(w_self, (0, col_start), (count, width))
    carry = jnp.dot(mean_piece, neigh_part, preferred_element_type=jnp.float32)
    pre = carry + jnp.dot(feat_piece, self_part, preferred_element_type=jnp.float32)
    pre = pre + lax.dynamic_slice_in_dim(bias, col_start, width)
    hidden = jnp.maximum(pre, 0.0).astype(jnp.bfloat16)
    tiles = hidden.reshape(tiles_per, TILE, width)
    placed = jnp.einsum("kt,tif->kif", select, tiles, preferred_element_type=jnp.float32)
    result = lax.all_to_all(
        placed.astype(jnp.bfloat16).reshape(n_bal, capacity * TILE, width),
        "bal",
        split_axis=0,
        concat_axis=2,
        tiled=True,
    )
    return result[None]


def tables(pm_ref, rows_ref, cols_ref, counts_ref, table, slots, cap):
    n_src = rows_ref.shape[0]
    table[...] = jnp.zeros(table.shape, jnp.int32)
    square = (TILE, TILE)
    lane = lax.broadcasted_iota(jnp.int32, square, 1)
    sub = lax.broadcasted_iota(jnp.int32, square, 0)

    def spread(row):
        return jnp.broadcast_to(row, square)

    def total(x):
        return jnp.sum(x, axis=0, keepdims=True)

    def flat(ref):
        return jnp.concatenate([ref[c : c + 1, :] for c in range(n_src)], axis=1)

    pm = pm_ref[...]
    pm = jnp.concatenate([pm, jnp.full((1, TILE - pm.shape[1]), 999, jnp.int32)], axis=1)
    pm_r = spread(pm)
    pm_c = pm_r.T
    earlier = jnp.where((pm_c == pm_r) & (sub < lane), 1, 0)
    place_c = spread(pm * cap + total(earlier)).T
    table[0:1, :] = total(jnp.where(place_c == lane, sub, 0))
    table[8:9, :] = total(jnp.where(pm_c == lane // cap, 1, 0))

    lane_row = lax.broadcasted_iota(jnp.int32, (1, TILE), 1)
    alive = jnp.zeros((1, TILE), jnp.int32)
    for c in range(n_src):
        alive = jnp.where(lane_row // slots == c, counts_ref[0, c], alive)
    rows_r = spread(flat(rows_ref))
    goes = total(jnp.where(rows_r == sub, place_c, 0))
    goes = jnp.where(lane_row % slots < alive, goes, 4096)
    goes_r = spread(goes)
    goes_c = goes_r.T
    rank_c = spread(total(jnp.where(goes_c * TILE + sub < goes_r * TILE + lane, 1, 0))).T
    pick = rank_c == lane
    source = (lane_row // slots) * HALF + flat(cols_ref)
    source_c = spread(source).T
    table[1:2, :] = total(jnp.where(pick, sub, 0))
    table[2:3, :] = total(jnp.where(pick, source_c, 0))
    mine = total(jnp.where(pick, goes_c, 0))
    before = total(jnp.where(rank_c + 1 == lane, goes_c, 0))
    table[3:4, :] = jnp.where((mine == before) & (lane_row % HALF != 0), 1, 0)
    upto = total(jnp.where(goes_c <= lane, 1, 0))
    below = total(jnp.where(goes_c < lane, 1, 0))
    left_end = jnp.minimum(upto, HALF)
    right_from = jnp.maximum(below, HALF)
    table[4:5, :] = jnp.maximum(left_end - 1, 0)
    table[5:6, :] = jnp.where(below < left_end, 1, 0)
    table[6:7, :] = jnp.maximum(upto - 1 - HALF, 0)
    table[7:8, :] = jnp.where(right_from < upto, 1, 0)


def layer_kernel(
    cap, slots, n_y, n_m, n_q, swap,
    feat_hbm, vals_hbm, rows_ref, cols_ref, counts_ref, ws_hbm, wn_hbm, bias_ref, pm_ref,
    out_v,
    feat, vals, turned, own, mirror, blocks, mirrors, sums, more, f_in, f_out, f_recv, m_in, m_out, m_recv, pre,
    ws_ref, wn_ref, ws_t, wn_t, bias_t, table_v, table,
    feat_sem, vals_sem, ws_sem, wn_sem, table_sem, mir_sem,
    swap_send, swap_recv, sib_send, sib_recv, y_send, y_recv, fwd_send, fwd_recv,
    msib_send, msib_recv, my_send, my_recv, mfwd_send, mfwd_recv,
    fs_sem, fr_sem, fms_sem, fmr_sem, ms_sem, mr_sem, mms_sem, mmr_sem,
):
    here = lax.axis_index("blk")
    me = lax.axis_index("bal")
    tiles, width, _ = own.shape
    wide = width + swap
    stay = width - swap
    n_bal = f_recv.shape[1] // width
    half = n_bal // 2
    at_end = (me % half < half // 2) == (me // half == 0)
    base = me // half * half
    partner = (me + half) % n_bal
    sibling = here + 1 - 2 * (here % 2)
    across = (here + 2) % 4
    far = (sibling + 2) % 4
    y_tiles = tiles // n_y
    m_tiles = tiles // n_m
    q_tiles = cap // n_q
    own_rows = pl.ds(pl.multiple_of(me * width, width), width)
    mirror_rows = pl.ds(pl.multiple_of(partner * width + stay, 16), swap)

    def near(o):
        return base + (me + o) % half

    def other(o):
        return (base + half) % n_bal + (me + o) % half

    def each(first, last, body, unroll=1):
        def step(i, carry):
            body(i)
            return carry

        lax.fori_loop(first, last, step, 0, unroll=unroll)

    def remote(src, dst, send, recv, axis, peer):
        return pltpu.make_async_remote_copy(
            src, dst, send, recv, device_id={axis: peer}, device_id_type=MESH
        )

    barrier = pltpu.get_barrier_semaphore()
    for peer in (sibling, across):
        pl.semaphore_signal(barrier, inc=1, device_id={"blk": peer}, device_id_type=MESH)
    each(
        1, n_bal,
        lambda o: pl.semaphore_signal(
            barrier, inc=1, device_id={"bal": (me + o) % n_bal}, device_id_type=MESH
        ),
    )

    span_y = y_tiles * TILE

    def load_feat(i):
        part = pl.ds(pl.multiple_of(i * span_y, span_y), span_y)
        return pltpu.make_async_copy(feat_hbm.at[:, part], feat.at[:, part], feat_sem.at[i])

    each(0, n_y, lambda i: load_feat(i).start())
    load_vals = pltpu.make_async_copy(vals_hbm, vals, vals_sem)
    load_ws = pltpu.make_async_copy(ws_hbm, ws_ref, ws_sem)
    load_wn = pltpu.make_async_copy(wn_hbm, wn_ref, wn_sem)

    def pack(t):
        x = feat[:, pl.ds(pl.multiple_of(t * TILE, TILE), TILE)]
        own[t] = x
        blocks[here * tiles + t] = x

    def pack_part(i):
        load_feat(i).wait()
        each(0, y_tiles, lambda t: pack(i * y_tiles + t), 4)

    tables(pm_ref, rows_ref, cols_ref, counts_ref, table_v, slots, cap)
    load_table = pltpu.make_async_copy(table_v, table, table_sem)
    load_table.start()
    each(0, n_y, pack_part)
    pl.semaphore_wait(barrier, n_bal + 1)

    def swap_copy(i):
        span = pl.ds(i * m_tiles, m_tiles)
        return remote(
            own.at[span, pl.ds(stay, swap)], mirror.at[span],
            swap_send.at[i], swap_recv.at[i], "bal", partner,
        )

    def y_copy(i, whose):
        return remote(
            own.at[pl.ds(i * y_tiles, y_tiles)],
            blocks.at[pl.ds(whose * tiles + i * y_tiles, y_tiles)],
            y_send.at[i], y_recv.at[i], "blk", across,
        )

    def fwd_copy(i, whose):
        span = pl.ds(whose * tiles + i * y_tiles, y_tiles)
        part = blocks.at[span]
        return remote(part, part, fwd_send.at[i], fwd_recv.at[i], "blk", sibling)

    def sib_copy(whose):
        return remote(
            own, blocks.at[pl.ds(whose * tiles, tiles)],
            sib_send, sib_recv, "blk", sibling,
        )

    def my_copy(i, whose):
        return remote(
            mirror.at[pl.ds(i * m_tiles, m_tiles)],
            mirrors.at[pl.ds(whose * tiles + i * m_tiles, m_tiles)],
            my_send.at[i], my_recv.at[i], "blk", across,
        )

    def msib_copy(i, whose):
        return remote(
            mirror.at[pl.ds(i * m_tiles, m_tiles)],
            mirrors.at[pl.ds(whose * tiles + i * m_tiles, m_tiles)],
            msib_send.at[i], msib_recv.at[i], "blk", sibling,
        )

    def mfwd_copy(i, whose):
        span = pl.ds(whose * tiles + i * m_tiles, m_tiles)
        part = mirrors.at[span]
        return remote(part, part, mfwd_send.at[i], mfwd_recv.at[i], "blk", sibling)

    def f_near(o, whose):
        rows = pl.ds(pl.multiple_of(whose * width, width), width)
        return remote(
            f_in.at[o, :, pl.ds(0, width)], f_recv.at[:, rows],
            fs_sem.at[o], fr_sem.at[whose], "bal", near(o),
        )

    def f_near_mirror(o, whose):
        rows = pl.ds(pl.multiple_of((whose + half) % n_bal * width + stay, 16), swap)
        return remote(
            f_in.at[o, :, pl.ds(width, swap)], f_recv.at[:, rows],
            fms_sem.at[o], fmr_sem.at[whose], "bal", near(o),
        )

    def f_other(o, whose):
        rows = pl.ds(pl.multiple_of(whose * width, width), stay)
        return remote(
            f_out.at[o], f_recv.at[:, rows],
            fs_sem.at[half + o], fr_sem.at[whose], "bal", other(o),
        )

    def m_near(q, o, whose):
        span = pl.ds(q * q_tiles, q_tiles)
        rows = pl.ds(pl.multiple_of(whose * width, width), width)
        return remote(
            m_in.at[o, span, pl.ds(0, width)], m_recv.at[span, rows],
            ms_sem.at[q, o], mr_sem.at[q, whose], "bal", near(o),
        )

    def m_near_mirror(q, o, whose):
        span = pl.ds(q * q_tiles, q_tiles)
        rows = pl.ds(pl.multiple_of((whose + half) % n_bal * width + stay, 16), swap)
        return remote(
            m_in.at[o, span, pl.ds(width, swap)], m_recv.at[span, rows],
            mms_sem.at[q, o], mmr_sem.at[q, whose], "bal", near(o),
        )

    def m_other(q, o, whose):
        span = pl.ds(q * q_tiles, q_tiles)
        rows = pl.ds(pl.multiple_of(whose * width, width), stay)
        return remote(
            m_out.at[o, span], m_recv.at[span, rows],
            ms_sem.at[q, half + o], mr_sem.at[q, whose], "bal", other(o),
        )

    each(0, n_m, lambda i: swap_copy(i).start())
    each(0, n_y, lambda i: y_copy(i, here).start())
    sib_copy(here).start()

    load_vals.start()
    load_ws.start()
    load_wn.start()
    load_table.wait()

    def send_f_near(o):
        def gather(k):
            f_in[o, k, :width, :] = own[table[0, near(o) * cap + k]]

        each(0, cap, gather, 4)
        f_near(o, me).start()

    def fill_f_other(o):
        def gather(k):
            f_out[o, k] = own[table[0, other(o) * cap + k]][:stay]

        each(0, cap, gather, 4)

    def keep_f(k):
        f_recv[k, own_rows, :] = own[table[0, me * cap + k]]

    each(1, half, send_f_near)
    if stay:
        each(0, half, fill_f_other)
    each(0, cap, keep_f, 4)
    load_vals.wait()
    load_ws.wait()
    ws_t[...] = ws_ref[...].T
    load_wn.wait()
    wn_t[...] = wn_ref[...].T

    def turn(j):
        turned[j, :TILE, :] = vals[table[1, j]].T
        turned[j, TILE:, :] = vals[table[1, j + HALF]].T

    each(0, HALF, turn, 2)
    bias_t[...] = jnp.broadcast_to(bias_ref[...], (TILE, bias_ref.shape[1])).T

    def pass_on(i):
        y_copy(i, across).wait_recv()
        fwd_copy(i, across).start()

    def take_mirror(i):
        swap_copy(i).wait_recv()
        my_copy(i, here).start()
        msib_copy(i, here).start()

    each(0, n_y, pass_on)
    each(0, n_m - 1, take_mirror)

    def send_f_other():
        each(0, half, lambda o: f_other(o, me).start())

    if stay:
        pl.when(at_end)(send_f_other)
    each(n_m - 1, n_m, take_mirror)
    keep_mirror = pltpu.make_async_copy(
        mirror, mirrors.at[pl.ds(here * tiles, tiles)], mir_sem
    )
    keep_mirror.start()

    def send_f_mirror(o):
        def gather(k):
            f_in[o, k, width:, :] = mirror[table[0, near(o) * cap + k]]

        each(0, cap, gather, 4)
        f_near_mirror(o, me).start()

    def keep_f_mirror(k):
        f_recv[k, mirror_rows, :] = mirror[table[0, me * cap + k]]

    each(1, half, send_f_mirror)
    if stay:
        pl.when(jnp.logical_not(at_end))(send_f_other)

    sib_copy(sibling).wait_recv()
    each(0, n_y, lambda i: fwd_copy(i, far).wait_recv())

    in_top = lax.broadcasted_iota(jnp.int32, (16, 2 * TILE), 0) < 8
    in_left = lax.broadcasted_iota(jnp.int32, (16, 2 * TILE), 1) < TILE
    ones = jnp.where(in_top == in_left, 1.0, 0.0).astype(jnp.bfloat16)
    deg_left = lax.broadcasted_iota(jnp.int32, (16, TILE), 0) < 8

    def products(j, held, count, extra):
        zeros = jnp.zeros((count, TILE), jnp.bfloat16)
        x = jnp.concatenate([held[table[2, j]], zeros], axis=1)
        y = jnp.concatenate([zeros, held[table[2, j + HALF]]], axis=1)
        lhs = jnp.concatenate([x, y] + extra, axis=0)
        return jnp.dot(lhs, turned[j], preferred_element_type=jnp.float32)

    def absorb(j, carry):
        left, right, deg = carry
        prod = products(j, blocks, width, [ones])
        keep_left, keep_right = table[3, j], table[3, j + HALF]
        left = jnp.where(keep_left > 0, left, 0.0) + prod[:width]
        right = jnp.where(keep_right > 0, right, 0.0) + prod[width : 2 * width]
        deg = jnp.where(jnp.where(deg_left, keep_left, keep_right) > 0, deg, 0.0)
        deg = deg + prod[2 * width :]
        sums[j, :width, :] = left
        sums[j, width : 2 * width, :] = right
        sums[j, 2 * width :, :] = deg
        return left, right, deg

    def absorb_mirror(j, carry):
        left, right = carry
        prod = products(j, mirrors, swap, [])
        left = jnp.where(table[3, j] > 0, left, 0.0) + prod[:swap]
        right = jnp.where(table[3, j + HALF] > 0, right, 0.0) + prod[swap:]
        more[j, :swap, :] = left
        more[j, swap:, :] = right
        return left, right

    empty = jnp.zeros((width, TILE), jnp.float32)
    lax.fori_loop(
        0, HALF, absorb, (empty, empty, jnp.zeros((16, TILE), jnp.float32)), unroll=2
    )

    def inverse_degree(p):
        left, right = sums.at[table[4, p]], sums.at[table[6, p]]
        degree = (
            1.0
            + jnp.where(table[5, p] > 0, left[2 * width : 2 * width + 8, :], 0.0)
            + jnp.where(table[7, p] > 0, right[2 * width + 8 :, :], 0.0)
        )
        return (1.0 / degree)[:1]

    def mean_piece(p, inverse, where, count, right_row):
        left, right = where.at[table[4, p]], where.at[table[6, p]]
        agg = jnp.where(table[5, p] > 0, left[:count, :], 0.0) + jnp.where(
            table[7, p] > 0, right[right_row : right_row + count, :], 0.0
        )
        return (agg * inverse).astype(jnp.bfloat16)

    def send_m_other(q):
        def to_other(o):
            def fill(k):
                p = other(o) * cap + q * q_tiles + k
                m_out[o, q * q_tiles + k] = mean_piece(p, inverse_degree(p), sums, stay, width)

            each(0, q_tiles, fill, q_tiles)
            m_other(q, o, me).start()

        each(0, half, to_other)

    def send_m_near(q):
        def to_near(o):
            def fill(k):
                p = near(o) * cap + q * q_tiles + k
                m_in[o, q * q_tiles + k, :width, :] = mean_piece(
                    p, inverse_degree(p), sums, width, width
                )

            each(0, q_tiles, fill, q_tiles)
            m_near(q, o, me).start()

        each(1, half, to_near)

    def pass_mirror_on(i):
        my_copy(i, across).wait_recv()
        mfwd_copy(i, across).start()

    def send_all_m_other():
        each(0, n_q, send_m_other)

    if stay:
        pl.when(at_end)(send_all_m_other)
    each(0, n_m, pass_mirror_on)
    each(0, n_q, send_m_near)
    if stay:
        pl.when(jnp.logical_not(at_end))(send_all_m_other)
    each(0, n_m, lambda i: msib_copy(i, sibling).wait_recv())
    each(0, n_m, lambda i: mfwd_copy(i, far).wait_recv())
    keep_mirror.wait()
    lax.fori_loop(0, HALF, absorb_mirror, (empty[:swap], empty[:swap]), unroll=2)

    def send_m_mirror(q):
        def to_near(o):
            def fill(k):
                p = near(o) * cap + q * q_tiles + k
                m_in[o, q * q_tiles + k, width:, :] = mean_piece(
                    p, inverse_degree(p), more, swap, swap
                )

            each(0, q_tiles, fill, q_tiles)
            m_near_mirror(q, o, me).start()

        each(1, half, to_near)

    each(0, n_q, send_m_mirror)

    def keep_m(k):
        p = me * cap + k
        inverse = inverse_degree(p)
        m_recv[k, own_rows, :] = mean_piece(p, inverse, sums, width, width)
        m_recv[k, mirror_rows, :] = mean_piece(p, inverse, more, swap, swap)

    each(0, cap, keep_m, 4)
    each(0, cap, keep_f_mirror, 4)

    def wait_f_near(o):
        f_near(o, near(o)).wait_recv()
        f_near_mirror(o, near(o)).wait_recv()

    each(1, half, wait_f_near)
    if stay:
        each(0, half, lambda o: f_other(o, other(o)).wait_recv())

    rows = q_tiles * TILE

    def times(weight, recv, q):
        x = jnp.concatenate([recv[q * q_tiles + k] for k in range(q_tiles)], axis=1)
        return jnp.dot(weight[...], x, preferred_element_type=jnp.float32)

    def self_part(q):
        pre[q] = times(ws_t, f_recv, q) + jnp.concatenate([bias_t[...]] * q_tiles, axis=1)

    each(0, n_q, self_part)
    live = table[8, me * cap]

    def finish(q):
        def wait_near(o):
            m_near(q, o, near(o)).wait_recv()
            m_near_mirror(q, o, near(o)).wait_recv()

        each(1, half, wait_near)
        if stay:
            each(0, half, lambda o: m_other(q, o, other(o)).wait_recv())
        hidden = jnp.maximum(pre[q] + times(wn_t, m_recv, q), 0.0)
        row = q * rows + lax.broadcasted_iota(jnp.int32, (1, rows), 1)
        hidden = jnp.where(row < live * TILE, hidden, 0.0).astype(jnp.bfloat16)
        out_v[0, 0, pl.ds(pl.multiple_of(q * rows, rows), rows), :] = hidden.T

    each(0, n_q, finish)

    def settle_near(o):
        f_near(o, me).wait_send()
        f_near_mirror(o, me).wait_send()

        def one(q):
            m_near(q, o, me).wait_send()
            m_near_mirror(q, o, me).wait_send()

        each(0, n_q, one)

    def settle_other(o):
        f_other(o, me).wait_send()
        each(0, n_q, lambda q: m_other(q, o, me).wait_send())

    def settle_y(i):
        y_copy(i, here).wait_send()
        fwd_copy(i, across).wait_send()

    def settle_mirror(i):
        swap_copy(i).wait_send()
        my_copy(i, here).wait_send()
        msib_copy(i, here).wait_send()
        mfwd_copy(i, across).wait_send()

    each(1, half, settle_near)
    if stay:
        each(0, half, settle_other)
    each(0, n_y, settle_y)
    each(0, n_m, settle_mirror)
    sib_copy(here).wait_send()


def layer(
    features, tile_values, tile_rows, tile_cols, tile_counts, w_self, w_neigh, bias, part_map
):
    n_blk = lax.axis_size("blk")
    n_bal = lax.axis_size("bal")
    slots = tile_rows.shape[2]
    tiles = part_map.shape[1]
    cap = 2 * tiles // n_bal
    width = features.shape[1]
    total = w_self.shape[0]
    fits = (
        n_blk == 4 and n_blk * slots == TILE and tiles == HALF and width == HALF
        and n_bal * cap == TILE
    )
    if not fits:
        return on_device(
            features, tile_values, tile_rows, tile_cols, tile_counts, w_self, w_neigh, bias,
            part_map,
        )
    n_y, n_m, n_q = 4, 4, 4
    swap = width // 2
    wide, stay, half = width + swap, width - swap, n_bal // 2
    bf16, f32 = jnp.bfloat16, jnp.float32
    vmem = pl.BlockSpec(memory_space=pltpu.VMEM)
    smem = pl.BlockSpec(memory_space=pltpu.SMEM)
    hbm = pl.BlockSpec(memory_space=pl.ANY)
    dma = pltpu.SemaphoreType.DMA
    return pl.pallas_call(
        functools.partial(layer_kernel, cap, slots, n_y, n_m, n_q, swap),
        out_shape=pltpu.VMEM((1, 1, cap * TILE, total), bf16),
        in_specs=[hbm, hbm, vmem, vmem, smem, hbm, hbm, vmem, vmem],
        out_specs=vmem,
        scratch_shapes=[
            pltpu.VMEM((width, tiles * TILE), bf16),
            pltpu.VMEM((n_blk * slots, TILE, TILE), bf16),
            pltpu.VMEM((HALF, 2 * TILE, TILE), bf16),
            pltpu.VMEM((tiles, width, TILE), bf16),
            pltpu.VMEM((tiles, swap, TILE), bf16),
            pltpu.VMEM((n_blk * tiles, width, TILE), bf16),
            pltpu.VMEM((n_blk * tiles, swap, TILE), bf16),
            pltpu.VMEM((HALF, 2 * width + 16, TILE), f32),
            pltpu.VMEM((HALF, 2 * swap, TILE), f32),
            pltpu.VMEM((half, cap, wide, TILE), bf16),
            pltpu.VMEM((half, cap, max(stay, 16), TILE), bf16),
            pltpu.VMEM((cap, total, TILE), bf16),
            pltpu.VMEM((half, cap, wide, TILE), bf16),
            pltpu.VMEM((half, cap, max(stay, 16), TILE), bf16),
            pltpu.VMEM((cap, total, TILE), bf16),
            pltpu.VMEM((n_q, total, cap // n_q * TILE), f32),
            pltpu.VMEM((total, total), bf16),
            pltpu.VMEM((total, total), bf16),
            pltpu.VMEM((total, total), bf16),
            pltpu.VMEM((total, total), bf16),
            pltpu.VMEM((total, TILE), f32),
            pltpu.VMEM((16, TILE), jnp.int32),
            pltpu.SMEM((16, TILE), jnp.int32),
            dma((n_y,)), dma, dma, dma, dma, dma,
            dma((n_m,)), dma((n_m,)), dma, dma, dma((n_y,)), dma((n_y,)), dma((n_y,)), dma((n_y,)),
            dma((n_m,)), dma((n_m,)), dma((n_m,)), dma((n_m,)), dma((n_m,)), dma((n_m,)),
            dma((n_bal,)), dma((n_bal,)), dma((half,)), dma((n_bal,)),
            dma((n_q, n_bal)), dma((n_q, n_bal)), dma((n_q, half)), dma((n_q, n_bal)),
        ],
        compiler_params=pltpu.CompilerParams(
            collective_id=0, has_side_effects=True, vmem_limit_bytes=56 * 2**20
        ),
        cost_estimate=pl.CostEstimate(
            flops=4 * cap * TILE * total * total, bytes_accessed=12 * 2**20, transcendentals=0
        ),
    )(
        features.T,
        tile_values.reshape(n_blk * slots, TILE, TILE),
        tile_rows[0],
        tile_cols[0],
        tile_counts,
        w_self,
        w_neigh,
        bias.reshape(1, total),
        part_map,
    )


def solution(mesh):
    placed = (
        P("blk", "bal"),
        P("blk", None, None, None, None),
        P("blk", None, None),
        P("blk", None, None),
        P("blk", None),
        P(),
        P(),
        P(),
        P("blk", None),
    )
    return jax.shard_map(
        layer,
        mesh=mesh,
        in_specs=placed,
        out_specs=P("blk", "bal", None, None),
        check_vma=False,
    )
```

```python
import functools
import jax
import jax.numpy as jnp
from jax import lax
from jax.experimental import pallas as pl
from jax.experimental.pallas import tpu as pltpu
from jax.sharding import PartitionSpec as P

TILE = 128
HALF = 64
MESH = pl.DeviceIdType.MESH


def from_behind(block, axis, distance):
    devices = range(lax.axis_size(axis))
    route = [((i - distance) % len(devices), i) for i in devices]
    return lax.ppermute(block, axis, route)


def advance(block, steps_by):
    return from_behind(block, "blk", steps_by)


def on_device(
    features, tile_values, tile_rows, tile_cols, tile_counts, w_self, w_neigh, bias, part_map
):
    n_blk = lax.axis_size("blk")
    n_bal = lax.axis_size("bal")
    here = lax.axis_index("blk")
    column = lax.axis_index("bal")
    width = features.shape[1]
    tiles_per = part_map.shape[1]
    values = tile_values[0]
    rows_idx = tile_rows[0]
    cols_idx = tile_cols[0]
    counts = tile_counts[0]
    slots = values.shape[1]
    live = jnp.arange(slots)[None, :] < counts[:, None]
    row_hot = (
        (rows_idx[:, :, None] == jnp.arange(tiles_per)[None, None, :]) & live[:, :, None]
    ).astype(jnp.float32)
    row_mass = jnp.einsum(
        "csij,j->csi", values, jnp.ones((TILE,), jnp.bfloat16), preferred_element_type=jnp.float32
    )
    degree = 1.0 + jnp.einsum("cst,csi->ti", row_hot, row_mass, precision=lax.Precision.HIGHEST)

    def absorb(total, block, source):
        tiles = block.reshape(tiles_per, TILE, width)
        vals = lax.dynamic_index_in_dim(values, source, 0, keepdims=False)
        picks = lax.dynamic_index_in_dim(cols_idx, source, 0, keepdims=False)
        targets = lax.dynamic_index_in_dim(rows_idx, source, 0, keepdims=False)
        alive = lax.dynamic_index_in_dim(live, source, 0, keepdims=False)
        gathered = jnp.take(tiles, picks, axis=0)
        prod = jnp.einsum("sij,sjf->sif", vals, gathered, preferred_element_type=jnp.float32)
        masked = jnp.where(alive[:, None, None], prod, 0.0)
        return total.at[targets].add(masked)

    empty = jnp.zeros((tiles_per, TILE, width), jnp.float32)

    def step_one(index, carry):
        total, block = carry
        total = absorb(total, block, (here - index) % n_blk)
        block = advance(block, 1)
        return (total, block)

    total, block = lax.fori_loop(0, n_blk - 1, step_one, (empty, features))
    total = absorb(total, block, (here - (n_blk - 1)) % n_blk)
    mean_agg = (total / degree[:, :, None]).astype(jnp.bfloat16).reshape(tiles_per * TILE, width)
    capacity = 2 * tiles_per // n_bal
    mapping = part_map[0]
    dest_hot = (mapping[:, None] == jnp.arange(n_bal)[None, :]).astype(jnp.int32)
    ranks = jnp.cumsum(dest_hot, axis=0) - dest_hot
    place = mapping * capacity + jnp.sum(ranks * dest_hot, axis=1)
    select = (jnp.arange(n_bal * capacity)[:, None] == place[None, :]).astype(jnp.bfloat16)
    col_start = column * width
    zeros_out = jnp.zeros((tiles_per * TILE, width), jnp.float32)
    carry = zeros_out
    mean_piece = lax.all_gather(mean_agg, "bal", axis=1, tiled=True)
    feat_piece = lax.all_gather(features, "bal", axis=1, tiled=True)
    count = mean_piece.shape[1]
    neigh_part = lax.dynamic_slice(w_neigh, (0, col_start), (count, width))
    self_part = lax.dynamic_slice(w_self, (0, col_start), (count, width))
    carry = jnp.dot(mean_piece, neigh_part, preferred_element_type=jnp.float32)
    pre = carry + jnp.dot(feat_piece, self_part, preferred_element_type=jnp.float32)
    pre = pre + lax.dynamic_slice_in_dim(bias, col_start, width)
    hidden = jnp.maximum(pre, 0.0).astype(jnp.bfloat16)
    tiles = hidden.reshape(tiles_per, TILE, width)
    placed = jnp.einsum("kt,tif->kif", select, tiles, preferred_element_type=jnp.float32)
    result = lax.all_to_all(
        placed.astype(jnp.bfloat16).reshape(n_bal, capacity * TILE, width),
        "bal",
        split_axis=0,
        concat_axis=2,
        tiled=True,
    )
    return result[None]


def tables(pm_ref, rows_ref, cols_ref, counts_ref, table, slots, cap):
    n_src = rows_ref.shape[0]
    table[...] = jnp.zeros(table.shape, jnp.int32)
    square = (TILE, TILE)
    lane = lax.broadcasted_iota(jnp.int32, square, 1)
    sub = lax.broadcasted_iota(jnp.int32, square, 0)

    def spread(row):
        return jnp.broadcast_to(row, square)

    def total(x):
        return jnp.sum(x, axis=0, keepdims=True)

    def flat(ref):
        return jnp.concatenate([ref[c : c + 1, :] for c in range(n_src)], axis=1)

    pm = pm_ref[...]
    pm = jnp.concatenate([pm, jnp.full((1, TILE - pm.shape[1]), 999, jnp.int32)], axis=1)
    pm_r = spread(pm)
    pm_c = pm_r.T
    earlier = jnp.where((pm_c == pm_r) & (sub < lane), 1, 0)
    place_c = spread(pm * cap + total(earlier)).T
    table[0:1, :] = total(jnp.where(place_c == lane, sub, 0))
    table[8:9, :] = total(jnp.where(pm_c == lane // cap, 1, 0))

    lane_row = lax.broadcasted_iota(jnp.int32, (1, TILE), 1)
    alive = jnp.zeros((1, TILE), jnp.int32)
    for c in range(n_src):
        alive = jnp.where(lane_row // slots == c, counts_ref[0, c], alive)
    rows_r = spread(flat(rows_ref))
    goes = total(jnp.where(rows_r == sub, place_c, 0))
    goes = jnp.where(lane_row % slots < alive, goes, 4096)
    goes_r = spread(goes)
    goes_c = goes_r.T
    rank_c = spread(total(jnp.where(goes_c * TILE + sub < goes_r * TILE + lane, 1, 0))).T
    pick = rank_c == lane
    source = (lane_row // slots) * HALF + flat(cols_ref)
    source_c = spread(source).T
    table[1:2, :] = total(jnp.where(pick, sub, 0))
    table[2:3, :] = total(jnp.where(pick, source_c, 0))
    mine = total(jnp.where(pick, goes_c, 0))
    before = total(jnp.where(rank_c + 1 == lane, goes_c, 0))
    table[3:4, :] = jnp.where((mine == before) & (lane_row % HALF != 0), 1, 0)
    upto = total(jnp.where(goes_c <= lane, 1, 0))
    below = total(jnp.where(goes_c < lane, 1, 0))
    left_end = jnp.minimum(upto, HALF)
    right_from = jnp.maximum(below, HALF)
    table[4:5, :] = jnp.maximum(left_end - 1, 0)
    table[5:6, :] = jnp.where(below < left_end, 1, 0)
    table[6:7, :] = jnp.maximum(upto - 1 - HALF, 0)
    table[7:8, :] = jnp.where(right_from < upto, 1, 0)


def layer_kernel(
    cap, slots, n_y, n_m, n_q, swap,
    feat_hbm, vals_hbm, rows_ref, cols_ref, counts_ref, ws_hbm, wn_hbm, bias_ref, pm_ref,
    out_v,
    feat, vals, turned, own, mirror, blocks, mirrors, sums, more, f_in, f_out, f_recv, m_in, m_out, m_recv, pre,
    ws_ref, wn_ref, ws_t, wn_t, bias_t, table_v, table,
    feat_sem, vals_sem, ws_sem, wn_sem, table_sem, mir_sem,
    swap_send, swap_recv, sib_send, sib_recv, y_send, y_recv, fwd_send, fwd_recv,
    msib_send, msib_recv, my_send, my_recv, mfwd_send, mfwd_recv,
    fs_sem, fr_sem, fms_sem, fmr_sem, ms_sem, mr_sem, mms_sem, mmr_sem,
):
    here = lax.axis_index("blk")
    me = lax.axis_index("bal")
    tiles, width, _ = own.shape
    wide = width + swap
    stay = width - swap
    n_bal = f_recv.shape[1] // width
    half = n_bal // 2
    at_end = (me % half < half // 2) == (me // half == 0)
    base = me // half * half
    partner = (me + half) % n_bal
    sibling = here + 1 - 2 * (here % 2)
    across = (here + 2) % 4
    far = (sibling + 2) % 4
    y_tiles = tiles // n_y
    m_tiles = tiles // n_m
    q_tiles = cap // n_q
    own_rows = pl.ds(pl.multiple_of(me * width, width), width)
    mirror_rows = pl.ds(pl.multiple_of(partner * width + stay, 16), swap)

    def near(o):
        return base + (me + o) % half

    def other(o):
        return (base + half) % n_bal + (me + o) % half

    def each(first, last, body, unroll=1):
        def step(i, carry):
            body(i)
            return carry

        lax.fori_loop(first, last, step, 0, unroll=unroll)

    def remote(src, dst, send, recv, axis, peer):
        return pltpu.make_async_remote_copy(
            src, dst, send, recv, device_id={axis: peer}, device_id_type=MESH
        )

    barrier = pltpu.get_barrier_semaphore()
    for peer in (sibling, across):
        pl.semaphore_signal(barrier, inc=1, device_id={"blk": peer}, device_id_type=MESH)
    each(
        1, n_bal,
        lambda o: pl.semaphore_signal(
            barrier, inc=1, device_id={"bal": (me + o) % n_bal}, device_id_type=MESH
        ),
    )

    span_y = y_tiles * TILE

    def load_feat(i):
        part = pl.ds(pl.multiple_of(i * span_y, span_y), span_y)
        return pltpu.make_async_copy(feat_hbm.at[:, part], feat.at[:, part], feat_sem.at[i])

    each(0, n_y, lambda i: load_feat(i).start())
    load_vals = pltpu.make_async_copy(vals_hbm, vals, vals_sem)
    load_ws = pltpu.make_async_copy(ws_hbm, ws_ref, ws_sem)
    load_wn = pltpu.make_async_copy(wn_hbm, wn_ref, wn_sem)

    def pack(t):
        x = feat[:, pl.ds(pl.multiple_of(t * TILE, TILE), TILE)]
        own[t] = x
        blocks[here * tiles + t] = x

    def pack_part(i):
        load_feat(i).wait()
        each(0, y_tiles, lambda t: pack(i * y_tiles + t), 4)

    tables(pm_ref, rows_ref, cols_ref, counts_ref, table_v, slots, cap)
    load_table = pltpu.make_async_copy(table_v, table, table_sem)
    load_table.start()
    each(0, n_y, pack_part)
    pl.semaphore_wait(barrier, n_bal + 1)

    def swap_copy(i):
        span = pl.ds(i * m_tiles, m_tiles)
        return remote(
            own.at[span, pl.ds(stay, swap)], mirror.at[span],
            swap_send.at[i], swap_recv.at[i], "bal", partner,
        )

    def y_copy(i, whose):
        return remote(
            own.at[pl.ds(i * y_tiles, y_tiles)],
            blocks.at[pl.ds(whose * tiles + i * y_tiles, y_tiles)],
            y_send.at[i], y_recv.at[i], "blk", across,
        )

    def fwd_copy(i, whose):
        span = pl.ds(whose * tiles + i * y_tiles, y_tiles)
        part = blocks.at[span]
        return remote(part, part, fwd_send.at[i], fwd_recv.at[i], "blk", sibling)

    def sib_copy(whose):
        return remote(
            own, blocks.at[pl.ds(whose * tiles, tiles)],
            sib_send, sib_recv, "blk", sibling,
        )

    def my_copy(i, whose):
        return remote(
            mirror.at[pl.ds(i * m_tiles, m_tiles)],
            mirrors.at[pl.ds(whose * tiles + i * m_tiles, m_tiles)],
            my_send.at[i], my_recv.at[i], "blk", across,
        )

    def msib_copy(i, whose):
        return remote(
            mirror.at[pl.ds(i * m_tiles, m_tiles)],
            mirrors.at[pl.ds(whose * tiles + i * m_tiles, m_tiles)],
            msib_send.at[i], msib_recv.at[i], "blk", sibling,
        )

    def mfwd_copy(i, whose):
        span = pl.ds(whose * tiles + i * m_tiles, m_tiles)
        part = mirrors.at[span]
        return remote(part, part, mfwd_send.at[i], mfwd_recv.at[i], "blk", sibling)

    def f_near(o, whose):
        rows = pl.ds(pl.multiple_of(whose * width, width), width)
        return remote(
            f_in.at[o, :, pl.ds(0, width)], f_recv.at[:, rows],
            fs_sem.at[o], fr_sem.at[whose], "bal", near(o),
        )

    def f_near_mirror(o, whose):
        rows = pl.ds(pl.multiple_of((whose + half) % n_bal * width + stay, 16), swap)
        return remote(
            f_in.at[o, :, pl.ds(width, swap)], f_recv.at[:, rows],
            fms_sem.at[o], fmr_sem.at[whose], "bal", near(o),
        )

    def f_other(o, whose):
        rows = pl.ds(pl.multiple_of(whose * width, width), stay)
        return remote(
            f_out.at[o], f_recv.at[:, rows],
            fs_sem.at[half + o], fr_sem.at[whose], "bal", other(o),
        )

    def m_near(q, o, whose):
        span = pl.ds(q * q_tiles, q_tiles)
        rows = pl.ds(pl.multiple_of(whose * width, width), width)
        return remote(
            m_in.at[o, span, pl.ds(0, width)], m_recv.at[span, rows],
            ms_sem.at[q, o], mr_sem.at[q, whose], "bal", near(o),
        )

    def m_near_mirror(q, o, whose):
        span = pl.ds(q * q_tiles, q_tiles)
        rows = pl.ds(pl.multiple_of((whose + half) % n_bal * width + stay, 16), swap)
        return remote(
            m_in.at[o, span, pl.ds(width, swap)], m_recv.at[span, rows],
            mms_sem.at[q, o], mmr_sem.at[q, whose], "bal", near(o),
        )

    def m_other(q, o, whose):
        span = pl.ds(q * q_tiles, q_tiles)
        rows = pl.ds(pl.multiple_of(whose * width, width), stay)
        return remote(
            m_out.at[o, span], m_recv.at[span, rows],
            ms_sem.at[q, half + o], mr_sem.at[q, whose], "bal", other(o),
        )

    each(0, n_m, lambda i: swap_copy(i).start())
    each(0, n_y, lambda i: y_copy(i, here).start())
    sib_copy(here).start()

    load_vals.start()
    load_ws.start()
    load_wn.start()
    load_table.wait()

    def send_f_near(o):
        def gather(k):
            f_in[o, k, :width, :] = own[table[0, near(o) * cap + k]]

        each(0, cap, gather, 4)
        f_near(o, me).start()

    def fill_f_other(o):
        def gather(k):
            f_out[o, k] = own[table[0, other(o) * cap + k]][:stay]

        each(0, cap, gather, 4)

    def keep_f(k):
        f_recv[k, own_rows, :] = own[table[0, me * cap + k]]

    each(1, half, send_f_near)
    if stay:
        each(0, half, fill_f_other)
    each(0, cap, keep_f, 4)
    load_vals.wait()
    load_ws.wait()
    ws_t[...] = ws_ref[...].T
    load_wn.wait()
    wn_t[...] = wn_ref[...].T

    def turn(j):
        turned[j, :TILE, :] = vals[table[1, j]].T
        turned[j, TILE:, :] = vals[table[1, j + HALF]].T

    each(0, HALF, turn, 2)
    bias_t[...] = jnp.broadcast_to(bias_ref[...], (TILE, bias_ref.shape[1])).T

    def pass_on(i):
        y_copy(i, across).wait_recv()
        fwd_copy(i, across).start()

    def take_mirror(i):
        swap_copy(i).wait_recv()
        my_copy(i, here).start()
        msib_copy(i, here).start()

    each(0, n_y, pass_on)
    each(0, n_m - 1, take_mirror)

    def send_f_other():
        each(0, half, lambda o: f_other(o, me).start())

    if stay:
        pl.when(at_end)(send_f_other)
    each(n_m - 1, n_m, take_mirror)
    keep_mirror = pltpu.make_async_copy(
        mirror, mirrors.at[pl.ds(here * tiles, tiles)], mir_sem
    )
    keep_mirror.start()

    def send_f_mirror(o):
        def gather(k):
            f_in[o, k, width:, :] = mirror[table[0, near(o) * cap + k]]

        each(0, cap, gather, 4)
        f_near_mirror(o, me).start()

    def keep_f_mirror(k):
        f_recv[k, mirror_rows, :] = mirror[table[0, me * cap + k]]

    each(1, half, send_f_mirror)
    if stay:
        pl.when(jnp.logical_not(at_end))(send_f_other)

    sib_copy(sibling).wait_recv()
    each(0, n_y, lambda i: fwd_copy(i, far).wait_recv())

    in_top = lax.broadcasted_iota(jnp.int32, (16, 2 * TILE), 0) < 8
    in_left = lax.broadcasted_iota(jnp.int32, (16, 2 * TILE), 1) < TILE
    ones = jnp.where(in_top == in_left, 1.0, 0.0).astype(jnp.bfloat16)
    deg_left = lax.broadcasted_iota(jnp.int32, (16, TILE), 0) < 8

    def products(j, held, count, extra):
        zeros = jnp.zeros((count, TILE), jnp.bfloat16)
        x = jnp.concatenate([held[table[2, j]], zeros], axis=1)
        y = jnp.concatenate([zeros, held[table[2, j + HALF]]], axis=1)
        lhs = jnp.concatenate([x, y] + extra, axis=0)
        return jnp.dot(lhs, turned[j], preferred_element_type=jnp.float32)

    def absorb(j, carry):
        left, right, deg = carry
        prod = products(j, blocks, width, [ones])
        keep_left, keep_right = table[3, j], table[3, j + HALF]
        left = jnp.where(keep_left > 0, left, 0.0) + prod[:width]
        right = jnp.where(keep_right > 0, right, 0.0) + prod[width : 2 * width]
        deg = jnp.where(jnp.where(deg_left, keep_left, keep_right) > 0, deg, 0.0)
        deg = deg + prod[2 * width :]
        sums[j, :width, :] = left
        sums[j, width : 2 * width, :] = right
        sums[j, 2 * width :, :] = deg
        return left, right, deg

    def absorb_mirror(j, carry):
        left, right = carry
        prod = products(j, mirrors, swap, [])
        left = jnp.where(table[3, j] > 0, left, 0.0) + prod[:swap]
        right = jnp.where(table[3, j + HALF] > 0, right, 0.0) + prod[swap:]
        more[j, :swap, :] = left
        more[j, swap:, :] = right
        return left, right

    empty = jnp.zeros((width, TILE), jnp.float32)
    lax.fori_loop(
        0, HALF, absorb, (empty, empty, jnp.zeros((16, TILE), jnp.float32)), unroll=2
    )

    def inverse_degree(p):
        left, right = sums.at[table[4, p]], sums.at[table[6, p]]
        degree = (
            1.0
            + jnp.where(table[5, p] > 0, left[2 * width : 2 * width + 8, :], 0.0)
            + jnp.where(table[7, p] > 0, right[2 * width + 8 :, :], 0.0)
        )
        return (1.0 / degree)[:1]

    def mean_piece(p, inverse, where, count, right_row):
        left, right = where.at[table[4, p]], where.at[table[6, p]]
        agg = jnp.where(table[5, p] > 0, left[:count, :], 0.0) + jnp.where(
            table[7, p] > 0, right[right_row : right_row + count, :], 0.0
        )
        return (agg * inverse).astype(jnp.bfloat16)

    def send_m_other(q):
        def to_other(o):
            def fill(k):
                p = other(o) * cap + q * q_tiles + k
                m_out[o, q * q_tiles + k] = mean_piece(p, inverse_degree(p), sums, stay, width)

            each(0, q_tiles, fill, q_tiles)
            m_other(q, o, me).start()

        each(0, half, to_other)

    def send_m_near(q):
        def to_near(o):
            def fill(k):
                p = near(o) * cap + q * q_tiles + k
                m_in[o, q * q_tiles + k, :width, :] = mean_piece(
                    p, inverse_degree(p), sums, width, width
                )

            each(0, q_tiles, fill, q_tiles)
            m_near(q, o, me).start()

        each(1, half, to_near)

    def pass_mirror_on(i):
        my_copy(i, across).wait_recv()
        mfwd_copy(i, across).start()

    def send_all_m_other():
        each(0, n_q, send_m_other)

    if stay:
        pl.when(at_end)(send_all_m_other)
    each(0, n_m, pass_mirror_on)
    each(0, n_q, send_m_near)
    if stay:
        pl.when(jnp.logical_not(at_end))(send_all_m_other)
    each(0, n_m, lambda i: msib_copy(i, sibling).wait_recv())
    each(0, n_m, lambda i: mfwd_copy(i, far).wait_recv())
    keep_mirror.wait()
    lax.fori_loop(0, HALF, absorb_mirror, (empty[:swap], empty[:swap]), unroll=2)

    def send_m_mirror(q):
        def to_near(o):
            def fill(k):
                p = near(o) * cap + q * q_tiles + k
                m_in[o, q * q_tiles + k, width:, :] = mean_piece(
                    p, inverse_degree(p), more, swap, swap
                )

            each(0, q_tiles, fill, q_tiles)
            m_near_mirror(q, o, me).start()

        each(1, half, to_near)

    each(0, n_q, send_m_mirror)

    def keep_m(k):
        p = me * cap + k
        inverse = inverse_degree(p)
        m_recv[k, own_rows, :] = mean_piece(p, inverse, sums, width, width)
        m_recv[k, mirror_rows, :] = mean_piece(p, inverse, more, swap, swap)

    each(0, cap, keep_m, 4)
    each(0, cap, keep_f_mirror, 4)

    def wait_f_near(o):
        f_near(o, near(o)).wait_recv()
        f_near_mirror(o, near(o)).wait_recv()

    each(1, half, wait_f_near)
    if stay:
        each(0, half, lambda o: f_other(o, other(o)).wait_recv())

    rows = q_tiles * TILE

    def times(weight, recv, q):
        x = jnp.concatenate([recv[q * q_tiles + k] for k in range(q_tiles)], axis=1)
        return jnp.dot(weight[...], x, preferred_element_type=jnp.float32)

    def self_part(q):
        pre[q] = times(ws_t, f_recv, q) + jnp.concatenate([bias_t[...]] * q_tiles, axis=1)

    each(0, n_q, self_part)
    live = table[8, me * cap]

    def finish(q):
        def wait_near(o):
            m_near(q, o, near(o)).wait_recv()
            m_near_mirror(q, o, near(o)).wait_recv()

        each(1, half, wait_near)
        if stay:
            each(0, half, lambda o: m_other(q, o, other(o)).wait_recv())
        hidden = jnp.maximum(pre[q] + times(wn_t, m_recv, q), 0.0)
        row = q * rows + lax.broadcasted_iota(jnp.int32, (1, rows), 1)
        hidden = jnp.where(row < live * TILE, hidden, 0.0).astype(jnp.bfloat16)
        out_v[0, 0, pl.ds(pl.multiple_of(q * rows, rows), rows), :] = hidden.T

    each(0, n_q, finish)

    def settle_near(o):
        f_near(o, me).wait_send()
        f_near_mirror(o, me).wait_send()

        def one(q):
            m_near(q, o, me).wait_send()
            m_near_mirror(q, o, me).wait_send()

        each(0, n_q, one)

    def settle_other(o):
        f_other(o, me).wait_send()
        each(0, n_q, lambda q: m_other(q, o, me).wait_send())

    def settle_y(i):
        y_copy(i, here).wait_send()
        fwd_copy(i, across).wait_send()

    def settle_mirror(i):
        swap_copy(i).wait_send()
        my_copy(i, here).wait_send()
        msib_copy(i, here).wait_send()
        mfwd_copy(i, across).wait_send()

    each(1, half, settle_near)
    if stay:
        each(0, half, settle_other)
    each(0, n_y, settle_y)
    each(0, n_m, settle_mirror)
    sib_copy(here).wait_send()


def layer(
    features, tile_values, tile_rows, tile_cols, tile_counts, w_self, w_neigh, bias, part_map
):
    n_blk = lax.axis_size("blk")
    n_bal = lax.axis_size("bal")
    slots = tile_rows.shape[2]
    tiles = part_map.shape[1]
    cap = 2 * tiles // n_bal
    width = features.shape[1]
    total = w_self.shape[0]
    fits = (
        n_blk == 4 and n_blk * slots == TILE and tiles == HALF and width == HALF
        and n_bal * cap == TILE
    )
    if not fits:
        return on_device(
            features, tile_values, tile_rows, tile_cols, tile_counts, w_self, w_neigh, bias,
            part_map,
        )
    n_y, n_m, n_q = 4, 4, 8
    swap = width // 2
    wide, stay, half = width + swap, width - swap, n_bal // 2
    bf16, f32 = jnp.bfloat16, jnp.float32
    vmem = pl.BlockSpec(memory_space=pltpu.VMEM)
    smem = pl.BlockSpec(memory_space=pltpu.SMEM)
    hbm = pl.BlockSpec(memory_space=pl.ANY)
    dma = pltpu.SemaphoreType.DMA
    return pl.pallas_call(
        functools.partial(layer_kernel, cap, slots, n_y, n_m, n_q, swap),
        out_shape=pltpu.VMEM((1, 1, cap * TILE, total), bf16),
        in_specs=[hbm, hbm, vmem, vmem, smem, hbm, hbm, vmem, vmem],
        out_specs=vmem,
        scratch_shapes=[
            pltpu.VMEM((width, tiles * TILE), bf16),
            pltpu.VMEM((n_blk * slots, TILE, TILE), bf16),
            pltpu.VMEM((HALF, 2 * TILE, TILE), bf16),
            pltpu.VMEM((tiles, width, TILE), bf16),
            pltpu.VMEM((tiles, swap, TILE), bf16),
            pltpu.VMEM((n_blk * tiles, width, TILE), bf16),
            pltpu.VMEM((n_blk * tiles, swap, TILE), bf16),
            pltpu.VMEM((HALF, 2 * width + 16, TILE), f32),
            pltpu.VMEM((HALF, 2 * swap, TILE), f32),
            pltpu.VMEM((half, cap, wide, TILE), bf16),
            pltpu.VMEM((half, cap, max(stay, 16), TILE), bf16),
            pltpu.VMEM((cap, total, TILE), bf16),
            pltpu.VMEM((half, cap, wide, TILE), bf16),
            pltpu.VMEM((half, cap, max(stay, 16), TILE), bf16),
            pltpu.VMEM((cap, total, TILE), bf16),
            pltpu.VMEM((n_q, total, cap // n_q * TILE), f32),
            pltpu.VMEM((total, total), bf16),
            pltpu.VMEM((total, total), bf16),
            pltpu.VMEM((total, total), bf16),
            pltpu.VMEM((total, total), bf16),
            pltpu.VMEM((total, TILE), f32),
            pltpu.VMEM((16, TILE), jnp.int32),
            pltpu.SMEM((16, TILE), jnp.int32),
            dma((n_y,)), dma, dma, dma, dma, dma,
            dma((n_m,)), dma((n_m,)), dma, dma, dma((n_y,)), dma((n_y,)), dma((n_y,)), dma((n_y,)),
            dma((n_m,)), dma((n_m,)), dma((n_m,)), dma((n_m,)), dma((n_m,)), dma((n_m,)),
            dma((n_bal,)), dma((n_bal,)), dma((half,)), dma((n_bal,)),
            dma((n_q, n_bal)), dma((n_q, n_bal)), dma((n_q, half)), dma((n_q, n_bal)),
        ],
        compiler_params=pltpu.CompilerParams(
            collective_id=0, has_side_effects=True, vmem_limit_bytes=56 * 2**20
        ),
        cost_estimate=pl.CostEstimate(
            flops=4 * cap * TILE * total * total, bytes_accessed=12 * 2**20, transcendentals=0
        ),
    )(
        features.T,
        tile_values.reshape(n_blk * slots, TILE, TILE),
        tile_rows[0],
        tile_cols[0],
        tile_counts,
        w_self,
        w_neigh,
        bias.reshape(1, total),
        part_map,
    )


def solution(mesh):
    placed = (
        P("blk", "bal"),
        P("blk", None, None, None, None),
        P("blk", None, None),
        P("blk", None, None),
        P("blk", None),
        P(),
        P(),
        P(),
        P("blk", None),
    )
    return jax.shard_map(
        layer,
        mesh=mesh,
        in_specs=placed,
        out_specs=P("blk", "bal", None, None),
        check_vma=False,
    )
```
